128 devices in a mesh: row: 8 (over z, core), col: 16 (over y, x).
Axes of the slice: x: 4, y: 4, z: 4, core: 2. Of those that a mesh axis runs over, the one named last changes fastest.
Arguments:
- currents: float32 [2, 524288], P(None, ('row', 'col')), may hold values from -6 to 6
- near_blocks: bfloat16 [16384, 2, 128, 128], P(('row', 'col')), may hold values from -0.5 to 0.5
- pair_local: int32 [128, 128], P(('row', 'col')), may hold values from 0 to 31
- pair_ghost: int32 [128, 128], P(('row', 'col')), may hold values from 0 to 287, as said below
- pair_counts: int32 [128], P(('row', 'col')), may hold values from 1 to 128, 9830 in all
- projection: float32 [4096, 128, 128], P(('row', 'col')), may hold values from -0.5 to 0.5
- stencil_cells: int32 [4096, 128], P(('row', 'col')), may hold values from 0 to 287231, as said below
- green: float32 [2, 32, 1024, 1024], P(None, 'col', 'row'), may hold values from -24 to 24
Outputs:
- product: float32 [2, 524288], P(None, ('row', 'col'))
The draws below stay inside these ranges and needn't reach their ends.
Inputs may be any that keep to these rules, and one draw needn't show every extreme that they name: `stencil_cells`: every index lies in a box of 4 x 4 x 8 cells of the tile with rims, the box's corner drawn per block; the extreme boxes occur. `pair_ghost`: n = entry // 32 names the tile offset (n // 3 - 1, n % 3 - 1) around the holder's tile, wrapping on the torus of tiles, and entry % 32 a block of that tile; no slot pairs a block with itself.
All inputs are finite; a program needn't handle non-finite values. No bound on the sum of `pair_counts` on one device may be relied on, other than what follows from the above.
Results may differ from the reference program's by a relative error of at most 0.005.
Values may be sent and summed in bfloat16 or wider, within the bound.
A program may use at most 128 MiB of HBM per device.

```python
import math
import jax
import jax.numpy as jnp
import numpy as np
from jax import lax

NGX = 1024
NGY = 1024
NGZ = 32
BLK = 128
BOXX = 4
BOXY = 4
BOXZ = 8
RIM = 2
NB = 32
PD = 128
STENCIL = 128
CX = 128
CY = 64
BLOCKS = 4096
UNK = 524288
PAIRS = 16384
N_ROW = 8
N_COL = 16
DEVICES = 128


def near_pairs(key):
    key_local, key_ghost = jax.random.split(key, 2)
    local = jax.random.randint(key_local, (DEVICES, PD), 0, NB).astype(jnp.int32)
    local = local.at[0, 0].set(0).at[0, 1].set(NB - 1)
    ghost = jax.random.randint(key_ghost, (DEVICES, PD), 0, 9 * NB).astype(jnp.int32)
    ghost = ghost.at[0, 0].set(0).at[0, 1].set(9 * NB - 1)
    clash = ghost == 4 * NB + local
    ghost = jnp.where(clash, 4 * NB + (local + 1) % NB, ghost).astype(jnp.int32)
    return (local, ghost)


def draw_pair_local(key, part):
    local, ghost = near_pairs(key)
    return local


def draw_pair_ghost(key, part):
    local, ghost = near_pairs(key)
    return ghost


def draw_stencil_cells(key, part):
    key = jax.random.fold_in(key, 7)
    key_x, key_y, key_z = jax.random.split(key, 3)
    span_x = CX + 2 * RIM - BOXX + 1
    span_y = CY + 2 * RIM - BOXY + 1
    span_z = NGZ - BOXZ + 1
    corner_x = jax.random.randint(key_x, (BLOCKS,), 0, span_x).astype(jnp.int32)
    corner_y = jax.random.randint(key_y, (BLOCKS,), 0, span_y).astype(jnp.int32)
    corner_z = jax.random.randint(key_z, (BLOCKS,), 0, span_z).astype(jnp.int32)
    corner_x = corner_x.at[0].set(span_x - 1).at[1].set(0)
    corner_y = corner_y.at[0].set(span_y - 1).at[1].set(0)
    corner_z = corner_z.at[0].set(span_z - 1).at[1].set(0)
    offset_x = jnp.arange(BOXX, dtype=jnp.int32)[None, :, None, None]
    offset_y = jnp.arange(BOXY, dtype=jnp.int32)[None, None, :, None]
    offset_z = jnp.arange(BOXZ, dtype=jnp.int32)[None, None, None, :]
    wide_y = CY + 2 * RIM
    cells = ((corner_x[:, None, None, None] + offset_x) * wide_y + corner_y[:, None, None, None] + offset_y) * NGZ
    cells = cells + corner_z[:, None, None, None] + offset_z
    return cells.reshape(BLOCKS, BOXX * BOXY * BOXZ).astype(jnp.int32)


def shard_levels(own_key, dims, cuts, least, largest):
    gain, own = 1.0, jax.random.fold_in(own_key, 6)
    for position, parts in cuts:
        heights = jnp.exp(jax.random.uniform(jax.random.fold_in(own, position), (parts,), jnp.float32, least / len(cuts), largest / len(cuts)))
        gain = gain * jnp.repeat(heights, dims[position] // parts).reshape([-1 if axis == position else 1 for axis in range(len(dims))])
    return gain


def profile(amount, total, bound, skew):
    weights = [(1 << 20) // math.isqrt(grade ** skew) + 1 for grade in range(2, amount + 1)]
    rest, given = total - bound - (amount - 1), [1] * (amount - 1)
    while rest > 0:
        candidates = [i for i in range(amount - 1) if given[i] < bound]
        pool, left = sum([weights[i] for i in candidates]), rest
        for i in candidates:
            addition = min(bound - given[i], max(1, left * weights[i] // pool), rest)
            given[i] = given[i] + addition
            rest = rest - addition
    return np.array([bound] + given)


def uneven(key, amount, total, most, slope):
    if amount == 2:
        one = jax.random.randint(key, (), max(1, total - most), min(most, total - 1) + 1)
        return jnp.stack([one, total - one])
    sizes = jnp.asarray(profile(amount, total, most, slope), jnp.int32)
    couples = (amount - 1) // 2
    source_of, receiver = sizes[1:1 + 2 * couples:2], sizes[2:2 + 2 * couples:2]
    room = jnp.minimum(source_of - 1, most - receiver)
    moved = jax.random.randint(jax.random.fold_in(key, 1), (couples,), 0, 1 << 20) % (room + 1)
    sizes = sizes.at[1:1 + 2 * couples:2].set(source_of - moved).at[2:2 + 2 * couples:2].set(receiver + moved)
    return sizes[jax.random.permutation(jax.random.fold_in(key, 2), amount)]


def noise(key, extent, scale, limit, pieces=(), held_as=jnp.bfloat16):
    loudness = shard_levels(key, extent, pieces, -0.22, 0.18) if pieces else 1.0
    values = jax.random.normal(key, extent, jnp.float32) * scale * loudness
    return jnp.minimum(jnp.maximum(values, -limit), limit).astype(held_as)


def setup_inputs(seed: int = 0) -> dict:
    seeds = jax.random.split(jax.random.key(seed), 9)
    currents = noise(seeds[0], (2, UNK), 1.0, 6.0, ((1, 128),), jnp.float32)
    near_blocks = noise(seeds[1], (PAIRS, 2, BLK, BLK), BLK ** -0.5, 0.5, ((0, 128),))
    pair_local = draw_pair_local(jax.random.fold_in(seeds[8], 71), 0)
    pair_ghost = draw_pair_ghost(jax.random.fold_in(seeds[8], 71), 0)
    pair_counts = uneven(seeds[4], DEVICES, DEVICES * PD * 3 // 5, PD, 2).astype(jnp.int32)
    projection = noise(seeds[5], (BLOCKS, STENCIL, BLK), BLK ** -0.5, 0.5, ((0, 128),), jnp.float32)
    stencil_cells = draw_stencil_cells(jax.random.fold_in(seeds[8], 71), 0)
    green = noise(seeds[7], (2, NGZ, NGY, NGX), 4.0, 24.0, ((1, 16), (2, 8)), jnp.float32)
    return dict(currents=currents, near_blocks=near_blocks, pair_local=pair_local, pair_ghost=pair_ghost, pair_counts=pair_counts, projection=projection, stencil_cells=stencil_cells, green=green)


def combine_parts(products):
    return jnp.stack([products[:, 0, 0] - products[:, 1, 1], products[:, 0, 1] + products[:, 1, 0]], axis=1)


def reference(currents, near_blocks, pair_local, pair_ghost, pair_counts, projection, stencil_cells, green):
    blocks = currents.reshape(2, BLOCKS, BLK)
    rounded = jnp.transpose(blocks.astype(jnp.bfloat16), (1, 0, 2))
    tile_dev = jnp.arange(DEVICES, dtype=jnp.int32)
    dev_row = (tile_dev // N_COL)[:, None]
    dev_col = (tile_dev % N_COL)[:, None]
    offset = pair_ghost // NB
    within = pair_ghost % NB
    near_row = (dev_row + offset // 3 - 1) % N_ROW
    near_col = (dev_col + offset % 3 - 1) % N_COL
    theirs = ((near_row * N_COL + near_col) * NB + within).astype(jnp.int32)
    mine = (tile_dev[:, None] * NB + pair_local).astype(jnp.int32)
    alive = (jnp.arange(PD, dtype=jnp.int32)[None, :] < pair_counts[:, None]).astype(jnp.float32)
    matrices = near_blocks.reshape(DEVICES, PD, 2, BLK, BLK)

    def one_device(items):
        matrix, here, there, living = items
        wide_matrix = matrix.astype(jnp.float32)
        local_vals = rounded[here].astype(jnp.float32)
        remote_vals = rounded[there].astype(jnp.float32)
        onward = jnp.einsum("pcij,pdj->pcdi", wide_matrix, remote_vals, precision=lax.Precision.HIGHEST)
        backward = jnp.einsum("pcij,pdi->pcdj", wide_matrix, local_vals, precision=lax.Precision.HIGHEST)
        return combine_parts(onward) * living[:, None, None], combine_parts(backward) * living[:, None, None]

    onward_all, backward_all = lax.map(one_device, (matrices, mine, theirs, alive))
    near = jnp.zeros((BLOCKS, 2, BLK), jnp.float32)
    near = near.at[mine.reshape(-1)].add(onward_all.reshape(-1, 2, BLK))
    near = near.at[theirs.reshape(-1)].add(backward_all.reshape(-1, 2, BLK))

    block_dev = jnp.arange(BLOCKS, dtype=jnp.int32) // NB
    tile_row = block_dev // N_COL
    tile_col = block_dev % N_COL
    wide_y = CY + 2 * RIM
    cell_x = stencil_cells // (wide_y * NGZ)
    cell_y = (stencil_cells // NGZ) % wide_y
    cell_z = stencil_cells % NGZ
    grid_x = (tile_row[:, None] * CX + cell_x - RIM) % NGX
    grid_y = (tile_col[:, None] * CY + cell_y - RIM) % NGY
    values = jnp.einsum("nkb,cnb->cnk", projection, blocks, precision=lax.Precision.HIGHEST)
    field = jnp.zeros((2, NGX, NGY, NGZ), jnp.float32).at[:, grid_x, grid_y, cell_z].add(values)
    spectrum = jnp.fft.fftn(field[0] + 1j * field[1])
    kernel = jnp.transpose(green[0] + 1j * green[1], (2, 1, 0))
    potential_c = jnp.fft.ifftn(spectrum * kernel)
    potential = jnp.stack([jnp.real(potential_c), jnp.imag(potential_c)]).astype(jnp.float32)
    picked = potential[:, grid_x, grid_y, cell_z]
    far = jnp.einsum("nkb,cnk->cnb", projection, picked, precision=lax.Precision.HIGHEST)
    total = far + jnp.transpose(near, (1, 0, 2))
    return total.reshape(2, UNK)
```

```python
import math

import jax
import jax.numpy as jnp
import ml_dtypes
import numpy as np
from jax import lax
from jax.experimental import pallas as pl
from jax.experimental.pallas import tpu as pltpu
from jax.sharding import PartitionSpec as P

N = 1024
NGZ = 32
NROW = 8
NCOL = 16
NB = 32
BLK = 128
XR = 144
WIDE_Y = 68
BF = jnp.bfloat16
F32 = jnp.float32
VMEM_LIMIT = 60 * 1024 * 1024


def bf(a):
    return np.asarray(a, dtype=np.float64).astype(ml_dtypes.bfloat16)


def split_np(a):
    high = bf(a)
    return high, bf(a - high.astype(np.float64))


def grid_tables():
    index = np.arange(N)[:, None] * np.arange(N)[None, :] % N
    angle = index * (2.0 * math.pi / N)
    return bf(np.cos(angle)), bf(np.sin(angle))


def depth_tables():
    index = np.arange(NGZ)[:, None] * np.arange(NGZ)[None, :] % NGZ
    angle = index * (2.0 * math.pi / NGZ)
    eye = np.eye(16)
    cos_high, cos_low = split_np(np.kron(np.cos(angle), eye))
    sin_high, sin_low = split_np(np.kron(np.sin(angle), eye))
    return cos_high, cos_low, sin_high, sin_low


def spread_table():
    lane = np.arange(128)[:, None]
    plane, ex, b = lane // 16, lane // 4 % 4, lane % 4
    wide = np.arange(2048)[None, :]
    hits = (wide // 512 == ex) & (wide // 128 % 4 == plane) & ((wide + 2) % 4 == b) & (lane < 64)
    return bf(hits.astype(np.float64))


def dot(a, b):
    return jnp.dot(a, b, preferred_element_type=F32)


def dot_nt(a, b):
    return lax.dot_general(a, b, (((1,), (1,)), ((), ())), preferred_element_type=F32)


def iota(shape, dim):
    return lax.broadcasted_iota(jnp.int32, shape, dim)


def high_low(a):
    high = a.astype(BF)
    return high, (a - high.astype(F32)).astype(BF)


def rows_high_low(a):
    high = a.astype(BF).astype(F32)
    return jnp.concatenate([high, a - high], axis=0).astype(BF)


def cell_codes(cells):
    z = cells & (NGZ - 1)
    t = cells >> 5
    x = (t * 15421) >> 20
    y = t - x * WIDE_Y
    corner_x = jnp.min(x, axis=1, keepdims=True)
    corner_y = jnp.min(y, axis=1, keepdims=True)
    code = z * 16 + (x - corner_x) * 4 + (y & 3)
    return code, corner_x, corner_y


def one_hot_rows(code_row):
    return jnp.where(iota((512, 128), 0) == code_row, 1.0, 0.0).astype(BF)


def project_kernel(cur, proj, cells, tch, tcl, tsh, tsl, out, codes, boxed):
    code, corner_x, corner_y = cell_codes(cells[...])
    codes[...] = code

    def block(i, carry):
        for u in range(4):
            g = i * 4 + u
            lhs = rows_high_low(cur[g])
            p_high, p_low = high_low(proj[g])
            first = dot_nt(lhs, p_high)
            values = first[0:2] + first[2:4] + dot_nt(lhs, p_low)[0:2]
            hot = one_hot_rows(codes[pl.ds(g, 1), :])
            placed = dot_nt(rows_high_low(values), hot)
            boxed[pl.ds(g, 1), :] = placed[0:1] + placed[2:3]
            boxed[pl.ds(NB + g, 1), :] = placed[1:2] + placed[3:4]
        return carry

    lax.fori_loop(0, NB // 4, block, 0)
    b_high, b_low = high_low(boxed[...])
    along_cos = dot(b_high, tch[...]) + dot(b_low, tch[...]) + dot(b_high, tcl[...])
    along_sin = dot(b_high, tsh[...]) + dot(b_low, tsh[...]) + dot(b_high, tsl[...])
    real = along_cos[:NB] + along_sin[NB:]
    imag = along_cos[NB:] - along_sin[:NB]
    lane = iota((NB, 64), 1)
    corners = jnp.where(lane == 0, corner_x, jnp.where(lane == 1, corner_y, 0)).astype(F32)
    for c in range(NCOL):
        part = slice(32 * c, 32 * c + 32)
        out[c] = jnp.concatenate([real[:, part], imag[:, part], corners], axis=1).astype(BF)


def local_x_of_row(shape, dim):
    row = iota(shape, dim)
    return jnp.where(row < 130, row + 2, jnp.where(row >= 142, row - 142, -64))


def store_starts(recv, starts):
    block = iota((512, 1), 0)
    start = recv[:, 65:66].astype(jnp.int32) + (block // NB) * 64 - 2
    starts[NB : NB + 512, :] = jnp.broadcast_to(start, (512, 128))
    starts[0:NB, :] = starts[512 : 512 + NB, :]
    starts[NB + 512 :, :] = starts[NB : 2 * NB, :]


def chunk_mask(starts, q):
    cell = 128 * q + iota((128, 128), 1)
    inside = ((cell - starts[64 * q : 64 * q + 128, :]) & (N - 1)) < 4
    return jnp.where(inside, 1.0, 0.0)


def image_kernel(recv, spread, cos, sin, out, wide, starts, img):
    def spread_rows(i, carry):
        rows = pl.ds(pl.multiple_of(i * 128, 128), 128)
        wide_rows = pl.ds(pl.multiple_of(i * 128 + NB, NB), 128)
        wide[wide_rows, :] = dot(recv[rows, :], spread[...]).astype(BF)
        return carry

    lax.fori_loop(0, 4, spread_rows, 0)
    wide[0:NB, :] = wide[512 : 512 + NB, :]
    wide[NB + 512 :, :] = wide[NB : 2 * NB, :]
    store_starts(recv, starts)
    pick = jnp.where(iota((16, 128), 1) == 64, 1.0, 0.0).astype(BF)
    corner = dot_nt(pick, recv[...])[0:8]
    corner = jnp.concatenate([corner[:, 480:], corner, corner[:, :NB]], axis=1)
    local_x = local_x_of_row((XR, 128), 0)
    for q in range(8):
        mask = chunk_mask(starts, q).astype(BF)
        mask = jnp.concatenate([mask] * 4, axis=1)
        corner_q = corner[0:1, 64 * q : 64 * q + 128].astype(jnp.int32)
        offset = local_x - corner_q
        lhs = [jnp.where(offset == ex, 1.0, 0.0).astype(BF) for ex in range(4)]
        rhs = [wide[64 * q : 64 * q + 128, 512 * ex : 512 * ex + 512] * mask for ex in range(4)]
        cells = dot(jnp.concatenate(lhs, axis=1), jnp.concatenate(rhs, axis=0)).astype(BF)
        for p in range(4):
            img[XR * p : XR * p + XR, 128 * q : 128 * q + 128] = cells[:, 128 * p : 128 * p + 128]

    def along_y(i, carry):
        lanes = pl.ds(pl.multiple_of(i * 256, 256), 256)
        real, imag = img[0 : 2 * XR, :], img[2 * XR :, :]
        cos_i, sin_i = cos[:, lanes], sin[:, lanes]
        out_real = (dot(real, cos_i) + dot(imag, sin_i)).astype(BF)
        out_imag = (dot(imag, cos_i) - dot(real, sin_i)).astype(BF)
        for j in range(2):
            out[2 * i + j, 0 : 2 * XR, :] = out_real[:, 128 * j : 128 * j + 128]
            out[2 * i + j, 2 * XR :, :] = out_imag[:, 128 * j : 128 * j + 128]
        return carry

    lax.fori_loop(0, 4, along_y, 0)


def spectrum_kernel(recv, green, cos, sin, out, d_one, d_two, h_one, h_two):
    low_rows = iota((16, 128), 0) < 8
    for r in range(NROW):
        before, after = (r - 1) % NROW, (r + 1) % NROW
        for p in range(4):
            base = XR * p
            main = recv[r, base : base + 128, :]
            lower = recv[before, base + 128 : base + XR, :].astype(F32)
            upper = recv[after, base + 128 : base + XR, :].astype(F32)
            head = main[0:16].astype(F32) + jnp.where(low_rows, lower, 0.0)
            tail = main[112:128].astype(F32) + jnp.where(low_rows, 0.0, upper)
            band = jnp.concatenate([head.astype(BF), main[16:112], tail.astype(BF)], axis=0)
            d_one[128 * r : 128 * r + 128, 128 * p : 128 * p + 128] = band
            if p < 2:
                d_two[128 * r : 128 * r + 128, 256 + 128 * p : 384 + 128 * p] = -band
            else:
                d_two[128 * r : 128 * r + 128, 128 * p - 256 : 128 * p - 128] = band

    def forward(i, carry):
        rows = pl.ds(pl.multiple_of(i * 256, 256), 256)
        spec = dot(cos[rows, :], d_one[...]) + dot(sin[rows, :], d_two[...])
        real, imag = spec[:, :256], spec[:, 256:]
        g_real, g_imag = green[0, rows, :], green[1, rows, :]
        h_real = (real * g_real - imag * g_imag).astype(BF)
        h_imag = (real * g_imag + imag * g_real).astype(BF)
        h_one[rows, 0:256] = h_real
        h_one[rows, 256:512] = h_imag
        h_two[rows, 0:256] = -h_imag
        h_two[rows, 256:512] = h_real
        return carry

    lax.fori_loop(0, 4, forward, 0)

    def inverse(i, carry):
        rows = pl.ds(pl.multiple_of(i * 256, 256), 256)
        back = (dot(cos[rows, :], h_one[...]) + dot(sin[rows, :], h_two[...])).astype(BF)
        for j in range(2):
            for p in range(4):
                out[2 * i + j, XR * p : XR * p + 128, :] = back[
                    128 * j : 128 * j + 128, 128 * p : 128 * p + 128
                ]
        return carry

    lax.fori_loop(0, 4, inverse, 0)
    for r in range(NROW):
        before, after = (r - 1) % NROW, (r + 1) % NROW
        for p in range(4):
            base = XR * p
            above = out[after, base : base + 16, :].astype(F32)
            below = out[before, base + 112 : base + 128, :].astype(F32)
            out[r, base + 128 : base + XR, :] = jnp.where(low_rows, above, below).astype(BF)


def gather_kernel(recv, near_info, spread, cos, sin, out, spec, pot, starts, hot, acc):
    for r in range(NROW):
        spec[:, 128 * r : 128 * r + 128] = recv[r]

    def along_y(i, carry):
        lanes = pl.ds(pl.multiple_of(i * 256, 256), 256)
        real, imag = spec[0 : 2 * XR, :], spec[2 * XR :, :]
        cos_i, sin_i = cos[:, lanes], sin[:, lanes]
        pot[0 : 2 * XR, lanes] = (dot(real, cos_i) - dot(imag, sin_i)).astype(BF)
        pot[2 * XR :, lanes] = (dot(imag, cos_i) + dot(real, sin_i)).astype(BF)
        return carry

    lax.fori_loop(0, 4, along_y, 0)
    store_starts(near_info, starts)
    local_x = local_x_of_row((512, XR), 1)
    offset = local_x - near_info[:, 64:65].astype(jnp.int32)
    for ex in range(4):
        hot[ex, NB : NB + 512, :] = jnp.where(offset == ex, 1.0, 0.0).astype(BF)
    hot[:, 0:NB, :] = hot[:, 512 : 512 + NB, :]
    hot[:, NB + 512 :, :] = hot[:, NB : 2 * NB, :]
    acc[...] = jnp.zeros_like(acc)
    for q in range(8):
        mask = chunk_mask(starts, q)
        mask = jnp.concatenate([mask] * 4, axis=1)
        cells = [pot[XR * p : XR * p + XR, 128 * q : 128 * q + 128] for p in range(4)]
        cells = jnp.concatenate(cells, axis=1)
        rows = slice(64 * q, 64 * q + 128)
        for ex in range(4):
            taken = (dot(hot[ex, rows, :], cells) * mask).astype(BF)
            lanes = slice(512 * ex, 512 * ex + 512)
            acc[rows, lanes] = acc[rows, lanes] + taken
    acc[512 : 512 + NB, :] = acc[512 : 512 + NB, :] + acc[0:NB, :]
    acc[NB : 2 * NB, :] = acc[NB : 2 * NB, :] + acc[NB + 512 :, :]

    def fold(i, carry):
        rows = pl.ds(pl.multiple_of(i * 128, 128), 128)
        wide_rows = pl.ds(pl.multiple_of(i * 128 + NB, NB), 128)
        out[rows, :] = dot_nt(acc[wide_rows, :], spread[...]).astype(BF)
        return carry

    lax.fori_loop(0, 4, fold, 0)


def back_kernel(recv, proj, cells, near, tch, tcl, tsh, tsl, out, codes, box_real, box_imag):
    code, _, _ = cell_codes(cells[...])
    codes[...] = code
    real = jnp.concatenate([recv[c, :, 0:32] for c in range(NCOL)], axis=1)
    imag = jnp.concatenate([recv[c, :, 32:64] for c in range(NCOL)], axis=1)
    both = jnp.concatenate([real, imag], axis=0)
    along_cos = dot(both, tch[...]) + dot(both, tcl[...])
    along_sin = dot(both, tsh[...]) + dot(both, tsl[...])
    box_real[...] = along_cos[:NB] - along_sin[NB:]
    box_imag[...] = along_cos[NB:] + along_sin[:NB]

    def block(i, carry):
        for u in range(4):
            g = i * 4 + u
            box = jnp.concatenate([box_real[pl.ds(g, 1), :], box_imag[pl.ds(g, 1), :]], axis=0)
            hot = one_hot_rows(codes[pl.ds(g, 1), :])
            picked = dot(rows_high_low(box), hot)
            lhs = rows_high_low(picked[0:2] + picked[2:4])
            p_high, p_low = high_low(proj[g])
            first = dot(lhs, p_high)
            out[g] = first[0:2] + first[2:4] + dot(lhs, p_low)[0:2] + near[g]
        return carry

    lax.fori_loop(0, NB // 4, block, 0)


def call(kernel, out_shape, scratch, *args):
    return pl.pallas_call(
        kernel,
        out_shape=out_shape,
        in_specs=[pl.BlockSpec(memory_space=pltpu.VMEM)] * len(args),
        out_specs=pl.BlockSpec(memory_space=pltpu.VMEM),
        scratch_shapes=scratch,
        compiler_params=pltpu.CompilerParams(vmem_limit_bytes=VMEM_LIMIT),
    )(*args)


def with_halo(value, sides, width):
    for axis, dim in sides:
        peers, length = (lax.axis_size(axis), value.shape[dim])
        up = [(i, (i + 1) % peers) for i in range(peers)]
        down = [(j, i) for i, j in up]
        last = lax.slice_in_dim(value, length - width, length, axis=dim)
        first = lax.slice_in_dim(value, 0, width, axis=dim)
        before = lax.ppermute(last, axis, up)
        after = lax.ppermute(first, axis, down)
        value = jnp.concatenate([before, value, after], axis=dim)
    return value


def combine_parts(products):
    return jnp.stack(
        [products[:, 0, 0] - products[:, 1, 1], products[:, 0, 1] + products[:, 1, 0]], axis=1
    )


def fold_rims(field, axis_pos, inner, width):
    middle = lax.slice_in_dim(field, 2 * width, 2 * width + inner, axis=axis_pos)
    lower = lax.slice_in_dim(field, 0, width, axis=axis_pos)
    upper = lax.slice_in_dim(field, inner + 3 * width, inner + 4 * width, axis=axis_pos)
    lower_pads = [(0, 0)] * field.ndim
    upper_pads = [(0, 0)] * field.ndim
    lower_pads[axis_pos] = (0, inner - width)
    upper_pads[axis_pos] = (inner - width, 0)
    return middle + jnp.pad(lower, lower_pads) + jnp.pad(upper, upper_pads)


def near_part(blocks, near_blocks, pair_local, pair_ghost, pair_counts):
    num_blocks, block_len = NB, BLK
    pair_slots = pair_ghost.shape[1]
    high = lax.Precision.HIGHEST
    local_bf = blocks.astype(BF)
    beside_all = with_halo(
        local_bf.reshape(2, 1, 1, num_blocks, block_len), (("row", 1), ("col", 2)), 1
    )
    beside_all = beside_all.reshape(2, 9 * num_blocks, block_len)
    picks = pair_ghost[0]
    owned = pair_local[0]
    living = (jnp.arange(pair_slots, dtype=jnp.int32) < pair_counts[0]).astype(F32)
    owner_table = owned[:, None] == jnp.arange(num_blocks, dtype=jnp.int32)[None, :]
    ghost_table = picks[:, None] == jnp.arange(9 * num_blocks, dtype=jnp.int32)[None, :]
    remote_vals = jnp.einsum(
        "ho,som->shm", ghost_table.astype(BF), beside_all, preferred_element_type=F32
    ).astype(BF)
    local_vals = jnp.einsum(
        "ho,som->shm", owner_table.astype(BF), local_bf, preferred_element_type=F32
    ).astype(BF)
    onward = jnp.einsum("pcij,dpj->pcdi", near_blocks, remote_vals, preferred_element_type=F32)
    backward = jnp.einsum("pcij,dpi->pcdj", near_blocks, local_vals, preferred_element_type=F32)
    onward = combine_parts(onward) * living[:, None, None]
    backward = combine_parts(backward) * living[:, None, None]
    near_own = jnp.einsum("pn,pcb->cnb", owner_table.astype(F32), onward, precision=high)
    spread_back = jnp.einsum("pn,pcb->cnb", ghost_table.astype(F32), backward, precision=high)
    spread_back = spread_back.reshape(2, 3, 3, num_blocks, block_len)
    widened_back = with_halo(spread_back.astype(BF), (("row", 1), ("col", 2)), 1).astype(F32)
    returned = fold_rims(fold_rims(widened_back, 1, 1, 1), 2, 1, 1).reshape(
        2, num_blocks, block_len
    )
    return near_own + returned


def per_device(
    currents, near_blocks, pair_local, pair_ghost, pair_counts, projection, stencil_cells, green
):
    cos, sin = (jnp.asarray(t) for t in grid_tables())
    depth = [jnp.asarray(t) for t in depth_tables()]
    spread = jnp.asarray(spread_table())
    shape = jax.ShapeDtypeStruct
    blocks = currents.reshape(2, NB, BLK)
    near = near_part(blocks, near_blocks, pair_local, pair_ghost, pair_counts)
    messages = call(
        project_kernel,
        shape((NCOL, NB, 128), BF),
        [pltpu.VMEM((NB, 128), jnp.int32), pltpu.VMEM((2 * NB, 512), F32)],
        jnp.transpose(blocks, (1, 0, 2)),
        projection,
        stencil_cells,
        *depth,
    )
    sources = lax.all_to_all(messages, "col", split_axis=0, concat_axis=0, tiled=True)
    sources = sources.reshape(NCOL * NB, 128)
    bands = call(
        image_kernel,
        shape((NROW, 4 * XR, 128), BF),
        [
            pltpu.VMEM((512 + 2 * NB, 2048), BF),
            pltpu.VMEM((512 + 2 * NB, 128), jnp.int32),
            pltpu.VMEM((4 * XR, N), BF),
        ],
        sources,
        spread,
        cos,
        sin,
    )
    pencils = lax.all_to_all(bands, "row", split_axis=0, concat_axis=0, tiled=True)
    turned = jnp.transpose(green, (0, 3, 1, 2)).reshape(2, N, 256) * (1.0 / (N * N * NGZ))
    pencils = call(
        spectrum_kernel,
        shape((NROW, 4 * XR, 128), BF),
        [pltpu.VMEM((N, 512), BF)] * 4,
        pencils,
        turned,
        cos,
        sin,
    )
    bands = lax.all_to_all(pencils, "row", split_axis=0, concat_axis=0, tiled=True)
    taken = call(
        gather_kernel,
        shape((NCOL * NB, 128), BF),
        [
            pltpu.VMEM((4 * XR, N), BF),
            pltpu.VMEM((4 * XR, N), BF),
            pltpu.VMEM((512 + 2 * NB, 128), jnp.int32),
            pltpu.VMEM((4, 512 + 2 * NB, XR), BF),
            pltpu.VMEM((512 + 2 * NB, 2048), BF),
        ],
        bands,
        sources,
        spread,
        cos,
        sin,
    )
    messages = lax.all_to_all(
        taken.reshape(NCOL, NB, 128), "col", split_axis=0, concat_axis=0, tiled=True
    )
    total = call(
        back_kernel,
        shape((NB, 2, BLK), F32),
        [pltpu.VMEM((NB, 128), jnp.int32), pltpu.VMEM((NB, 512), F32), pltpu.VMEM((NB, 512), F32)],
        messages,
        projection,
        stencil_cells,
        jnp.transpose(near, (1, 0, 2)),
        *depth,
    )
    return jnp.transpose(total, (1, 0, 2)).reshape(2, NB * BLK)


def solution(mesh):
    in_specs = (
        P(None, ("row", "col")),
        P(("row", "col"), None, None, None),
        P(("row", "col"), None),
        P(("row", "col"), None),
        P(("row", "col")),
        P(("row", "col"), None, None),
        P(("row", "col"), None),
        P(None, "col", "row", None),
    )
    out_specs = P(None, ("row", "col"))
    return jax.shard_map(
        per_device, mesh=mesh, in_specs=in_specs, out_specs=out_specs, check_vma=False
    )
```

```python
import math

import jax
import jax.numpy as jnp
import ml_dtypes
import numpy as np
from jax import lax
from jax.experimental import pallas as pl
from jax.experimental.pallas import tpu as pltpu
from jax.sharding import PartitionSpec as P

N = 1024
NGZ = 32
NROW = 8
NCOL = 16
NB = 32
BLK = 128
XR = 144
WIDE_Y = 68
BF = jnp.bfloat16
F32 = jnp.float32
VMEM_LIMIT = 60 * 1024 * 1024


def bf(a):
    return np.asarray(a, dtype=np.float64).astype(ml_dtypes.bfloat16)


def split_np(a):
    high = bf(a)
    return high, bf(a - high.astype(np.float64))


def grid_tables():
    index = np.arange(N)[:, None] * np.arange(N)[None, :] % N
    angle = index * (2.0 * math.pi / N)
    return bf(np.cos(angle)), bf(np.sin(angle))


def depth_tables():
    index = np.arange(NGZ)[:, None] * np.arange(NGZ)[None, :] % NGZ
    angle = index * (2.0 * math.pi / NGZ)
    eye = np.eye(16)
    cos_high, cos_low = split_np(np.kron(np.cos(angle), eye))
    sin_high, sin_low = split_np(np.kron(np.sin(angle), eye))
    return cos_high, cos_low, sin_high, sin_low


def spread_table():
    lane = np.arange(128)[:, None]
    plane, ex, b = lane // 16, lane // 4 % 4, lane % 4
    wide = np.arange(2048)[None, :]
    hits = (wide // 512 == ex) & (wide // 128 % 4 == plane) & ((wide + 2) % 4 == b) & (lane < 64)
    return bf(hits.astype(np.float64))


def dot(a, b):
    return jnp.dot(a, b, preferred_element_type=F32)


def dot_nt(a, b):
    return lax.dot_general(a, b, (((1,), (1,)), ((), ())), preferred_element_type=F32)


def iota(shape, dim):
    return lax.broadcasted_iota(jnp.int32, shape, dim)


def high_low(a):
    high = a.astype(BF)
    return high, (a - high.astype(F32)).astype(BF)


def rows_high_low(a):
    high = a.astype(BF).astype(F32)
    return jnp.concatenate([high, a - high], axis=0).astype(BF)


def cell_codes(cells):
    z = cells & (NGZ - 1)
    t = cells >> 5
    x = (t * 15421) >> 20
    y = t - x * WIDE_Y
    corner_x = jnp.min(x, axis=1, keepdims=True)
    corner_y = jnp.min(y, axis=1, keepdims=True)
    code = z * 16 + (x - corner_x) * 4 + (y & 3)
    return code, corner_x, corner_y


def one_hot_rows(code_row):
    return jnp.where(iota((512, 128), 0) == code_row, 1.0, 0.0).astype(BF)


def project_kernel(cur, proj, cells, tch, tcl, tsh, tsl, out, codes, boxed):
    code, corner_x, corner_y = cell_codes(cells[...])
    codes[...] = code

    def block(i, carry):
        for u in range(4):
            g = i * 4 + u
            lhs = rows_high_low(cur[g])
            p_high, p_low = high_low(proj[g])
            first = dot_nt(lhs, p_high)
            values = first[0:2] + first[2:4] + dot_nt(lhs, p_low)[0:2]
            hot = one_hot_rows(codes[pl.ds(g, 1), :])
            placed = dot_nt(rows_high_low(values), hot)
            boxed[pl.ds(g, 1), :] = placed[0:1] + placed[2:3]
            boxed[pl.ds(NB + g, 1), :] = placed[1:2] + placed[3:4]
        return carry

    lax.fori_loop(0, NB // 4, block, 0)
    b_high, b_low = high_low(boxed[...])
    along_cos = dot(b_high, tch[...]) + dot(b_low, tch[...]) + dot(b_high, tcl[...])
    along_sin = dot(b_high, tsh[...]) + dot(b_low, tsh[...]) + dot(b_high, tsl[...])
    real = along_cos[:NB] + along_sin[NB:]
    imag = along_cos[NB:] - along_sin[:NB]
    lane = iota((NB, 64), 1)
    corners = jnp.where(lane == 0, corner_x, jnp.where(lane == 1, corner_y, 0)).astype(F32)
    for c in range(NCOL):
        part = slice(32 * c, 32 * c + 32)
        out[c] = jnp.concatenate([real[:, part], imag[:, part], corners], axis=1).astype(BF)


def local_x_of_row(shape, dim):
    row = iota(shape, dim)
    return jnp.where(row < 130, row + 2, jnp.where(row >= 142, row - 142, -64))


def store_starts(recv, starts):
    block = iota((512, 1), 0)
    start = recv[:, 65:66].astype(jnp.int32) + (block // NB) * 64 - 2
    starts[NB : NB + 512, :] = jnp.broadcast_to(start, (512, 128))
    starts[0:NB, :] = starts[512 : 512 + NB, :]
    starts[NB + 512 :, :] = starts[NB : 2 * NB, :]


def chunk_mask(starts, q):
    cell = 128 * q + iota((128, 128), 1)
    inside = ((cell - starts[64 * q : 64 * q + 128, :]) & (N - 1)) < 4
    return jnp.where(inside, 1.0, 0.0)


def build_image(recv, spread, wide, starts, img):
    def spread_rows(i, carry):
        rows = pl.ds(pl.multiple_of(i * 128, 128), 128)
        wide_rows = pl.ds(pl.multiple_of(i * 128 + NB, NB), 128)
        wide[wide_rows, :] = dot(recv[rows, :], spread[...]).astype(BF)
        return carry

    lax.fori_loop(0, 4, spread_rows, 0)
    wide[0:NB, :] = wide[512 : 512 + NB, :]
    wide[NB + 512 :, :] = wide[NB : 2 * NB, :]
    store_starts(recv, starts)
    pick = jnp.where(iota((16, 128), 1) == 64, 1.0, 0.0).astype(BF)
    corner = dot_nt(pick, recv[...])[0:8]
    corner = jnp.concatenate([corner[:, 480:], corner, corner[:, :NB]], axis=1)
    local_x = local_x_of_row((XR, 128), 0)
    for q in range(8):
        mask = chunk_mask(starts, q).astype(BF)
        mask = jnp.concatenate([mask] * 4, axis=1)
        corner_q = corner[0:1, 64 * q : 64 * q + 128].astype(jnp.int32)
        offset = local_x - corner_q
        lhs = [jnp.where(offset == ex, 1.0, 0.0).astype(BF) for ex in range(4)]
        rhs = [wide[64 * q : 64 * q + 128, 512 * ex : 512 * ex + 512] * mask for ex in range(4)]
        cells = dot(jnp.concatenate(lhs, axis=1), jnp.concatenate(rhs, axis=0)).astype(BF)
        for kz in range(2):
            for c in range(2):
                p = 2 * c + kz
                img[kz, XR * c : XR * c + XR, 128 * q : 128 * q + 128] = cells[:, 128 * p : 128 * p + 128]


def forward_y(kz, img, cos, sin, out):
    def lanes_of(i, carry):
        lanes = pl.ds(pl.multiple_of(i * 256, 256), 256)
        by_cos = dot(img[kz], cos[:, lanes])
        by_sin = dot(img[kz], sin[:, lanes])
        real = (by_cos[:XR] + by_sin[XR:]).astype(BF)
        imag = (by_cos[XR:] - by_sin[:XR]).astype(BF)
        for j in range(2):
            out[kz, 2 * i + j, 0:XR, :] = real[:, 128 * j : 128 * j + 128]
            out[kz, 2 * i + j, XR:, :] = imag[:, 128 * j : 128 * j + 128]
        return carry

    lax.fori_loop(0, 4, lanes_of, 0)


def along_x(kz, recv, green, cos, sin, out, d_one, d_two, h_one, h_two):
    low_rows = iota((16, 128), 0) < 8

    def gather_band(r, carry):
        before, after = lax.rem(r + NROW - 1, NROW), lax.rem(r + 1, NROW)
        rows = pl.ds(pl.multiple_of(r * 128, 128), 128)
        for c in range(2):
            base = XR * c
            main = recv[kz, r, base : base + 128, :]
            lower = recv[kz, before, base + 128 : base + XR, :].astype(F32)
            upper = recv[kz, after, base + 128 : base + XR, :].astype(F32)
            head = main[0:16].astype(F32) + jnp.where(low_rows, lower, 0.0)
            tail = main[112:128].astype(F32) + jnp.where(low_rows, 0.0, upper)
            band = jnp.concatenate([head.astype(BF), main[16:112], tail.astype(BF)], axis=0)
            d_one[rows, 128 * c : 128 * c + 128] = band
            if c == 0:
                d_two[rows, 128:256] = -band
            else:
                d_two[rows, 0:128] = band
        return carry

    lax.fori_loop(0, NROW, gather_band, 0)

    def forward(i, carry):
        rows = pl.ds(pl.multiple_of(i * 256, 256), 256)
        spec = dot(cos[rows, :], d_one[...]) + dot(sin[rows, :], d_two[...])
        real, imag = spec[:, :128], spec[:, 128:]
        lanes = slice(128 * kz, 128 * kz + 128)
        g_real, g_imag = green[0, rows, lanes], green[1, rows, lanes]
        h_real = (real * g_real - imag * g_imag).astype(BF)
        h_imag = (real * g_imag + imag * g_real).astype(BF)
        h_one[rows, 0:128] = h_real
        h_one[rows, 128:256] = h_imag
        h_two[rows, 0:128] = -h_imag
        h_two[rows, 128:256] = h_real
        return carry

    lax.fori_loop(0, 4, forward, 0)

    def inverse(i, carry):
        rows = pl.ds(pl.multiple_of(i * 256, 256), 256)
        back = (dot(cos[rows, :], h_one[...]) + dot(sin[rows, :], h_two[...])).astype(BF)
        for j in range(2):
            for c in range(2):
                out[kz, 2 * i + j, XR * c : XR * c + 128, :] = back[
                    128 * j : 128 * j + 128, 128 * c : 128 * c + 128
                ]
        return carry

    lax.fori_loop(0, 4, inverse, 0)

    def rims(r, carry):
        before, after = lax.rem(r + NROW - 1, NROW), lax.rem(r + 1, NROW)
        for c in range(2):
            base = XR * c
            above = out[kz, after, base : base + 16, :].astype(F32)
            below = out[kz, before, base + 112 : base + 128, :].astype(F32)
            out[kz, r, base + 128 : base + XR, :] = jnp.where(low_rows, above, below).astype(BF)
        return carry

    lax.fori_loop(0, NROW, rims, 0)


def inverse_y(kz, recv, cos, sin, spec, pot):
    for r in range(NROW):
        spec[:, 128 * r : 128 * r + 128] = recv[kz, r]

    def lanes_of(i, carry):
        lanes = pl.ds(pl.multiple_of(i * 256, 256), 256)
        by_cos = dot(spec[...], cos[:, lanes])
        by_sin = dot(spec[...], sin[:, lanes])
        pot[0:XR, lanes] = (by_cos[:XR] - by_sin[XR:]).astype(BF)
        pot[XR:, lanes] = (by_cos[XR:] + by_sin[:XR]).astype(BF)
        return carry

    lax.fori_loop(0, 4, lanes_of, 0)


def build_hot(recv, hot):
    local_x = local_x_of_row((512, XR), 1)
    offset = local_x - recv[:, 64:65].astype(jnp.int32)
    for ex in range(4):
        hot[ex, NB : NB + 512, :] = jnp.where(offset == ex, 1.0, 0.0).astype(BF)
    hot[:, 0:NB, :] = hot[:, 512 : 512 + NB, :]
    hot[:, NB + 512 :, :] = hot[:, NB : 2 * NB, :]


def pick_cells(kz, pot, starts, hot, acc):
    for q in range(8):
        mask = chunk_mask(starts, q)
        mask = jnp.concatenate([mask] * 2, axis=1)
        cells = [pot[XR * c : XR * c + XR, 128 * q : 128 * q + 128] for c in range(2)]
        cells = jnp.concatenate(cells, axis=1)
        rows = slice(64 * q, 64 * q + 128)
        for ex in range(4):
            taken = (dot(hot[ex, rows, :], cells) * mask).astype(BF)
            for c in range(2):
                lane = 512 * ex + 256 * c + 128 * kz
                lanes = slice(lane, lane + 128)
                acc[rows, lanes] = acc[rows, lanes] + taken[:, 128 * c : 128 * c + 128]


def middle_kernel(
    recv, spread, green, cos, sin, out,
    wide, starts, img, hot, acc, spec, pot, d_one, d_two, h_one, h_two,
    send_a, recv_a, send_b, recv_b, sem_send_a, sem_recv_a, sem_send_b, sem_recv_b,
):
    me = lax.axis_index("row")
    barrier = pltpu.get_barrier_semaphore()
    for j in range(1, NROW):
        peer = lax.rem(me + j, NROW)
        pl.semaphore_signal(
            barrier, inc=1, device_id={"row": peer}, device_id_type=pl.DeviceIdType.MESH
        )

    def copies(kz, source, target, sem_send, sem_recv):
        result = []
        for j in range(1, NROW):
            peer = lax.rem(me + j, NROW)
            result.append(
                pltpu.make_async_remote_copy(
                    src_ref=source.at[kz, peer],
                    dst_ref=target.at[kz, me],
                    send_sem=sem_send.at[kz, j],
                    recv_sem=sem_recv.at[kz, j],
                    device_id={"row": peer},
                    device_id_type=pl.DeviceIdType.MESH,
                )
            )
        return result

    build_image(recv, spread, wide, starts, img)
    first, second = [], []
    for kz in range(2):
        forward_y(kz, img, cos, sin, send_a)
        if kz == 0:
            pl.semaphore_wait(barrier, NROW - 1)
        first.append(copies(kz, send_a, recv_a, sem_send_a, sem_recv_a))
        for copy in first[kz]:
            copy.start()
        recv_a[kz, me] = send_a[kz, me]
    build_hot(recv, hot)
    acc[...] = jnp.zeros_like(acc)
    for kz in range(2):
        for copy in first[kz]:
            copy.wait_recv()
        along_x(kz, recv_a, green, cos, sin, send_b, d_one, d_two, h_one, h_two)
        second.append(copies(kz, send_b, recv_b, sem_send_b, sem_recv_b))
        for copy in second[kz]:
            copy.start()
        recv_b[kz, me] = send_b[kz, me]
    for kz in range(2):
        for copy in second[kz]:
            copy.wait_recv()
        inverse_y(kz, recv_b, cos, sin, spec, pot)
        pick_cells(kz, pot, starts, hot, acc)
    acc[512 : 512 + NB, :] = acc[512 : 512 + NB, :] + acc[0:NB, :]
    acc[NB : 2 * NB, :] = acc[NB : 2 * NB, :] + acc[NB + 512 :, :]

    def fold(i, carry):
        rows = pl.ds(pl.multiple_of(i * 128, 128), 128)
        wide_rows = pl.ds(pl.multiple_of(i * 128 + NB, NB), 128)
        out[rows, :] = dot_nt(acc[wide_rows, :], spread[...]).astype(BF)
        return carry

    lax.fori_loop(0, 4, fold, 0)
    for kz in range(2):
        for copy in first[kz] + second[kz]:
            copy.wait_send()


def back_kernel(recv, proj, cells, near, tch, tcl, tsh, tsl, out, codes, box_real, box_imag):
    code, _, _ = cell_codes(cells[...])
    codes[...] = code
    real = jnp.concatenate([recv[c, :, 0:32] for c in range(NCOL)], axis=1)
    imag = jnp.concatenate([recv[c, :, 32:64] for c in range(NCOL)], axis=1)
    both = jnp.concatenate([real, imag], axis=0)
    along_cos = dot(both, tch[...]) + dot(both, tcl[...])
    along_sin = dot(both, tsh[...]) + dot(both, tsl[...])
    box_real[...] = along_cos[:NB] - along_sin[NB:]
    box_imag[...] = along_cos[NB:] + along_sin[:NB]

    def block(i, carry):
        for u in range(4):
            g = i * 4 + u
            box = jnp.concatenate([box_real[pl.ds(g, 1), :], box_imag[pl.ds(g, 1), :]], axis=0)
            hot = one_hot_rows(codes[pl.ds(g, 1), :])
            picked = dot(rows_high_low(box), hot)
            lhs = rows_high_low(picked[0:2] + picked[2:4])
            p_high, p_low = high_low(proj[g])
            first = dot(lhs, p_high)
            out[g] = first[0:2] + first[2:4] + dot(lhs, p_low)[0:2] + near[g]
        return carry

    lax.fori_loop(0, NB // 4, block, 0)


def call(kernel, out_shape, scratch, *args, **params):
    return pl.pallas_call(
        kernel,
        out_shape=out_shape,
        in_specs=[pl.BlockSpec(memory_space=pltpu.VMEM)] * len(args),
        out_specs=pl.BlockSpec(memory_space=pltpu.VMEM),
        scratch_shapes=scratch,
        compiler_params=pltpu.CompilerParams(vmem_limit_bytes=VMEM_LIMIT, **params),
    )(*args)


def with_halo(value, sides, width):
    for axis, dim in sides:
        peers, length = (lax.axis_size(axis), value.shape[dim])
        up = [(i, (i + 1) % peers) for i in range(peers)]
        down = [(j, i) for i, j in up]
        last = lax.slice_in_dim(value, length - width, length, axis=dim)
        first = lax.slice_in_dim(value, 0, width, axis=dim)
        before = lax.ppermute(last, axis, up)
        after = lax.ppermute(first, axis, down)
        value = jnp.concatenate([before, value, after], axis=dim)
    return value


def combine_parts(products):
    return jnp.stack(
        [products[:, 0, 0] - products[:, 1, 1], products[:, 0, 1] + products[:, 1, 0]], axis=1
    )


def fold_rims(field, axis_pos, inner, width):
    middle = lax.slice_in_dim(field, 2 * width, 2 * width + inner, axis=axis_pos)
    lower = lax.slice_in_dim(field, 0, width, axis=axis_pos)
    upper = lax.slice_in_dim(field, inner + 3 * width, inner + 4 * width, axis=axis_pos)
    lower_pads = [(0, 0)] * field.ndim
    upper_pads = [(0, 0)] * field.ndim
    lower_pads[axis_pos] = (0, inner - width)
    upper_pads[axis_pos] = (inner - width, 0)
    return middle + jnp.pad(lower, lower_pads) + jnp.pad(upper, upper_pads)


def near_part(blocks, near_blocks, pair_local, pair_ghost, pair_counts):
    num_blocks, block_len = NB, BLK
    pair_slots = pair_ghost.shape[1]
    high = lax.Precision.HIGHEST
    local_bf = blocks.astype(BF)
    beside_all = with_halo(
        local_bf.reshape(2, 1, 1, num_blocks, block_len), (("row", 1), ("col", 2)), 1
    )
    beside_all = beside_all.reshape(2, 9 * num_blocks, block_len)
    picks = pair_ghost[0]
    owned = pair_local[0]
    living = (jnp.arange(pair_slots, dtype=jnp.int32) < pair_counts[0]).astype(F32)
    owner_table = owned[:, None] == jnp.arange(num_blocks, dtype=jnp.int32)[None, :]
    ghost_table = picks[:, None] == jnp.arange(9 * num_blocks, dtype=jnp.int32)[None, :]
    remote_vals = jnp.einsum(
        "ho,som->shm", ghost_table.astype(BF), beside_all, preferred_element_type=F32
    ).astype(BF)
    local_vals = jnp.einsum(
        "ho,som->shm", owner_table.astype(BF), local_bf, preferred_element_type=F32
    ).astype(BF)
    onward = jnp.einsum("pcij,dpj->pcdi", near_blocks, remote_vals, preferred_element_type=F32)
    backward = jnp.einsum("pcij,dpi->pcdj", near_blocks, local_vals, preferred_element_type=F32)
    onward = combine_parts(onward) * living[:, None, None]
    backward = combine_parts(backward) * living[:, None, None]
    near_own = jnp.einsum("pn,pcb->cnb", owner_table.astype(F32), onward, precision=high)
    spread_back = jnp.einsum("pn,pcb->cnb", ghost_table.astype(F32), backward, precision=high)
    spread_back = spread_back.reshape(2, 3, 3, num_blocks, block_len)
    widened_back = with_halo(spread_back.astype(BF), (("row", 1), ("col", 2)), 1).astype(F32)
    returned = fold_rims(fold_rims(widened_back, 1, 1, 1), 2, 1, 1).reshape(
        2, num_blocks, block_len
    )
    return near_own + returned


def per_device(
    currents, near_blocks, pair_local, pair_ghost, pair_counts, projection, stencil_cells, green
):
    cos, sin = (jnp.asarray(t) for t in grid_tables())
    depth = [jnp.asarray(t) for t in depth_tables()]
    spread = jnp.asarray(spread_table())
    shape = jax.ShapeDtypeStruct
    blocks = currents.reshape(2, NB, BLK)
    near = near_part(blocks, near_blocks, pair_local, pair_ghost, pair_counts)
    messages = call(
        project_kernel,
        shape((NCOL, NB, 128), BF),
        [pltpu.VMEM((NB, 128), jnp.int32), pltpu.VMEM((2 * NB, 512), F32)],
        jnp.transpose(blocks, (1, 0, 2)),
        projection,
        stencil_cells,
        *depth,
    )
    sources = lax.all_to_all(messages, "col", split_axis=0, concat_axis=0, tiled=True)
    sources = sources.reshape(NCOL * NB, 128)
    turned = jnp.transpose(green, (0, 3, 1, 2)).reshape(2, N, 256) * (1.0 / (N * N * NGZ))
    grid_bytes = (2, NROW, 2 * XR, 128)
    taken = call(
        middle_kernel,
        shape((NCOL * NB, 128), BF),
        [
            pltpu.VMEM((512 + 2 * NB, 2048), BF),
            pltpu.VMEM((512 + 2 * NB, 128), jnp.int32),
            pltpu.VMEM((2, 2 * XR, N), BF),
            pltpu.VMEM((4, 512 + 2 * NB, XR), BF),
            pltpu.VMEM((512 + 2 * NB, 2048), BF),
            pltpu.VMEM((2 * XR, N), BF),
            pltpu.VMEM((2 * XR, N), BF),
        ]
        + [pltpu.VMEM((N, 256), BF)] * 4
        + [pltpu.VMEM(grid_bytes, BF)] * 4
        + [pltpu.SemaphoreType.DMA((2, NROW))] * 4,
        sources,
        spread,
        turned,
        cos,
        sin,
        collective_id=1,
        has_side_effects=True,
    )
    messages = lax.all_to_all(
        taken.reshape(NCOL, NB, 128), "col", split_axis=0, concat_axis=0, tiled=True
    )
    total = call(
        back_kernel,
        shape((NB, 2, BLK), F32),
        [pltpu.VMEM((NB, 128), jnp.int32), pltpu.VMEM((NB, 512), F32), pltpu.VMEM((NB, 512), F32)],
        messages,
        projection,
        stencil_cells,
        jnp.transpose(near, (1, 0, 2)),
        *depth,
    )
    return jnp.transpose(total, (1, 0, 2)).reshape(2, NB * BLK)


def solution(mesh):
    in_specs = (
        P(None, ("row", "col")),
        P(("row", "col"), None, None, None),
        P(("row", "col"), None),
        P(("row", "col"), None),
        P(("row", "col")),
        P(("row", "col"), None, None),
        P(("row", "col"), None),
        P(None, "col", "row", None),
    )
    out_specs = P(None, ("row", "col"))
    return jax.shard_map(
        per_device, mesh=mesh, in_specs=in_specs, out_specs=out_specs, check_vma=False
    )
```

```python
import math

import jax
import jax.numpy as jnp
import ml_dtypes
import numpy as np
from jax import lax
from jax.experimental import pallas as pl
from jax.experimental.pallas import tpu as pltpu
from jax.sharding import PartitionSpec as P

N = 1024
NGZ = 32
NROW = 8
NCOL = 16
NB = 32
BLK = 128
PAIRS = 128
XR = 144
WIDE_Y = 68
BF = jnp.bfloat16
F32 = jnp.float32
VMEM_LIMIT = 60 * 1024 * 1024


def bf(a):
    return np.asarray(a, dtype=np.float64).astype(ml_dtypes.bfloat16)


def split_np(a):
    high = bf(a)
    return high, bf(a - high.astype(np.float64))


def grid_tables():
    index = np.arange(N)[:, None] * np.arange(N)[None, :] % N
    angle = index * (2.0 * math.pi / N)
    return bf(np.cos(angle)), bf(np.sin(angle))


def depth_tables():
    index = np.arange(NGZ)[:, None] * np.arange(NGZ)[None, :] % NGZ
    angle = index * (2.0 * math.pi / NGZ)
    eye = np.eye(16)
    cos_high, cos_low = split_np(np.kron(np.cos(angle), eye))
    sin_high, sin_low = split_np(np.kron(np.sin(angle), eye))
    return cos_high, cos_low, sin_high, sin_low


def spread_table():
    lane = np.arange(128)[:, None]
    plane, ex, b = lane // 16, lane // 4 % 4, lane % 4
    wide = np.arange(2048)[None, :]
    hits = (wide // 512 == ex) & (wide // 128 % 4 == plane) & ((wide + 2) % 4 == b) & (lane < 64)
    return bf(hits.astype(np.float64))


def dot(a, b):
    return jnp.dot(a, b, preferred_element_type=F32)


def dot_nt(a, b):
    return lax.dot_general(a, b, (((1,), (1,)), ((), ())), preferred_element_type=F32)


def iota(shape, dim):
    return lax.broadcasted_iota(jnp.int32, shape, dim)


def high_low(a):
    high = a.astype(BF)
    return high, (a - high.astype(F32)).astype(BF)


def rows_high_low(a):
    high = a.astype(BF).astype(F32)
    return jnp.concatenate([high, a - high], axis=0).astype(BF)


def cell_codes(cells):
    z = cells & (NGZ - 1)
    t = cells >> 5
    x = (t * 15421) >> 20
    y = t - x * WIDE_Y
    corner_x = jnp.min(x, axis=1, keepdims=True)
    corner_y = jnp.min(y, axis=1, keepdims=True)
    code = z * 16 + (x - corner_x) * 4 + (y & 3)
    return code, corner_x, corner_y


def one_hot_rows(code_row):
    return jnp.where(iota((512, 128), 0) == code_row, 1.0, 0.0).astype(BF)


def project(cur, proj, cells, tch, tcl, tsh, tsl, out, codes, p_high, p_low, hots, vals, boxed):
    code, corner_x, corner_y = cell_codes(cells[...])
    codes[...] = code

    def values_of(i, carry):
        for u in range(8):
            g = i * 8 + u
            lhs = rows_high_low(cur[:, pl.ds(pl.multiple_of(g * BLK, BLK), BLK)])
            high, low = high_low(proj[g])
            p_high[g] = high
            p_low[g] = low
            first = dot_nt(lhs, high)
            vals[g] = first[0:2] + first[2:4] + dot_nt(lhs, low)[0:2]
        return carry

    lax.fori_loop(0, NB // 8, values_of, 0)

    def boxes_of(i, carry):
        for u in range(8):
            g = i * 8 + u
            hot = one_hot_rows(codes[pl.ds(g, 1), :])
            hots[g] = hot
            placed = dot_nt(rows_high_low(vals[g]), hot)
            boxed[pl.ds(g, 1), :] = placed[0:1] + placed[2:3]
            boxed[pl.ds(NB + g, 1), :] = placed[1:2] + placed[3:4]
        return carry

    lax.fori_loop(0, NB // 8, boxes_of, 0)
    b_high, b_low = high_low(boxed[...])
    along_cos = dot(b_high, tch[...]) + dot(b_low, tch[...]) + dot(b_high, tcl[...])
    along_sin = dot(b_high, tsh[...]) + dot(b_low, tsh[...]) + dot(b_high, tsl[...])
    real = along_cos[:NB] + along_sin[NB:]
    imag = along_cos[NB:] - along_sin[:NB]
    lane = iota((NB, 64), 1)
    corners = jnp.where(lane == 0, corner_x, jnp.where(lane == 1, corner_y, 0)).astype(F32)
    for c in range(NCOL):
        part = slice(32 * c, 32 * c + 32)
        message = jnp.concatenate([real[:, part], imag[:, part], corners], axis=1)
        out[NB * c : NB * c + NB, :] = message.astype(BF)


def local_x_of_row(shape, dim):
    row = iota(shape, dim)
    return jnp.where(row < 130, row + 2, jnp.where(row >= 142, row - 142, -64))


def store_starts(recv, starts):
    block = iota((512, 1), 0)
    start = recv[:, 65:66].astype(jnp.int32) + (block // NB) * 64 - 2
    starts[NB : NB + 512, :] = jnp.broadcast_to(start, (512, 128))
    starts[0:NB, :] = starts[512 : 512 + NB, :]
    starts[NB + 512 :, :] = starts[NB : 2 * NB, :]


def chunk_mask(starts, q):
    cell = 128 * q + iota((128, 128), 1)
    inside = ((cell - starts[64 * q : 64 * q + 128, :]) & (N - 1)) < 4
    return jnp.where(inside, 1.0, 0.0)


def build_image(recv, spread, wide, starts, img):
    def spread_rows(i, carry):
        rows = pl.ds(pl.multiple_of(i * 128, 128), 128)
        wide_rows = pl.ds(pl.multiple_of(i * 128 + NB, NB), 128)
        wide[wide_rows, :] = dot(recv[rows, :], spread[...]).astype(BF)
        return carry

    lax.fori_loop(0, 4, spread_rows, 0)
    wide[0:NB, :] = wide[512 : 512 + NB, :]
    wide[NB + 512 :, :] = wide[NB : 2 * NB, :]
    store_starts(recv, starts)
    pick = jnp.where(iota((16, 128), 1) == 64, 1.0, 0.0).astype(BF)
    corner = dot_nt(pick, recv[...])[0:8]
    corner = jnp.concatenate([corner[:, 480:], corner, corner[:, :NB]], axis=1)
    local_x = local_x_of_row((XR, 128), 0)
    for q in range(8):
        mask = chunk_mask(starts, q).astype(BF)
        mask = jnp.concatenate([mask] * 4, axis=1)
        corner_q = corner[0:1, 64 * q : 64 * q + 128].astype(jnp.int32)
        offset = local_x - corner_q
        lhs = [jnp.where(offset == ex, 1.0, 0.0).astype(BF) for ex in range(4)]
        rhs = [wide[64 * q : 64 * q + 128, 512 * ex : 512 * ex + 512] * mask for ex in range(4)]
        cells = dot(jnp.concatenate(lhs, axis=1), jnp.concatenate(rhs, axis=0)).astype(BF)
        for kz in range(2):
            for c in range(2):
                p = 2 * c + kz
                img[kz, XR * c : XR * c + XR, 128 * q : 128 * q + 128] = cells[:, 128 * p : 128 * p + 128]


def forward_y(kz, img, cos, sin, out):
    def lanes_of(i, carry):
        lanes = pl.ds(pl.multiple_of(i * 256, 256), 256)
        by_cos = dot(img[kz], cos[:, lanes])
        by_sin = dot(img[kz], sin[:, lanes])
        real = (by_cos[:XR] + by_sin[XR:]).astype(BF)
        imag = (by_cos[XR:] - by_sin[:XR]).astype(BF)
        for j in range(2):
            out[kz, 2 * i + j, 0:XR, :] = real[:, 128 * j : 128 * j + 128]
            out[kz, 2 * i + j, XR:, :] = imag[:, 128 * j : 128 * j + 128]
        return carry

    lax.fori_loop(0, 4, lanes_of, 0)


def along_x(kz, recv, green, cos, sin, out, d_one, d_two, h_one, h_two):
    low_rows = iota((16, 128), 0) < 8

    def gather_band(r, carry):
        before, after = lax.rem(r + NROW - 1, NROW), lax.rem(r + 1, NROW)
        rows = pl.ds(pl.multiple_of(r * 128, 128), 128)
        for c in range(2):
            base = XR * c
            main = recv[kz, r, base : base + 128, :]
            lower = recv[kz, before, base + 128 : base + XR, :].astype(F32)
            upper = recv[kz, after, base + 128 : base + XR, :].astype(F32)
            head = main[0:16].astype(F32) + jnp.where(low_rows, lower, 0.0)
            tail = main[112:128].astype(F32) + jnp.where(low_rows, 0.0, upper)
            band = jnp.concatenate([head.astype(BF), main[16:112], tail.astype(BF)], axis=0)
            d_one[rows, 128 * c : 128 * c + 128] = band
            if c == 0:
                d_two[rows, 128:256] = -band
            else:
                d_two[rows, 0:128] = band
        return carry

    lax.fori_loop(0, NROW, gather_band, 0)

    def forward(i, carry):
        rows = pl.ds(pl.multiple_of(i * 256, 256), 256)
        spec = dot(cos[rows, :], d_one[...]) + dot(sin[rows, :], d_two[...])
        real, imag = spec[:, :128], spec[:, 128:]
        lanes = slice(128 * kz, 128 * kz + 128)
        g_real, g_imag = green[0, rows, lanes], green[1, rows, lanes]
        h_real = (real * g_real - imag * g_imag).astype(BF)
        h_imag = (real * g_imag + imag * g_real).astype(BF)
        h_one[rows, 0:128] = h_real
        h_one[rows, 128:256] = h_imag
        h_two[rows, 0:128] = -h_imag
        h_two[rows, 128:256] = h_real
        return carry

    lax.fori_loop(0, 4, forward, 0)

    def inverse(i, carry):
        rows = pl.ds(pl.multiple_of(i * 256, 256), 256)
        back = (dot(cos[rows, :], h_one[...]) + dot(sin[rows, :], h_two[...])).astype(BF)
        for j in range(2):
            for c in range(2):
                out[kz, 2 * i + j, XR * c : XR * c + 128, :] = back[
                    128 * j : 128 * j + 128, 128 * c : 128 * c + 128
                ]
        return carry

    lax.fori_loop(0, 4, inverse, 0)

    def rims(r, carry):
        before, after = lax.rem(r + NROW - 1, NROW), lax.rem(r + 1, NROW)
        for c in range(2):
            base = XR * c
            above = out[kz, after, base : base + 16, :].astype(F32)
            below = out[kz, before, base + 112 : base + 128, :].astype(F32)
            out[kz, r, base + 128 : base + XR, :] = jnp.where(low_rows, above, below).astype(BF)
        return carry

    lax.fori_loop(0, NROW, rims, 0)


def inverse_y(kz, recv, cos, sin, spec, pot):
    for r in range(NROW):
        spec[:, 128 * r : 128 * r + 128] = recv[kz, r]

    def lanes_of(i, carry):
        lanes = pl.ds(pl.multiple_of(i * 256, 256), 256)
        by_cos = dot(spec[...], cos[:, lanes])
        by_sin = dot(spec[...], sin[:, lanes])
        pot[0:XR, lanes] = (by_cos[:XR] - by_sin[XR:]).astype(BF)
        pot[XR:, lanes] = (by_cos[XR:] + by_sin[:XR]).astype(BF)
        return carry

    lax.fori_loop(0, 4, lanes_of, 0)


def build_hot(recv, hot):
    local_x = local_x_of_row((512, XR), 1)
    offset = local_x - recv[:, 64:65].astype(jnp.int32)
    for ex in range(4):
        hot[ex, NB : NB + 512, :] = jnp.where(offset == ex, 1.0, 0.0).astype(BF)
    hot[:, 0:NB, :] = hot[:, 512 : 512 + NB, :]
    hot[:, NB + 512 :, :] = hot[:, NB : 2 * NB, :]


def pick_cells(kz, pot, starts, hot, acc):
    for q in range(8):
        mask = chunk_mask(starts, q)
        mask = jnp.concatenate([mask] * 2, axis=1)
        cells = [pot[XR * c : XR * c + XR, 128 * q : 128 * q + 128] for c in range(2)]
        cells = jnp.concatenate(cells, axis=1)
        rows = slice(64 * q, 64 * q + 128)
        for ex in range(4):
            taken = (dot(hot[ex, rows, :], cells) * mask).astype(BF)
            for c in range(2):
                lane = 512 * ex + 256 * c + 128 * kz
                lanes = slice(lane, lane + 128)
                acc[rows, lanes] = acc[rows, lanes] + taken[:, 128 * c : 128 * c + 128]


def back_project(recv, near, tch, tcl, tsh, tsl, out, p_high, p_low, hots, box_real, box_imag, vals):
    real = jnp.concatenate([recv[NB * c : NB * c + NB, 0:32] for c in range(NCOL)], axis=1)
    imag = jnp.concatenate([recv[NB * c : NB * c + NB, 32:64] for c in range(NCOL)], axis=1)
    both = jnp.concatenate([real, imag], axis=0)
    along_cos = dot(both, tch[...]) + dot(both, tcl[...])
    along_sin = dot(both, tsh[...]) + dot(both, tsl[...])
    box_real[...] = along_cos[:NB] - along_sin[NB:]
    box_imag[...] = along_cos[NB:] + along_sin[:NB]

    def values_of(i, carry):
        for u in range(8):
            g = i * 8 + u
            box = jnp.concatenate([box_real[pl.ds(g, 1), :], box_imag[pl.ds(g, 1), :]], axis=0)
            picked = dot(rows_high_low(box), hots[g])
            vals[g] = picked[0:2] + picked[2:4]
        return carry

    lax.fori_loop(0, NB // 8, values_of, 0)

    def blocks_of(i, carry):
        for u in range(8):
            g = i * 8 + u
            lhs = rows_high_low(vals[g])
            first = dot(lhs, p_high[g])
            far = first[0:2] + first[2:4] + dot(lhs, p_low[g])[0:2]
            row = near[pl.ds(g, 1), :]
            beside = jnp.concatenate([row[:, :BLK], row[:, BLK:]], axis=0)
            out[:, pl.ds(pl.multiple_of(g * BLK, BLK), BLK)] = far + beside
        return carry

    lax.fori_loop(0, NB // 8, blocks_of, 0)


def column_of(row):
    return jnp.transpose(jnp.broadcast_to(row.astype(F32), (8, 128)))[:, 0:1].astype(jnp.int32)


def near_backward(beside, owned, picks, count, matrices, back_a, lv_one, lv_two, spread_back):
    hits = jnp.where(iota((PAIRS, NB), 1) == column_of(owned[...]), 1.0, 0.0).astype(BF)
    local = dot(hits, beside[4])
    real, imag = local[:, :BLK], local[:, BLK:]
    lv_one[...] = jnp.concatenate([real, -imag], axis=1)
    lv_two[...] = jnp.concatenate([imag, real], axis=1)
    first_row = iota((8, 2 * BLK), 0) == 0

    def pairs_of(i, carry):
        for u in range(8):
            p = i * 8 + u
            lhs = jnp.where(first_row, lv_one[pl.ds(p, 1), :], lv_two[pl.ds(p, 1), :]).astype(BF)
            got = dot(lhs, matrices[p])
            back_a[pl.ds(p, 1), :] = jnp.concatenate([got[0:1], got[1:2]], axis=1)
        return carry

    lax.fori_loop(0, PAIRS // 8, pairs_of, 0)
    alive = iota((9 * NB, PAIRS), 1) < count[0]
    hits = (iota((9 * NB, PAIRS), 0) == picks[...]) & alive
    table = jnp.where(hits, 1.0, 0.0).astype(BF)
    high, low = high_low(back_a[...])
    total = (dot(table, high) + dot(table, low)).astype(BF)
    for n in range(9):
        spread_back[n] = total[NB * n : NB * n + NB, :]


def near_onward(beside, owned, picks, count, matrices, on_a, on_b, lv_one, near):
    hits = jnp.where(iota((PAIRS, 9 * NB), 1) == column_of(picks[...]), 1.0, 0.0).astype(BF)
    lv_one[...] = dot(hits, jnp.concatenate([beside[n] for n in range(9)], axis=0))
    first_row = iota((8, BLK), 0) == 0

    def pairs_of(i, carry):
        for u in range(8):
            p = i * 8 + u
            row = lv_one[pl.ds(p, 1), :]
            lhs = jnp.where(first_row, row[:, :BLK], row[:, BLK:]).astype(BF)
            got = dot_nt(lhs, matrices[p])
            on_a[pl.ds(p, 1), :] = got[0:1]
            on_b[pl.ds(p, 1), :] = got[1:2]
        return carry

    lax.fori_loop(0, PAIRS // 8, pairs_of, 0)
    real = on_a[:, :BLK] - on_b[:, BLK:]
    imag = on_b[:, :BLK] + on_a[:, BLK:]
    alive = iota((NB, PAIRS), 1) < count[0]
    table = jnp.where((iota((NB, PAIRS), 0) == owned[...]) & alive, 1.0, 0.0).astype(BF)
    high, low = high_low(jnp.concatenate([real, imag], axis=1))
    near[...] = dot(table, high) + dot(table, low)


def turn_green(green, turned):
    for c in range(2):
        for kz in range(2):

            def part(i, carry):
                rows = pl.ds(pl.multiple_of(i * 128, 128), 128)
                block = jnp.transpose(green[c, kz, :, rows])
                turned[c, rows, 128 * kz : 128 * kz + 128] = block * (1.0 / (N * N * NGZ))
                return carry

            lax.fori_loop(0, 8, part, 0)


def whole_kernel(
    cur, cells, owned, picks, count, near_hbm, proj_hbm, green_hbm,
    tch_hbm, tcl_hbm, tsh_hbm, tsl_hbm, spread_hbm, cos_hbm, sin_hbm, out,
    matrices, proj, green, tch, tcl, tsh, tsl, spread, cos, sin, load_sem,
    codes, p_high, p_low, hots, vals, boxed, box_real, box_imag,
    beside, spread_back, back, on_a, on_b, lv_one, lv_two, near, turned,
    wide, starts, img, hot, acc, spec, pot, d_one, d_two, h_one, h_two,
    send_a, recv_a, send_b, recv_b, sem_send_a, sem_recv_a, sem_send_b, sem_recv_b,
    send_c, recv_c, send_d, recv_d, sem_send_c, sem_recv_c, sem_send_d, sem_recv_d,
    sem_send_h, sem_recv_h, sem_send_r, sem_recv_r,
):
    row, col = lax.axis_index("row"), lax.axis_index("col")
    mesh_ids = pl.DeviceIdType.MESH

    def row_peer(j):
        return (lax.rem(row + j, NROW), col)

    def col_peer(j):
        return (row, lax.rem(col + j, NCOL))

    def tile_peer(n):
        return (lax.rem(row + n // 3 - 1 + NROW, NROW), lax.rem(col + n % 3 - 1 + NCOL, NCOL))

    barrier = pltpu.get_barrier_semaphore()
    peers = [row_peer(j) for j in range(1, NROW)] + [col_peer(j) for j in range(1, NCOL)]
    peers += [tile_peer(n) for n in (0, 2, 6, 8)]
    for peer in peers:
        pl.semaphore_signal(barrier, inc=1, device_id=peer, device_id_type=mesh_ids)

    pairs = [
        (proj_hbm, proj), (tch_hbm, tch), (tcl_hbm, tcl), (tsh_hbm, tsh), (tsl_hbm, tsl),
        (near_hbm, matrices), (spread_hbm, spread), (cos_hbm, cos), (sin_hbm, sin),
        (green_hbm, green),
    ]
    loads = [pltpu.make_async_copy(a, b, load_sem.at[i]) for i, (a, b) in enumerate(pairs)]
    for load in loads:
        load.start()

    def remote(source, target, sem_send, sem_recv, peer):
        return pltpu.make_async_remote_copy(
            src_ref=source,
            dst_ref=target,
            send_sem=sem_send,
            recv_sem=sem_recv,
            device_id=peer,
            device_id_type=mesh_ids,
        )

    def row_copies(kz, source, target, sem_send, sem_recv):
        return [
            remote(
                source.at[kz, row_peer(j)[0]],
                target.at[kz, row],
                sem_send.at[kz, j],
                sem_recv.at[kz, j],
                row_peer(j),
            )
            for j in range(1, NROW)
        ]

    def tile_rows(c):
        return pl.ds(pl.multiple_of(c * NB, NB), NB)

    def col_copies(source, target, sem_send, sem_recv):
        return [
            remote(
                source.at[tile_rows(col_peer(j)[1])],
                target.at[tile_rows(col)],
                sem_send.at[j],
                sem_recv.at[j],
                col_peer(j),
            )
            for j in range(1, NCOL)
        ]

    for g in range(NB):
        two = cur[:, BLK * g : BLK * g + BLK]
        vals[g] = two
    rounded = jnp.concatenate([vals[:, 0, :], vals[:, 1, :]], axis=1).astype(BF)
    beside[4] = rounded
    for load in loads[:5]:
        load.wait()
    project(cur, proj, cells, tch, tcl, tsh, tsl, send_c, codes, p_high, p_low, hots, vals, boxed)
    pl.semaphore_wait(barrier, len(peers))
    third = col_copies(send_c, recv_c, sem_send_c, sem_recv_c)
    for copy in third:
        copy.start()
    halo = [
        remote(beside.at[4], beside.at[8 - n], sem_send_h.at[n], sem_recv_h.at[n], tile_peer(n))
        for n in range(9)
        if n != 4
    ]
    for copy in halo:
        copy.start()
    recv_c[tile_rows(col), :] = send_c[tile_rows(col), :]
    loads[5].wait()
    near_backward(beside, owned, picks, count, matrices, on_a, lv_one, lv_two, spread_back)
    back[4] = spread_back[4]
    returns = [
        remote(spread_back.at[n], back.at[8 - n], sem_send_r.at[n], sem_recv_r.at[n], tile_peer(n))
        for n in range(9)
        if n != 4
    ]
    for copy in returns:
        copy.start()
    for load in loads[6:]:
        load.wait()
    for copy in third:
        copy.wait_recv()
    build_image(recv_c, spread, wide, starts, img)
    first, second = [], []
    for kz in range(2):
        forward_y(kz, img, cos, sin, send_a)
        first.append(row_copies(kz, send_a, recv_a, sem_send_a, sem_recv_a))
        for copy in first[kz]:
            copy.start()
        recv_a[kz, row] = send_a[kz, row]
    turn_green(green, turned)
    for copy in halo:
        copy.wait_recv()
    near_onward(beside, owned, picks, count, matrices, on_a, on_b, lv_one, near)
    for kz in range(2):
        for copy in first[kz]:
            copy.wait_recv()
        along_x(kz, recv_a, turned, cos, sin, send_b, d_one, d_two, h_one, h_two)
        second.append(row_copies(kz, send_b, recv_b, sem_send_b, sem_recv_b))
        for copy in second[kz]:
            copy.start()
        recv_b[kz, row] = send_b[kz, row]
    build_hot(recv_c, hot)
    acc[...] = jnp.zeros_like(acc)
    for copy in returns:
        copy.wait_recv()
    total = near[...]
    for n in range(9):
        total = total + back[n].astype(F32)
    near[...] = total
    for kz in range(2):
        for copy in second[kz]:
            copy.wait_recv()
        inverse_y(kz, recv_b, cos, sin, spec, pot)
        pick_cells(kz, pot, starts, hot, acc)
    acc[512 : 512 + NB, :] = acc[512 : 512 + NB, :] + acc[0:NB, :]
    acc[NB : 2 * NB, :] = acc[NB : 2 * NB, :] + acc[NB + 512 :, :]

    def fold(i, carry):
        rows = pl.ds(pl.multiple_of(i * 128, 128), 128)
        wide_rows = pl.ds(pl.multiple_of(i * 128 + NB, NB), 128)
        send_d[rows, :] = dot_nt(acc[wide_rows, :], spread[...]).astype(BF)
        return carry

    lax.fori_loop(0, 4, fold, 0)
    fourth = col_copies(send_d, recv_d, sem_send_d, sem_recv_d)
    for copy in fourth:
        copy.start()
    recv_d[tile_rows(col), :] = send_d[tile_rows(col), :]
    for copy in fourth:
        copy.wait_recv()
    back_project(
        recv_d, near, tch, tcl, tsh, tsl, out, p_high, p_low, hots, box_real, box_imag, vals
    )
    for copy in first[0] + first[1] + second[0] + second[1] + third + fourth + halo + returns:
        copy.wait_send()


def per_device(
    currents, near_blocks, pair_local, pair_ghost, pair_counts, projection, stencil_cells, green
):
    tables = [jnp.asarray(t) for t in depth_tables()]
    tables.append(jnp.asarray(spread_table()))
    tables += [jnp.asarray(t) for t in grid_tables()]
    vmem, dma = pltpu.VMEM, pltpu.SemaphoreType.DMA
    grid_part = (2, NROW, 2 * XR, 128)
    wrapped = 512 + 2 * NB
    scratch = [
        vmem((PAIRS, 2 * BLK, BLK), BF),
        vmem((NB, BLK, BLK), F32),
        vmem((2, 2, 128, N), F32),
        *[vmem((512, 512), BF)] * 4,
        vmem((128, 2048), BF),
        *[vmem((N, N), BF)] * 2,
        dma((10,)),
        vmem((NB, BLK), jnp.int32),
        *[vmem((NB, BLK, BLK), BF)] * 2,
        vmem((NB, 512, BLK), BF),
        vmem((NB, 2, BLK), F32),
        vmem((2 * NB, 512), F32),
        *[vmem((NB, 512), F32)] * 2,
        *[vmem((9, NB, 2 * BLK), BF)] * 3,
        *[vmem((PAIRS, 2 * BLK), F32)] * 4,
        vmem((NB, 2 * BLK), F32),
        vmem((2, N, 256), F32),
        vmem((wrapped, 2048), BF),
        vmem((wrapped, 128), jnp.int32),
        vmem((2, 2 * XR, N), BF),
        vmem((4, wrapped, XR), BF),
        vmem((wrapped, 2048), BF),
        *[vmem((2 * XR, N), BF)] * 2,
        *[vmem((N, 256), BF)] * 4,
        *[vmem(grid_part, BF)] * 4,
        *[dma((2, NROW))] * 4,
        *[vmem((NCOL * NB, 128), BF)] * 4,
        *[dma((NCOL,))] * 4,
        *[dma((9,))] * 4,
    ]
    in_vmem = pl.BlockSpec(memory_space=pltpu.VMEM)
    in_smem = pl.BlockSpec(memory_space=pltpu.SMEM)
    anywhere = pl.BlockSpec(memory_space=pl.ANY)
    return pl.pallas_call(
        whole_kernel,
        out_shape=jax.ShapeDtypeStruct((2, NB * BLK), F32),
        in_specs=[in_vmem] * 4 + [in_smem] + [anywhere] * 10,
        out_specs=in_vmem,
        scratch_shapes=scratch,
        compiler_params=pltpu.CompilerParams(
            vmem_limit_bytes=VMEM_LIMIT, collective_id=1, has_side_effects=True
        ),
    )(
        currents,
        stencil_cells,
        pair_local,
        pair_ghost,
        pair_counts,
        near_blocks.reshape(PAIRS, 2 * BLK, BLK),
        projection,
        green,
        *tables,
    )


def solution(mesh):
    in_specs = (
        P(None, ("row", "col")),
        P(("row", "col"), None, None, None),
        P(("row", "col"), None),
        P(("row", "col"), None),
        P(("row", "col")),
        P(("row", "col"), None, None),
        P(("row", "col"), None),
        P(None, "col", "row", None),
    )
    out_specs = P(None, ("row", "col"))
    return jax.shard_map(
        per_device, mesh=mesh, in_specs=in_specs, out_specs=out_specs, check_vma=False
    )
```

```python
import math

import jax
import jax.numpy as jnp
import ml_dtypes
import numpy as np
from jax import lax
from jax.experimental import pallas as pl
from jax.experimental.pallas import tpu as pltpu
from jax.sharding import PartitionSpec as P

N = 1024
NGZ = 32
NROW = 8
NCOL = 16
NB = 32
BLK = 128
PAIRS = 128
XR = 144
WIDE_Y = 68
BF = jnp.bfloat16
F32 = jnp.float32
VMEM_LIMIT = 60 * 1024 * 1024


def bf(a):
    return np.asarray(a, dtype=np.float64).astype(ml_dtypes.bfloat16)


def split_np(a):
    high = bf(a)
    return high, bf(a - high.astype(np.float64))


def grid_tables():
    index = np.arange(N)[:, None] * np.arange(N)[None, :] % N
    angle = index * (2.0 * math.pi / N)
    return bf(np.cos(angle)), bf(np.sin(angle))


def depth_tables():
    index = np.arange(NGZ)[:, None] * np.arange(NGZ)[None, :] % NGZ
    angle = index * (2.0 * math.pi / NGZ)
    eye = np.eye(16)
    cos_high, cos_low = split_np(np.kron(np.cos(angle), eye))
    sin_high, sin_low = split_np(np.kron(np.sin(angle), eye))
    return cos_high, cos_low, sin_high, sin_low


def spread_table():
    lane = np.arange(128)[:, None]
    plane, ex, b = lane // 16, lane // 4 % 4, lane % 4
    wide = np.arange(2048)[None, :]
    hits = (wide // 512 == ex) & (wide // 128 % 4 == plane) & ((wide + 2) % 4 == b) & (lane < 64)
    return bf(hits.astype(np.float64))


def dot(a, b):
    return jnp.dot(a, b, preferred_element_type=F32)


def dot_nt(a, b):
    return lax.dot_general(a, b, (((1,), (1,)), ((), ())), preferred_element_type=F32)


def iota(shape, dim):
    return lax.broadcasted_iota(jnp.int32, shape, dim)


def high_low(a):
    high = a.astype(BF)
    return high, (a - high.astype(F32)).astype(BF)


def rows_high_low(a):
    high = a.astype(BF).astype(F32)
    return jnp.concatenate([high, a - high], axis=0).astype(BF)


def cell_codes(cells):
    z = cells & (NGZ - 1)
    t = cells >> 5
    x = (t * 15421) >> 20
    y = t - x * WIDE_Y
    corner_x = jnp.min(x, axis=1, keepdims=True)
    corner_y = jnp.min(y, axis=1, keepdims=True)
    code = z * 16 + (x - corner_x) * 4 + (y & 3)
    return code, corner_x, corner_y


def one_hot_rows(code_row):
    return jnp.where(iota((512, 128), 0) == code_row, 1.0, 0.0).astype(BF)


def project(cur, proj, cells, tch, tcl, tsh, tsl, out, codes, p_high, p_low, hots, vals, boxed):
    code, corner_x, corner_y = cell_codes(cells[...])
    codes[...] = code

    def values_of(i, carry):
        for u in range(8):
            g = i * 8 + u
            lhs = rows_high_low(cur[:, pl.ds(pl.multiple_of(g * BLK, BLK), BLK)])
            high, low = high_low(proj[g])
            p_high[g] = high
            p_low[g] = low
            first = dot_nt(lhs, high)
            vals[g] = first[0:2] + first[2:4] + dot_nt(lhs, low)[0:2]
        return carry

    lax.fori_loop(0, NB // 8, values_of, 0)

    def boxes_of(i, carry):
        for u in range(8):
            g = i * 8 + u
            hot = one_hot_rows(codes[pl.ds(g, 1), :])
            hots[g] = hot
            placed = dot_nt(rows_high_low(vals[g]), hot)
            boxed[pl.ds(g, 1), :] = placed[0:1] + placed[2:3]
            boxed[pl.ds(NB + g, 1), :] = placed[1:2] + placed[3:4]
        return carry

    lax.fori_loop(0, NB // 8, boxes_of, 0)
    b_high, b_low = high_low(boxed[...])
    along_cos = dot(b_high, tch[...]) + dot(b_low, tch[...]) + dot(b_high, tcl[...])
    along_sin = dot(b_high, tsh[...]) + dot(b_low, tsh[...]) + dot(b_high, tsl[...])
    real = along_cos[:NB] + along_sin[NB:]
    imag = along_cos[NB:] - along_sin[:NB]
    lane = iota((NB, 64), 1)
    corners = jnp.where(lane == 0, corner_x, jnp.where(lane == 1, corner_y, 0)).astype(F32)
    for c in range(NCOL):
        part = slice(32 * c, 32 * c + 32)
        message = jnp.concatenate([real[:, part], imag[:, part], corners], axis=1)
        out[NB * c : NB * c + NB, :] = message.astype(BF)


def local_x_of_row(shape, dim):
    row = iota(shape, dim)
    return jnp.where(row < 130, row + 2, jnp.where(row >= 142, row - 142, -64))


def store_starts(recv, starts):
    block = iota((512, 1), 0)
    start = recv[:, 65:66].astype(jnp.int32) + (block // NB) * 64 - 2
    starts[NB : NB + 512, :] = jnp.broadcast_to(start, (512, 128))
    starts[0:NB, :] = starts[512 : 512 + NB, :]
    starts[NB + 512 :, :] = starts[NB : 2 * NB, :]


def chunk_mask(starts, q):
    cell = 128 * q + iota((128, 128), 1)
    inside = ((cell - starts[64 * q : 64 * q + 128, :]) & (N - 1)) < 4
    return jnp.where(inside, 1.0, 0.0)


def build_image(recv, spread, wide, starts, img):
    def spread_rows(i, carry):
        rows = pl.ds(pl.multiple_of(i * 128, 128), 128)
        wide_rows = pl.ds(pl.multiple_of(i * 128 + NB, NB), 128)
        wide[wide_rows, :] = dot(recv[rows, :], spread[...]).astype(BF)
        return carry

    lax.fori_loop(0, 4, spread_rows, 0)
    wide[0:NB, :] = wide[512 : 512 + NB, :]
    wide[NB + 512 :, :] = wide[NB : 2 * NB, :]
    store_starts(recv, starts)
    pick = jnp.where(iota((16, 128), 1) == 64, 1.0, 0.0).astype(BF)
    corner = dot_nt(pick, recv[...])[0:8]
    corner = jnp.concatenate([corner[:, 480:], corner, corner[:, :NB]], axis=1)
    local_x = local_x_of_row((XR, 128), 0)
    for q in range(8):
        mask = chunk_mask(starts, q).astype(BF)
        mask = jnp.concatenate([mask] * 4, axis=1)
        corner_q = corner[0:1, 64 * q : 64 * q + 128].astype(jnp.int32)
        offset = local_x - corner_q
        lhs = [jnp.where(offset == ex, 1.0, 0.0).astype(BF) for ex in range(4)]
        rhs = [wide[64 * q : 64 * q + 128, 512 * ex : 512 * ex + 512] * mask for ex in range(4)]
        cells = dot(jnp.concatenate(lhs, axis=1), jnp.concatenate(rhs, axis=0)).astype(BF)
        for kz in range(2):
            for c in range(2):
                p = 2 * c + kz
                img[kz, XR * c : XR * c + XR, 128 * q : 128 * q + 128] = cells[:, 128 * p : 128 * p + 128]


def forward_y(kz, chip, img, cos, sin, out, slot):
    lanes = pl.ds(pl.multiple_of(chip * 256, 256), 256)
    by_cos = dot(img[kz], cos[:, lanes])
    by_sin = dot(img[kz], sin[:, lanes])
    real = (by_cos[:XR] + by_sin[XR:]).astype(BF)
    imag = (by_cos[XR:] - by_sin[:XR]).astype(BF)
    for j in range(2):
        out[kz, slot + j, 0:XR, :] = real[:, 128 * j : 128 * j + 128]
        out[kz, slot + j, XR:, :] = imag[:, 128 * j : 128 * j + 128]


def along_x(kz, recv, green, cos, sin, out, d_one, d_two, h_one, h_two):
    low_rows = iota((16, 128), 0) < 8

    def gather_band(r, carry):
        before, after = lax.rem(r + NROW - 1, NROW), lax.rem(r + 1, NROW)
        rows = pl.ds(pl.multiple_of(r * 128, 128), 128)
        for c in range(2):
            base = XR * c
            main = recv[kz, r, base : base + 128, :]
            lower = recv[kz, before, base + 128 : base + XR, :].astype(F32)
            upper = recv[kz, after, base + 128 : base + XR, :].astype(F32)
            head = main[0:16].astype(F32) + jnp.where(low_rows, lower, 0.0)
            tail = main[112:128].astype(F32) + jnp.where(low_rows, 0.0, upper)
            band = jnp.concatenate([head.astype(BF), main[16:112], tail.astype(BF)], axis=0)
            d_one[rows, 128 * c : 128 * c + 128] = band
            if c == 0:
                d_two[rows, 128:256] = -band
            else:
                d_two[rows, 0:128] = band
        return carry

    lax.fori_loop(0, NROW, gather_band, 0)

    def forward(i, carry):
        rows = pl.ds(pl.multiple_of(i * 256, 256), 256)
        spec = dot(cos[rows, :], d_one[...]) + dot(sin[rows, :], d_two[...])
        real, imag = spec[:, :128], spec[:, 128:]
        lanes = slice(128 * kz, 128 * kz + 128)
        g_real, g_imag = green[0, rows, lanes], green[1, rows, lanes]
        h_real = (real * g_real - imag * g_imag).astype(BF)
        h_imag = (real * g_imag + imag * g_real).astype(BF)
        h_one[rows, 0:128] = h_real
        h_one[rows, 128:256] = h_imag
        h_two[rows, 0:128] = -h_imag
        h_two[rows, 128:256] = h_real
        return carry

    lax.fori_loop(0, 4, forward, 0)

    def inverse(i, carry):
        rows = pl.ds(pl.multiple_of(i * 256, 256), 256)
        back = (dot(cos[rows, :], h_one[...]) + dot(sin[rows, :], h_two[...])).astype(BF)
        for j in range(2):
            for c in range(2):
                out[kz, 2 * i + j, XR * c : XR * c + 128, :] = back[
                    128 * j : 128 * j + 128, 128 * c : 128 * c + 128
                ]
        return carry

    lax.fori_loop(0, 4, inverse, 0)

    def rims(r, carry):
        before, after = lax.rem(r + NROW - 1, NROW), lax.rem(r + 1, NROW)
        for c in range(2):
            base = XR * c
            above = out[kz, after, base : base + 16, :].astype(F32)
            below = out[kz, before, base + 112 : base + 128, :].astype(F32)
            out[kz, r, base + 128 : base + XR, :] = jnp.where(low_rows, above, below).astype(BF)
        return carry

    lax.fori_loop(0, NROW, rims, 0)


def inverse_y(kz, recv, slots, chips, cos, sin, spec, pot):
    for m, slot in enumerate(slots):
        for j in range(2):
            spec[:, 256 * m + 128 * j : 256 * m + 128 * j + 128] = recv[kz, slot + j]

    def lanes_of(i, carry):
        lanes = pl.ds(pl.multiple_of(i * 256, 256), 256)
        by_cos, by_sin = 0.0, 0.0
        for m, chip in enumerate(chips):
            rows = pl.ds(pl.multiple_of(chip * 256, 256), 256)
            part = spec[:, 256 * m : 256 * m + 256]
            by_cos = by_cos + dot(part, cos[rows, lanes])
            by_sin = by_sin + dot(part, sin[rows, lanes])
        pot[0:XR, lanes] = (by_cos[:XR] - by_sin[XR:]).astype(BF)
        pot[XR:, lanes] = (by_cos[XR:] + by_sin[:XR]).astype(BF)
        return carry

    lax.fori_loop(0, 4, lanes_of, 0)


def build_hot(recv, hot):
    local_x = local_x_of_row((512, XR), 1)
    offset = local_x - recv[:, 64:65].astype(jnp.int32)
    for ex in range(4):
        hot[ex, NB : NB + 512, :] = jnp.where(offset == ex, 1.0, 0.0).astype(BF)
    hot[:, 0:NB, :] = hot[:, 512 : 512 + NB, :]
    hot[:, NB + 512 :, :] = hot[:, NB : 2 * NB, :]


def pick_cells(kz, pot, starts, hot, acc):
    for q in range(8):
        mask = chunk_mask(starts, q)
        mask = jnp.concatenate([mask] * 2, axis=1)
        cells = [pot[XR * c : XR * c + XR, 128 * q : 128 * q + 128] for c in range(2)]
        cells = jnp.concatenate(cells, axis=1)
        rows = slice(64 * q, 64 * q + 128)
        for ex in range(4):
            taken = (dot(hot[ex, rows, :], cells) * mask).astype(BF)
            for c in range(2):
                lane = 512 * ex + 256 * c + 128 * kz
                lanes = slice(lane, lane + 128)
                acc[rows, lanes] = acc[rows, lanes] + taken[:, 128 * c : 128 * c + 128]


def fold_cells(acc, spread, out, extra):
    acc[512 : 512 + NB, :] = acc[512 : 512 + NB, :] + acc[0:NB, :]
    acc[NB : 2 * NB, :] = acc[NB : 2 * NB, :] + acc[NB + 512 :, :]

    def fold(i, carry):
        rows = pl.ds(pl.multiple_of(i * 128, 128), 128)
        wide_rows = pl.ds(pl.multiple_of(i * 128 + NB, NB), 128)
        cells = dot_nt(acc[wide_rows, :], spread[...])
        if extra is not None:
            cells = cells + extra[rows, :].astype(F32)
        out[rows, :] = cells.astype(BF)
        return carry

    lax.fori_loop(0, 4, fold, 0)


def back_project(recv, near, tch, tcl, tsh, tsl, out, p_high, p_low, hots, box_real, box_imag, vals):
    real = jnp.concatenate([recv[NB * c : NB * c + NB, 0:32] for c in range(NCOL)], axis=1)
    imag = jnp.concatenate([recv[NB * c : NB * c + NB, 32:64] for c in range(NCOL)], axis=1)
    both = jnp.concatenate([real, imag], axis=0)
    along_cos = dot(both, tch[...]) + dot(both, tcl[...])
    along_sin = dot(both, tsh[...]) + dot(both, tsl[...])
    box_real[...] = along_cos[:NB] - along_sin[NB:]
    box_imag[...] = along_cos[NB:] + along_sin[:NB]

    def values_of(i, carry):
        for u in range(8):
            g = i * 8 + u
            box = jnp.concatenate([box_real[pl.ds(g, 1), :], box_imag[pl.ds(g, 1), :]], axis=0)
            picked = dot(rows_high_low(box), hots[g])
            vals[g] = picked[0:2] + picked[2:4]
        return carry

    lax.fori_loop(0, NB // 8, values_of, 0)

    def blocks_of(i, carry):
        for u in range(8):
            g = i * 8 + u
            lhs = rows_high_low(vals[g])
            first = dot(lhs, p_high[g])
            far = first[0:2] + first[2:4] + dot(lhs, p_low[g])[0:2]
            row = near[pl.ds(g, 1), :]
            beside = jnp.concatenate([row[:, :BLK], row[:, BLK:]], axis=0)
            out[:, pl.ds(pl.multiple_of(g * BLK, BLK), BLK)] = far + beside
        return carry

    lax.fori_loop(0, NB // 8, blocks_of, 0)


def column_of(row):
    return jnp.transpose(jnp.broadcast_to(row.astype(F32), (8, 128)))[:, 0:1].astype(jnp.int32)


def near_backward(beside, owned, picks, count, matrices, back_a, lv_one, lv_two, spread_back):
    hits = jnp.where(iota((PAIRS, NB), 1) == column_of(owned[...]), 1.0, 0.0).astype(BF)
    local = dot(hits, beside[4])
    real, imag = local[:, :BLK], local[:, BLK:]
    lv_one[...] = jnp.concatenate([real, -imag], axis=1)
    lv_two[...] = jnp.concatenate([imag, real], axis=1)
    first_row = iota((8, 2 * BLK), 0) == 0

    def pairs_of(i, carry):
        for u in range(8):
            p = i * 8 + u
            lhs = jnp.where(first_row, lv_one[pl.ds(p, 1), :], lv_two[pl.ds(p, 1), :]).astype(BF)
            got = dot(lhs, matrices[p])
            back_a[pl.ds(p, 1), :] = jnp.concatenate([got[0:1], got[1:2]], axis=1)
        return carry

    lax.fori_loop(0, PAIRS // 8, pairs_of, 0)
    alive = iota((9 * NB, PAIRS), 1) < count[0]
    hits = (iota((9 * NB, PAIRS), 0) == picks[...]) & alive
    table = jnp.where(hits, 1.0, 0.0).astype(BF)
    high, low = high_low(back_a[...])
    total = (dot(table, high) + dot(table, low)).astype(BF)
    for n in range(9):
        spread_back[n] = total[NB * n : NB * n + NB, :]


def near_onward(beside, owned, picks, count, matrices, on_a, on_b, lv_one, near):
    hits = jnp.where(iota((PAIRS, 9 * NB), 1) == column_of(picks[...]), 1.0, 0.0).astype(BF)
    lv_one[...] = dot(hits, jnp.concatenate([beside[n] for n in range(9)], axis=0))
    first_row = iota((8, BLK), 0) == 0

    def pairs_of(i, carry):
        for u in range(8):
            p = i * 8 + u
            row = lv_one[pl.ds(p, 1), :]
            lhs = jnp.where(first_row, row[:, :BLK], row[:, BLK:]).astype(BF)
            got = dot_nt(lhs, matrices[p])
            on_a[pl.ds(p, 1), :] = got[0:1]
            on_b[pl.ds(p, 1), :] = got[1:2]
        return carry

    lax.fori_loop(0, PAIRS // 8, pairs_of, 0)
    real = on_a[:, :BLK] - on_b[:, BLK:]
    imag = on_b[:, :BLK] + on_a[:, BLK:]
    alive = iota((NB, PAIRS), 1) < count[0]
    table = jnp.where((iota((NB, PAIRS), 0) == owned[...]) & alive, 1.0, 0.0).astype(BF)
    high, low = high_low(jnp.concatenate([real, imag], axis=1))
    near[...] = dot(table, high) + dot(table, low)


def turn_green(green, turned):
    for c in range(2):
        for kz in range(2):

            def part(i, carry):
                rows = pl.ds(pl.multiple_of(i * 128, 128), 128)
                block = jnp.transpose(green[c, kz, :, rows])
                turned[c, rows, 128 * kz : 128 * kz + 128] = block * (1.0 / (N * N * NGZ))
                return carry

            lax.fori_loop(0, 8, part, 0)


def whole_kernel(
    cur, cells, owned, picks, count, near_hbm, proj_hbm, green_hbm,
    tch_hbm, tcl_hbm, tsh_hbm, tsl_hbm, spread_hbm, cos_hbm, sin_hbm, out,
    matrices, proj, green, tch, tcl, tsh, tsl, spread, cos, sin, load_sem,
    codes, p_high, p_low, hots, vals, boxed, box_real, box_imag,
    beside, spread_back, back, on_a, on_b, lv_one, lv_two, near, turned,
    wide, starts, img, hot, acc, spec, pot, d_one, d_two, h_one, h_two,
    send_a, recv_a, send_b, recv_b, sem_send_a, sem_recv_a, sem_send_b, sem_recv_b,
    send_c, recv_c, send_d, recv_d, sem_send_c, sem_recv_c, sem_send_d, sem_recv_d,
    sem_send_h, sem_recv_h, sem_send_r, sem_recv_r,
    far_c, far_starts, far_hot, far_a, recv_f, send_q, recv_q, sem_far,
):
    row, col = lax.axis_index("row"), lax.axis_index("col")
    mesh_ids = pl.DeviceIdType.MESH

    def row_peer(j):
        return (lax.rem(row + j, NROW), col)

    def col_peer(j):
        return (row, lax.rem(col + j, NCOL))

    def tile_peer(n):
        return (lax.rem(row + n // 3 - 1 + NROW, NROW), lax.rem(col + n % 3 - 1 + NCOL, NCOL))

    barrier = pltpu.get_barrier_semaphore()
    peers = [row_peer(j) for j in range(1, NROW)] + [col_peer(j) for j in range(1, NCOL)]
    peers += [tile_peer(n) for n in (0, 2, 6, 8)]
    for peer in peers:
        pl.semaphore_signal(barrier, inc=1, device_id=peer, device_id_type=mesh_ids)

    pairs = [
        (proj_hbm, proj), (tch_hbm, tch), (tcl_hbm, tcl), (tsh_hbm, tsh), (tsl_hbm, tsl),
        (green_hbm, green), (near_hbm, matrices), (spread_hbm, spread), (cos_hbm, cos),
        (sin_hbm, sin),
    ]
    loads = [pltpu.make_async_copy(a, b, load_sem.at[i]) for i, (a, b) in enumerate(pairs)]
    for load in loads:
        load.start()

    def remote(source, target, sem_send, sem_recv, peer):
        return pltpu.make_async_remote_copy(
            src_ref=source,
            dst_ref=target,
            send_sem=sem_send,
            recv_sem=sem_recv,
            device_id=peer,
            device_id_type=mesh_ids,
        )

    z, core = row // 2, lax.rem(row, 2)
    sibling = 2 * z + 1 - core
    far, far_sibling = lax.rem(row + 4, NROW), lax.rem(sibling + 4, NROW)
    chips = [lax.rem(z + 1, 4), lax.rem(z + 3, 4)]

    def row_copy(kz, source, target, sems, j, peer):
        return remote(source, target, sems[0].at[kz, j], sems[1].at[kz, j], (peer, col))

    def tile_rows(c):
        return pl.ds(pl.multiple_of(c * NB, NB), NB)

    def col_copies(source, target, sem_send, sem_recv):
        return [
            remote(
                source.at[tile_rows(col_peer(j)[1])],
                target.at[tile_rows(col)],
                sem_send.at[j],
                sem_recv.at[j],
                col_peer(j),
            )
            for j in range(1, NCOL)
        ]

    for g in range(NB):
        two = cur[:, BLK * g : BLK * g + BLK]
        vals[g] = two
    rounded = jnp.concatenate([vals[:, 0, :], vals[:, 1, :]], axis=1).astype(BF)
    beside[4] = rounded
    for load in loads[:5]:
        load.wait()
    project(cur, proj, cells, tch, tcl, tsh, tsl, send_c, codes, p_high, p_low, hots, vals, boxed)
    loads[5].wait()
    turn_green(green, turned)
    pl.semaphore_wait(barrier, len(peers))
    third = col_copies(send_c, recv_c, sem_send_c, sem_recv_c)
    for copy in third:
        copy.start()
    halo = [
        remote(beside.at[4], beside.at[8 - n], sem_send_h.at[n], sem_recv_h.at[n], tile_peer(n))
        for n in range(9)
        if n != 4
    ]
    for copy in halo:
        copy.start()
    recv_c[tile_rows(col), :] = send_c[tile_rows(col), :]
    loads[6].wait()
    near_backward(beside, owned, picks, count, matrices, on_a, lv_one, lv_two, spread_back)
    back[4] = spread_back[4]
    returns = [
        remote(spread_back.at[n], back.at[8 - n], sem_send_r.at[n], sem_recv_r.at[n], tile_peer(n))
        for n in range(9)
        if n != 4
    ]
    for copy in returns:
        copy.start()
    for load in loads[7:]:
        load.wait()
    for copy in third:
        copy.wait_recv()
    over = remote(recv_c, far_c, sem_far.at[0], sem_far.at[1], (far, col))
    over.start()
    build_image(recv_c, spread, wide, starts, img)
    sems_a, sems_b = (sem_send_a, sem_recv_a), (sem_send_b, sem_recv_b)
    first, second, beyond = [[], []], [[], []], [[], []]
    for kz in range(2):
        for m in range(2):
            forward_y(kz, chips[m], img, cos, sin, send_a, 2 * chips[m])
            for j in range(2):
                peer = 2 * chips[m] + lax.rem(core + j, 2)
                copy = row_copy(
                    kz, send_a.at[kz, peer], recv_a.at[kz, row], sems_a, 2 * m + j, peer
                )
                copy.start()
                first[kz].append(copy)
        forward_y(kz, z, img, cos, sin, send_a, 2 * z)
        copy = row_copy(kz, send_a.at[kz, sibling], recv_a.at[kz, row], sems_a, 4, sibling)
        copy.start()
        first[kz].append(copy)
        recv_a[kz, row] = send_a[kz, row]
    over.wait_recv()
    build_image(far_c, spread, wide, far_starts, img)
    for kz in range(2):
        forward_y(kz, z, img, cos, sin, far_a, 0)
        copy = row_copy(kz, far_a.at[kz, 1 - core], recv_a.at[kz, far], sems_a, 5, sibling)
        copy.start()
        first[kz].append(copy)
        recv_a[kz, far] = far_a[kz, core]
    build_hot(recv_c, hot)
    build_hot(far_c, far_hot)
    acc[...] = jnp.zeros_like(acc)
    for kz in range(2):
        for copy in first[kz]:
            copy.wait_recv()
        along_x(kz, recv_a, turned, cos, sin, send_b, d_one, d_two, h_one, h_two)
        targets = [2 * chip + lax.rem(core + j, 2) for chip in chips for j in range(2)]
        targets.append(sibling)
        for j, peer in enumerate(targets):
            copy = row_copy(kz, send_b.at[kz, peer], recv_b.at[kz, row], sems_b, j, peer)
            copy.start()
            second[kz].append(copy)
        copy = row_copy(kz, send_b.at[kz, far_sibling], recv_f.at[kz, core], sems_b, 5, sibling)
        copy.start()
        beyond[kz].append(copy)
        recv_b[kz, row] = send_b[kz, row]
        recv_f[kz, core] = send_b[kz, far]
    for kz in range(2):
        beyond[kz][0].wait_recv()
        inverse_y(kz, recv_f, [0], [z], cos, sin, spec, pot)
        pick_cells(kz, pot, far_starts, far_hot, acc)
    fold_cells(acc, spread, send_q, None)
    home = remote(send_q, recv_q, sem_far.at[2], sem_far.at[3], (far, col))
    home.start()
    acc[...] = jnp.zeros_like(acc)
    held = [z] + chips
    for kz in range(2):
        for copy in second[kz]:
            copy.wait_recv()
        inverse_y(kz, recv_b, [2 * chip for chip in held], held, cos, sin, spec, pot)
        pick_cells(kz, pot, starts, hot, acc)
    home.wait_recv()
    fold_cells(acc, spread, send_d, recv_q)
    fourth = col_copies(send_d, recv_d, sem_send_d, sem_recv_d)
    for copy in fourth:
        copy.start()
    recv_d[tile_rows(col), :] = send_d[tile_rows(col), :]
    for copy in halo:
        copy.wait_recv()
    near_onward(beside, owned, picks, count, matrices, on_a, on_b, lv_one, near)
    for copy in returns:
        copy.wait_recv()
    total = near[...]
    for n in range(9):
        total = total + back[n].astype(F32)
    near[...] = total
    for copy in fourth:
        copy.wait_recv()
    back_project(
        recv_d, near, tch, tcl, tsh, tsl, out, p_high, p_low, hots, box_real, box_imag, vals
    )
    for kz in range(2):
        for copy in first[kz] + second[kz] + beyond[kz]:
            copy.wait_send()
    for copy in third + fourth + halo + returns + [over, home]:
        copy.wait_send()


def per_device(
    currents, near_blocks, pair_local, pair_ghost, pair_counts, projection, stencil_cells, green
):
    tables = [jnp.asarray(t) for t in depth_tables()]
    tables.append(jnp.asarray(spread_table()))
    tables += [jnp.asarray(t) for t in grid_tables()]
    vmem, dma = pltpu.VMEM, pltpu.SemaphoreType.DMA
    grid_part = (2, NROW, 2 * XR, 128)
    wrapped = 512 + 2 * NB
    scratch = [
        vmem((PAIRS, 2 * BLK, BLK), BF),
        vmem((NB, BLK, BLK), F32),
        vmem((2, 2, 128, N), F32),
        *[vmem((512, 512), BF)] * 4,
        vmem((128, 2048), BF),
        *[vmem((N, N), BF)] * 2,
        dma((10,)),
        vmem((NB, BLK), jnp.int32),
        *[vmem((NB, BLK, BLK), BF)] * 2,
        vmem((NB, 512, BLK), BF),
        vmem((NB, 2, BLK), F32),
        vmem((2 * NB, 512), F32),
        *[vmem((NB, 512), F32)] * 2,
        *[vmem((9, NB, 2 * BLK), BF)] * 3,
        *[vmem((PAIRS, 2 * BLK), F32)] * 4,
        vmem((NB, 2 * BLK), F32),
        vmem((2, N, 256), F32),
        vmem((wrapped, 2048), BF),
        vmem((wrapped, 128), jnp.int32),
        vmem((2, 2 * XR, N), BF),
        vmem((4, wrapped, XR), BF),
        vmem((wrapped, 2048), BF),
        *[vmem((2 * XR, N), BF)] * 2,
        *[vmem((N, 256), BF)] * 4,
        *[vmem(grid_part, BF)] * 4,
        *[dma((2, NROW))] * 4,
        *[vmem((NCOL * NB, 128), BF)] * 4,
        *[dma((NCOL,))] * 4,
        *[dma((9,))] * 4,
        vmem((NCOL * NB, 128), BF),
        vmem((wrapped, 128), jnp.int32),
        vmem((4, wrapped, XR), BF),
        *[vmem((2, 2, 2 * XR, 128), BF)] * 2,
        *[vmem((NCOL * NB, 128), BF)] * 2,
        dma((4,)),
    ]
    in_vmem = pl.BlockSpec(memory_space=pltpu.VMEM)
    in_smem = pl.BlockSpec(memory_space=pltpu.SMEM)
    anywhere = pl.BlockSpec(memory_space=pl.ANY)
    return pl.pallas_call(
        whole_kernel,
        out_shape=jax.ShapeDtypeStruct((2, NB * BLK), F32),
        in_specs=[in_vmem] * 4 + [in_smem] + [anywhere] * 10,
        out_specs=in_vmem,
        scratch_shapes=scratch,
        compiler_params=pltpu.CompilerParams(
            vmem_limit_bytes=VMEM_LIMIT, collective_id=1, has_side_effects=True
        ),
    )(
        currents,
        stencil_cells,
        pair_local,
        pair_ghost,
        pair_counts,
        near_blocks.reshape(PAIRS, 2 * BLK, BLK),
        projection,
        green,
        *tables,
    )


def solution(mesh):
    in_specs = (
        P(None, ("row", "col")),
        P(("row", "col"), None, None, None),
        P(("row", "col"), None),
        P(("row", "col"), None),
        P(("row", "col")),
        P(("row", "col"), None, None),
        P(("row", "col"), None),
        P(None, "col", "row", None),
    )
    out_specs = P(None, ("row", "col"))
    return jax.shard_map(
        per_device, mesh=mesh, in_specs=in_specs, out_specs=out_specs, check_vma=False
    )
```

```python
import math

import jax
import jax.numpy as jnp
import ml_dtypes
import numpy as np
from jax import lax
from jax.experimental import pallas as pl
from jax.experimental.pallas import tpu as pltpu
from jax.sharding import PartitionSpec as P

N = 1024
NGZ = 32
NROW = 8
NCOL = 16
NB = 32
BLK = 128
PAIRS = 128
XR = 144
WIDE_Y = 68
BF = jnp.bfloat16
F32 = jnp.float32
VMEM_LIMIT = 60 * 1024 * 1024


def bf(a):
    return np.asarray(a, dtype=np.float64).astype(ml_dtypes.bfloat16)


def split_np(a):
    high = bf(a)
    return high, bf(a - high.astype(np.float64))


def grid_tables():
    odd = 2 * np.arange(N) + 1
    angle = (odd[:, None] * odd[None, :] % (4 * N)) * (math.pi / (2 * N))
    return bf(np.cos(angle)), bf(np.sin(angle))


def depth_tables():
    index = np.arange(NGZ)[:, None] * np.arange(NGZ)[None, :] % NGZ
    angle = index * (2.0 * math.pi / NGZ)
    eye = np.eye(16)
    cos_high, cos_low = split_np(np.kron(np.cos(angle), eye))
    sin_high, sin_low = split_np(np.kron(np.sin(angle), eye))
    return cos_high, cos_low, sin_high, sin_low


def spread_tables():
    lane = np.arange(128)[:, None]
    plane, ex, b = lane // 16, lane // 4 % 4, lane % 4
    wide = np.arange(2048)[None, :]
    hits = (wide // 512 == ex) & (wide // 128 % 4 == plane) & (lane < 64)
    ahead = hits & ((wide + 2) % 4 == b)
    backwards = hits & ((wide + 2) % 4 == 3 - b)
    return bf(ahead.astype(np.float64)), bf(backwards.astype(np.float64))


def dot(a, b):
    return jnp.dot(a, b, preferred_element_type=F32)


def dot_nt(a, b):
    return lax.dot_general(a, b, (((1,), (1,)), ((), ())), preferred_element_type=F32)


def iota(shape, dim):
    return lax.broadcasted_iota(jnp.int32, shape, dim)


def high_low(a):
    high = a.astype(BF)
    return high, (a - high.astype(F32)).astype(BF)


def rows_high_low(a):
    high = a.astype(BF).astype(F32)
    return jnp.concatenate([high, a - high], axis=0).astype(BF)


def cell_codes(cells):
    z = cells & (NGZ - 1)
    t = cells >> 5
    x = (t * 15421) >> 20
    y = t - x * WIDE_Y
    corner_x = jnp.min(x, axis=1, keepdims=True)
    corner_y = jnp.min(y, axis=1, keepdims=True)
    code = z * 16 + (x - corner_x) * 4 + (y & 3)
    return code, corner_x, corner_y


def one_hot_rows(code_row):
    return jnp.where(iota((512, 128), 0) == code_row, 1.0, 0.0).astype(BF)


def store_twist(corner_x, corner_y, row, col, twist):
    lane = iota((NB, 128), 1)
    x = (corner_x + ((lane >> 2) & 3) + 128 * row - 2) & (N - 1)
    y = (corner_y + ((lane - corner_y) & 3) + 64 * col - 2) & (N - 1)
    angle = (x + y).astype(F32) * (math.pi / N)
    twist[0] = jnp.concatenate([jnp.cos(angle)] * 4, axis=1)
    twist[1] = jnp.concatenate([jnp.sin(angle)] * 4, axis=1)


def project(
    cur, proj, cells, tch, tcl, tsh, tsl, out, codes, p_high, p_low, hots, vals, boxed, row, col, twist
):
    code, corner_x, corner_y = cell_codes(cells[...])
    codes[...] = code

    def values_of(i, carry):
        for u in range(8):
            g = i * 8 + u
            lhs = rows_high_low(cur[:, pl.ds(pl.multiple_of(g * BLK, BLK), BLK)])
            high, low = high_low(proj[g])
            p_high[g] = high
            p_low[g] = low
            first = dot_nt(lhs, high)
            vals[g] = first[0:2] + first[2:4] + dot_nt(lhs, low)[0:2]
        return carry

    lax.fori_loop(0, NB // 8, values_of, 0)

    def boxes_of(i, carry):
        for u in range(8):
            g = i * 8 + u
            hot = one_hot_rows(codes[pl.ds(g, 1), :])
            hots[g] = hot
            placed = dot_nt(rows_high_low(vals[g]), hot)
            boxed[pl.ds(g, 1), :] = placed[0:1] + placed[2:3]
            boxed[pl.ds(NB + g, 1), :] = placed[1:2] + placed[3:4]
        return carry

    lax.fori_loop(0, NB // 8, boxes_of, 0)
    b_high, b_low = high_low(boxed[...])
    along_cos = dot(b_high, tch[...]) + dot(b_low, tch[...]) + dot(b_high, tcl[...])
    along_sin = dot(b_high, tsh[...]) + dot(b_low, tsh[...]) + dot(b_high, tsl[...])
    store_twist(corner_x, corner_y, row, col, twist)
    plain_real = along_cos[:NB] + along_sin[NB:]
    plain_imag = along_cos[NB:] - along_sin[:NB]
    real = plain_real * twist[0] - plain_imag * twist[1]
    imag = plain_real * twist[1] + plain_imag * twist[0]
    lane = iota((NB, 64), 1)
    corners = jnp.where(lane == 0, corner_x, jnp.where(lane == 1, corner_y, 0)).astype(F32)
    for c in range(NCOL):
        part = slice(32 * c, 32 * c + 32)
        message = jnp.concatenate([real[:, part], imag[:, part], corners], axis=1)
        out[NB * c : NB * c + NB, :] = message.astype(BF)


def local_x_of_row(shape, dim, band):
    row = iota(shape, dim)
    tile = row - 128
    main = jnp.where(band >= 4, 129 - row, row + 2)
    upper = jnp.where(lax.rem(band + 1, NROW) >= 4, 137 - tile, 130 + tile)
    upper = jnp.where((upper >= 130) & (upper < 132), upper, -64)
    lower = jnp.where(lax.rem(band + NROW - 1, NROW) >= 4, 9 - tile, tile - 14)
    lower = jnp.where((lower >= 0) & (lower < 2), lower, -64)
    return jnp.where(row < 128, main, jnp.where(tile < 8, upper, lower))


def store_starts(recv, starts):
    block = iota((512, 1), 0)
    start = recv[:, 65:66].astype(jnp.int32) + (block // NB) * 64 - 2
    starts[NB : NB + 512, :] = jnp.broadcast_to(start, (512, 128))
    starts[0:NB, :] = starts[512 : 512 + NB, :]
    starts[NB + 512 :, :] = starts[NB : 2 * NB, :]


def chunk_mask(starts, q):
    lane = iota((128, 128), 1)
    cell = 128 * q + lane if q < 4 else 128 * q + 127 - lane
    inside = ((cell - starts[64 * q : 64 * q + 128, :]) & (N - 1)) < 4
    return jnp.where(inside, 1.0, 0.0)


def image_chunk(q, corner, local_x, wides, starts):
    first = 64 * q if q < 4 else 64 * q - 256
    wide = wides[0] if q < 4 else wides[1]
    mask = chunk_mask(starts, q).astype(BF)
    mask = jnp.concatenate([mask] * 4, axis=1)
    offset = local_x - corner[0:1, 64 * q : 64 * q + 128].astype(jnp.int32)
    lhs = [jnp.where(offset == ex, 1.0, 0.0).astype(BF) for ex in range(4)]
    rhs = [wide[first : first + 128, 512 * ex : 512 * ex + 512] * mask for ex in range(4)]
    return dot(jnp.concatenate(lhs, axis=1), jnp.concatenate(rhs, axis=0))


def build_image(recv, band, spreads, padded, wides, starts, odd, even):
    padded[0:NB, :] = recv[512 - NB :, :]
    padded[NB : NB + 512, :] = recv[...]
    padded[NB + 512 :, :] = recv[0:NB, :]

    def spread_lanes(i, carry):
        lanes = pl.ds(pl.multiple_of(i * 512, 512), 512)
        wides[0][:, lanes] = dot(padded[0:320, :], spreads[0][:, lanes]).astype(BF)
        wides[1][:, lanes] = dot(padded[256:576, :], spreads[1][:, lanes]).astype(BF)
        return carry

    lax.fori_loop(0, 4, spread_lanes, 0)
    store_starts(recv, starts)
    pick = jnp.where(iota((16, 128), 1) == 64, 1.0, 0.0).astype(BF)
    corner = dot_nt(pick, recv[...])[0:8]
    corner = jnp.concatenate([corner[:, 480:], corner, corner[:, :NB]], axis=1)
    local_x = local_x_of_row((XR, 128), 0, band)
    for q in range(4):
        ahead = image_chunk(q, corner, local_x, wides, starts)
        backwards = image_chunk(7 - q, corner, local_x, wides, starts)
        minus, plus = (ahead - backwards).astype(BF), (ahead + backwards).astype(BF)
        for kz in range(2):
            for c in range(2):
                p = 2 * c + kz
                place = (kz, slice(XR * c, XR * c + XR), slice(128 * q, 128 * q + 128))
                odd[place] = minus[:, 128 * p : 128 * p + 128]
                even[place] = plus[:, 128 * p : 128 * p + 128]


def forward_y(kz, chip, odd, even, cos, sin, out, slot):
    lanes = pl.ds(pl.multiple_of(chip * 256, 256), 256)
    by_cos = dot(odd[kz], cos[0:512, lanes])
    by_sin = dot(even[kz], sin[0:512, lanes])
    real = (by_cos[:XR] + by_sin[XR:]).astype(BF)
    imag = (by_cos[XR:] - by_sin[:XR]).astype(BF)
    for j in range(2):
        out[kz, slot + j, 0:XR, :] = real[:, 128 * j : 128 * j + 128]
        out[kz, slot + j, XR:, :] = imag[:, 128 * j : 128 * j + 128]


def along_x(kz, recv, green, cos, sin, out, d_one, d_two, h_one, h_two):
    none = jnp.zeros((8, 128), F32)
    for r in range(NROW):
        before, after = (r - 1) % NROW, (r + 1) % NROW
        back = r >= 4
        start = 512 + 128 * (7 - r) if back else 128 * r
        rows = slice(start, start + 128)
        for c in range(2):
            base = XR * c
            main = recv[kz, r, base : base + 128, :]
            upper = recv[kz, before, base + 128 : base + XR, :].astype(F32)[0:8]
            lower = recv[kz, after, base + 128 : base + XR, :].astype(F32)[8:16]
            head, tail = (lower, upper) if back else (upper, lower)
            head = main[0:16].astype(F32) + jnp.concatenate([head, none], axis=0)
            tail = main[112:128].astype(F32) + jnp.concatenate([none, tail], axis=0)
            band = jnp.concatenate([head.astype(BF), main[16:112], tail.astype(BF)], axis=0)
            d_one[rows, 128 * c : 128 * c + 128] = -band if back else band
            d_two[rows, 128 - 128 * c : 256 - 128 * c] = -band if c == 0 else band

    def forward(i, carry):
        rows = pl.ds(pl.multiple_of(i * 256, 256), 256)
        high_rows = pl.ds(pl.multiple_of(i * 256 + 512, 256), 256)
        cos_i, sin_i = cos[rows, 0:512], sin[rows, 0:512]
        by_cos = dot(cos_i, d_one[0:512, :]) + dot(cos_i, d_one[512:, :])
        by_sin = dot(sin_i, d_two[0:512, :]) + dot(sin_i, d_two[512:, :])
        lanes = slice(128 * kz, 128 * kz + 128)
        parts = []
        for spec, where in ((by_sin + by_cos, rows), (by_sin - by_cos, high_rows)):
            real, imag = spec[:, :128], spec[:, 128:]
            g_real, g_imag = green[0, where, lanes], green[1, where, lanes]
            parts.append((real * g_real - imag * g_imag, real * g_imag + imag * g_real))
        (low_real, low_imag), (high_real, high_imag) = parts
        h_one[rows, 0:128] = (low_real - high_real).astype(BF)
        h_one[rows, 128:256] = (low_imag - high_imag).astype(BF)
        h_two[rows, 0:128] = -(low_imag + high_imag).astype(BF)
        h_two[rows, 128:256] = (low_real + high_real).astype(BF)
        return carry

    lax.fori_loop(0, 2, forward, 0)

    def inverse(i, carry):
        rows = pl.ds(pl.multiple_of(i * 256, 256), 256)
        by_cos = dot(cos[rows, 0:512], h_one[...])
        by_sin = dot(sin[rows, 0:512], h_two[...])
        low, high = (by_sin + by_cos).astype(BF), (by_sin - by_cos).astype(BF)
        for j in range(2):
            for c in range(2):
                place = (slice(128 * j, 128 * j + 128), slice(128 * c, 128 * c + 128))
                out[kz, 2 * i + j, XR * c : XR * c + 128, :] = low[place]
                out[kz, 7 - 2 * i - j, XR * c : XR * c + 128, :] = high[place]
        return carry

    lax.fori_loop(0, 2, inverse, 0)
    for r in range(NROW):
        before, after = (r - 1) % NROW, (r + 1) % NROW
        for c in range(2):
            base = XR * c
            above = out[kz, after, base : base + 16, :].astype(F32)[0:8]
            if after >= 4:
                above = out[kz, after, base + 112 : base + 128, :].astype(F32)[8:16]
            below = out[kz, before, base + 112 : base + 128, :].astype(F32)[8:16]
            if before >= 4:
                below = out[kz, before, base : base + 16, :].astype(F32)[0:8]
            out[kz, r, base + 128 : base + XR, :] = jnp.concatenate([above, below], axis=0).astype(BF)


def inverse_y(kz, recv, slots, chips, cos, sin, spec, pot):
    for m, slot in enumerate(slots):
        for j in range(2):
            spec[:, 256 * m + 128 * j : 256 * m + 128 * j + 128] = recv[kz, slot + j]

    def lanes_of(i, carry):
        lanes = pl.ds(pl.multiple_of(i * 256, 256), 256)
        by_cos, by_sin = 0.0, 0.0
        for m, chip in enumerate(chips):
            rows = pl.ds(pl.multiple_of(chip * 256, 256), 256)
            part = spec[:, 256 * m : 256 * m + 256]
            by_cos = by_cos + dot(part, cos[rows, lanes])
            by_sin = by_sin + dot(part, sin[rows, lanes])
        high_lanes = pl.ds(pl.multiple_of(i * 256 + 512, 256), 256)
        pot[0:XR, lanes] = (by_cos[:XR] - by_sin[XR:]).astype(BF)
        pot[XR:, lanes] = (by_cos[XR:] + by_sin[:XR]).astype(BF)
        pot[0:XR, high_lanes] = -(by_cos[:XR] + by_sin[XR:]).astype(BF)
        pot[XR:, high_lanes] = (by_sin[:XR] - by_cos[XR:]).astype(BF)
        return carry

    lax.fori_loop(0, 2, lanes_of, 0)


def build_hot(recv, band, hot):
    local_x = local_x_of_row((512, XR), 1, band)
    offset = local_x - recv[:, 64:65].astype(jnp.int32)
    for ex in range(4):
        hot[ex, NB : NB + 512, :] = jnp.where(offset == ex, 1.0, 0.0).astype(BF)
    hot[:, 0:NB, :] = hot[:, 512 : 512 + NB, :]
    hot[:, NB + 512 :, :] = hot[:, NB : 2 * NB, :]


def pick_cells(kz, pot, starts, hot, accs):
    for q in range(8):
        mask = chunk_mask(starts, q)
        mask = jnp.concatenate([mask] * 2, axis=1)
        lane = 128 * q if q < 4 else 512 + 128 * (7 - q)
        cells = [pot[XR * c : XR * c + XR, lane : lane + 128] for c in range(2)]
        cells = jnp.concatenate(cells, axis=1)
        first = 64 * q if q < 4 else 64 * q - 256
        rows = slice(first, first + 128)
        acc = accs[0] if q < 4 else accs[1]
        for ex in range(4):
            taken = (dot(hot[ex, 64 * q : 64 * q + 128, :], cells) * mask).astype(BF)
            for c in range(2):
                lane = 512 * ex + 256 * c + 128 * kz
                lanes = slice(lane, lane + 128)
                acc[rows, lanes] = acc[rows, lanes] + taken[:, 128 * c : 128 * c + 128]


def clear_cells(accs):
    for acc in accs:
        acc[...] = jnp.zeros_like(acc)


def fold_cells(accs, spreads, out, extra):
    a = dot_nt(accs[0][...], spreads[0][...])
    b = dot_nt(accs[1][...], spreads[1][...])
    pieces = [a[32:64] + b[288:320], a[64:256], a[256:320] + b[0:64], b[64:256], b[256:288] + a[0:32]]
    cells = jnp.concatenate(pieces, axis=0)
    if extra is not None:
        cells = cells + extra[...].astype(F32)
    out[...] = cells.astype(BF)


def back_project(
    recv, near, tch, tcl, tsh, tsl, out, p_high, p_low, hots, box_real, box_imag, vals, twist
):
    real = jnp.concatenate([recv[NB * c : NB * c + NB, 0:32] for c in range(NCOL)], axis=1)
    imag = jnp.concatenate([recv[NB * c : NB * c + NB, 32:64] for c in range(NCOL)], axis=1)
    real, imag = real.astype(F32), imag.astype(F32)
    turned_real = real * twist[0] + imag * twist[1]
    turned_imag = imag * twist[0] - real * twist[1]
    b_high, b_low = high_low(jnp.concatenate([turned_real, turned_imag], axis=0))
    along_cos = dot(b_high, tch[...]) + dot(b_low, tch[...]) + dot(b_high, tcl[...])
    along_sin = dot(b_high, tsh[...]) + dot(b_low, tsh[...]) + dot(b_high, tsl[...])
    box_real[...] = along_cos[:NB] - along_sin[NB:]
    box_imag[...] = along_cos[NB:] + along_sin[:NB]

    def values_of(i, carry):
        for u in range(8):
            g = i * 8 + u
            box = jnp.concatenate([box_real[pl.ds(g, 1), :], box_imag[pl.ds(g, 1), :]], axis=0)
            picked = dot(rows_high_low(box), hots[g])
            vals[g] = picked[0:2] + picked[2:4]
        return carry

    lax.fori_loop(0, NB // 8, values_of, 0)

    def blocks_of(i, carry):
        for u in range(8):
            g = i * 8 + u
            lhs = rows_high_low(vals[g])
            first = dot(lhs, p_high[g])
            far = first[0:2] + first[2:4] + dot(lhs, p_low[g])[0:2]
            row = near[pl.ds(g, 1), :]
            beside = jnp.concatenate([row[:, :BLK], row[:, BLK:]], axis=0)
            out[:, pl.ds(pl.multiple_of(g * BLK, BLK), BLK)] = far + beside
        return carry

    lax.fori_loop(0, NB // 8, blocks_of, 0)


def column_of(row):
    return jnp.transpose(jnp.broadcast_to(row.astype(F32), (8, 128)))[:, 0:1].astype(jnp.int32)


def near_backward(beside, owned, picks, count, matrices, back_a, lv_one, lv_two, spread_back):
    hits = jnp.where(iota((PAIRS, NB), 1) == column_of(owned[...]), 1.0, 0.0).astype(BF)
    local = dot(hits, beside[4])
    real, imag = local[:, :BLK], local[:, BLK:]
    lv_one[...] = jnp.concatenate([real, -imag], axis=1)
    lv_two[...] = jnp.concatenate([imag, real], axis=1)
    first_row = iota((8, 2 * BLK), 0) == 0

    def pairs_of(i, carry):
        for u in range(8):
            p = i * 8 + u
            lhs = jnp.where(first_row, lv_one[pl.ds(p, 1), :], lv_two[pl.ds(p, 1), :]).astype(BF)
            got = dot(lhs, matrices[p])
            back_a[pl.ds(p, 1), :] = jnp.concatenate([got[0:1], got[1:2]], axis=1)
        return carry

    lax.fori_loop(0, PAIRS // 8, pairs_of, 0)
    alive = iota((9 * NB, PAIRS), 1) < count[0]
    hits = (iota((9 * NB, PAIRS), 0) == picks[...]) & alive
    table = jnp.where(hits, 1.0, 0.0).astype(BF)
    high, low = high_low(back_a[...])
    total = (dot(table, high) + dot(table, low)).astype(BF)
    for n in range(9):
        spread_back[n] = total[NB * n : NB * n + NB, :]


def near_onward(beside, owned, picks, count, matrices, on_a, on_b, lv_one, near):
    hits = jnp.where(iota((PAIRS, 9 * NB), 1) == column_of(picks[...]), 1.0, 0.0).astype(BF)
    lv_one[...] = dot(hits, jnp.concatenate([beside[n] for n in range(9)], axis=0))
    first_row = iota((8, BLK), 0) == 0

    def pairs_of(i, carry):
        for u in range(8):
            p = i * 8 + u
            row = lv_one[pl.ds(p, 1), :]
            lhs = jnp.where(first_row, row[:, :BLK], row[:, BLK:]).astype(BF)
            got = dot_nt(lhs, matrices[p])
            on_a[pl.ds(p, 1), :] = got[0:1]
            on_b[pl.ds(p, 1), :] = got[1:2]
        return carry

    lax.fori_loop(0, PAIRS // 8, pairs_of, 0)
    real = on_a[:, :BLK] - on_b[:, BLK:]
    imag = on_b[:, :BLK] + on_a[:, BLK:]
    alive = iota((NB, PAIRS), 1) < count[0]
    table = jnp.where((iota((NB, PAIRS), 0) == owned[...]) & alive, 1.0, 0.0).astype(BF)
    high, low = high_low(jnp.concatenate([real, imag], axis=1))
    near[...] = dot(table, high) + dot(table, low)


def turn_green(green, turned):
    turn = jnp.where(iota((128, 128), 0) + iota((128, 128), 1) == 127, 1.0, 0.0).astype(BF)
    for c in range(2):
        for kz in range(2):

            def part(i, carry):
                rows = pl.ds(pl.multiple_of(i * 128, 128), 128)
                high_rows = pl.ds(pl.multiple_of(896 - i * 128, 128), 128)
                target = pl.ds(pl.multiple_of(i * 128 + 512, 128), 128)
                lanes = slice(128 * kz, 128 * kz + 128)
                scale = 1.0 / (N * N * NGZ)
                turned[c, rows, lanes] = jnp.transpose(green[c, kz, :, rows]) * scale
                high, low = high_low(green[c, kz, :, high_rows] * scale)
                turned[c, target, lanes] = dot_nt(turn, high) + dot_nt(turn, low)
                return carry

            lax.fori_loop(0, 4, part, 0)


def whole_kernel(
    cur, cells, owned, picks, count, near_hbm, proj_hbm, green_hbm,
    tch_hbm, tcl_hbm, tsh_hbm, tsl_hbm, ahead_hbm, backwards_hbm, cos_hbm, sin_hbm, out,
    matrices, proj, green, tch, tcl, tsh, tsl, ahead, backwards, cos, sin, load_sem, twist,
    codes, p_high, p_low, hots, vals, boxed, box_real, box_imag,
    beside, spread_back, back, on_a, on_b, lv_one, lv_two, near, turned,
    padded, wide_a, wide_b, starts, odd, even, hot, acc_a, acc_b, spec, pot, d_one, d_two, h_one, h_two,
    send_a, recv_a, send_b, recv_b, sem_send_a, sem_recv_a, sem_send_b, sem_recv_b,
    send_c, recv_c, send_d, recv_d, sem_send_c, sem_recv_c, sem_send_d, sem_recv_d,
    sem_send_h, sem_recv_h, sem_send_r, sem_recv_r,
    far_c, far_starts, far_hot, far_a, recv_f, send_q, recv_q, sem_far,
):
    row, col = lax.axis_index("row"), lax.axis_index("col")
    mesh_ids = pl.DeviceIdType.MESH

    def row_peer(j):
        return (lax.rem(row + j, NROW), col)

    def col_peer(j):
        return (row, lax.rem(col + j, NCOL))

    def tile_peer(n):
        return (lax.rem(row + n // 3 - 1 + NROW, NROW), lax.rem(col + n % 3 - 1 + NCOL, NCOL))

    barrier = pltpu.get_barrier_semaphore()
    peers = [row_peer(j) for j in range(1, NROW)] + [col_peer(j) for j in range(1, NCOL)]
    peers += [tile_peer(n) for n in (0, 2, 6, 8)]
    for peer in peers:
        pl.semaphore_signal(barrier, inc=1, device_id=peer, device_id_type=mesh_ids)

    pairs = [
        (proj_hbm, proj), (tch_hbm, tch), (tcl_hbm, tcl), (tsh_hbm, tsh), (tsl_hbm, tsl),
        (near_hbm, matrices), (ahead_hbm, ahead), (backwards_hbm, backwards), (cos_hbm, cos),
        (sin_hbm, sin), (green_hbm, green),
    ]
    loads = [pltpu.make_async_copy(a, b, load_sem.at[i]) for i, (a, b) in enumerate(pairs)]
    for load in loads:
        load.start()

    def remote(source, target, sem_send, sem_recv, peer):
        return pltpu.make_async_remote_copy(
            src_ref=source,
            dst_ref=target,
            send_sem=sem_send,
            recv_sem=sem_recv,
            device_id=peer,
            device_id_type=mesh_ids,
        )

    z, core = row // 2, lax.rem(row, 2)
    sibling = 2 * z + 1 - core
    far, far_sibling = lax.rem(row + 4, NROW), lax.rem(sibling + 4, NROW)
    chips = [lax.rem(z + 1, 4), lax.rem(z + 3, 4)]

    def row_copy(kz, source, target, sems, j, peer):
        return remote(source, target, sems[0].at[kz, j], sems[1].at[kz, j], (peer, col))

    def tile_rows(c):
        return pl.ds(pl.multiple_of(c * NB, NB), NB)

    def col_copies(source, target, sem_send, sem_recv):
        return [
            remote(
                source.at[tile_rows(col_peer(j)[1])],
                target.at[tile_rows(col)],
                sem_send.at[j],
                sem_recv.at[j],
                col_peer(j),
            )
            for j in range(1, NCOL)
        ]

    for g in range(NB):
        two = cur[:, BLK * g : BLK * g + BLK]
        vals[g] = two
    rounded = jnp.concatenate([vals[:, 0, :], vals[:, 1, :]], axis=1).astype(BF)
    beside[4] = rounded
    for load in loads[:5]:
        load.wait()
    spreads, wides, accs = (ahead, backwards), (wide_a, wide_b), (acc_a, acc_b)
    project(
        cur, proj, cells, tch, tcl, tsh, tsl, send_c, codes, p_high, p_low, hots, vals, boxed,
        row, col, twist,
    )
    pl.semaphore_wait(barrier, len(peers))
    third = col_copies(send_c, recv_c, sem_send_c, sem_recv_c)
    for copy in third:
        copy.start()
    halo = [
        remote(beside.at[4], beside.at[8 - n], sem_send_h.at[n], sem_recv_h.at[n], tile_peer(n))
        for n in range(9)
        if n != 4
    ]
    for copy in halo:
        copy.start()
    recv_c[tile_rows(col), :] = send_c[tile_rows(col), :]
    loads[5].wait()
    near_backward(beside, owned, picks, count, matrices, on_a, lv_one, lv_two, spread_back)
    back[4] = spread_back[4]
    returns = [
        remote(spread_back.at[n], back.at[8 - n], sem_send_r.at[n], sem_recv_r.at[n], tile_peer(n))
        for n in range(9)
        if n != 4
    ]
    for copy in returns:
        copy.start()
    for load in loads[6:]:
        load.wait()
    for copy in third:
        copy.wait_recv()
    over = remote(recv_c, far_c, sem_far.at[0], sem_far.at[1], (far, col))
    over.start()
    build_image(recv_c, row, spreads, padded, wides, starts, odd, even)
    sems_a, sems_b = (sem_send_a, sem_recv_a), (sem_send_b, sem_recv_b)
    first, second, beyond = [[], []], [[], []], [[], []]
    for kz in range(2):
        for m in range(2):
            forward_y(kz, chips[m], odd, even, cos, sin, send_a, 2 * chips[m])
            for j in range(2):
                peer = 2 * chips[m] + lax.rem(core + j, 2)
                copy = row_copy(
                    kz, send_a.at[kz, peer], recv_a.at[kz, row], sems_a, 2 * m + j, peer
                )
                copy.start()
                first[kz].append(copy)
        forward_y(kz, z, odd, even, cos, sin, send_a, 2 * z)
        copy = row_copy(kz, send_a.at[kz, sibling], recv_a.at[kz, row], sems_a, 4, sibling)
        copy.start()
        first[kz].append(copy)
        recv_a[kz, row] = send_a[kz, row]
    over.wait_recv()
    build_image(far_c, far, spreads, padded, wides, far_starts, odd, even)
    for kz in range(2):
        forward_y(kz, z, odd, even, cos, sin, far_a, 0)
        copy = row_copy(kz, far_a.at[kz, 1 - core], recv_a.at[kz, far], sems_a, 5, sibling)
        copy.start()
        first[kz].append(copy)
        recv_a[kz, far] = far_a[kz, core]
    turn_green(green, turned)
    build_hot(recv_c, row, hot)
    build_hot(far_c, far, far_hot)
    clear_cells(accs)
    for kz in range(2):
        for copy in first[kz]:
            copy.wait_recv()
        along_x(kz, recv_a, turned, cos, sin, send_b, d_one, d_two, h_one, h_two)
        targets = [2 * chip + lax.rem(core + j, 2) for chip in chips for j in range(2)]
        targets.append(sibling)
        for j, peer in enumerate(targets):
            copy = row_copy(kz, send_b.at[kz, peer], recv_b.at[kz, row], sems_b, j, peer)
            copy.start()
            second[kz].append(copy)
        copy = row_copy(kz, send_b.at[kz, far_sibling], recv_f.at[kz, core], sems_b, 5, sibling)
        copy.start()
        beyond[kz].append(copy)
        recv_b[kz, row] = send_b[kz, row]
        recv_f[kz, core] = send_b[kz, far]
    for kz in range(2):
        beyond[kz][0].wait_recv()
        inverse_y(kz, recv_f, [0], [z], cos, sin, spec, pot)
        pick_cells(kz, pot, far_starts, far_hot, accs)
    fold_cells(accs, spreads, send_q, None)
    home = remote(send_q, recv_q, sem_far.at[2], sem_far.at[3], (far, col))
    home.start()
    clear_cells(accs)
    held = [z] + chips
    for kz in range(2):
        for copy in second[kz]:
            copy.wait_recv()
        inverse_y(kz, recv_b, [2 * chip for chip in held], held, cos, sin, spec, pot)
        pick_cells(kz, pot, starts, hot, accs)
    home.wait_recv()
    fold_cells(accs, spreads, send_d, recv_q)
    fourth = col_copies(send_d, recv_d, sem_send_d, sem_recv_d)
    for copy in fourth:
        copy.start()
    recv_d[tile_rows(col), :] = send_d[tile_rows(col), :]
    for copy in halo:
        copy.wait_recv()
    near_onward(beside, owned, picks, count, matrices, on_a, on_b, lv_one, near)
    for copy in returns:
        copy.wait_recv()
    total = near[...]
    for n in range(9):
        total = total + back[n].astype(F32)
    near[...] = total
    for copy in fourth:
        copy.wait_recv()
    back_project(
        recv_d, near, tch, tcl, tsh, tsl, out, p_high, p_low, hots, box_real, box_imag, vals, twist
    )
    for kz in range(2):
        for copy in first[kz] + second[kz] + beyond[kz]:
            copy.wait_send()
    for copy in third + fourth + halo + returns + [over, home]:
        copy.wait_send()


def per_device(
    currents, near_blocks, pair_local, pair_ghost, pair_counts, projection, stencil_cells, green
):
    tables = [jnp.asarray(t) for t in depth_tables()]
    tables += [jnp.asarray(t) for t in spread_tables()]
    tables += [jnp.asarray(t) for t in grid_tables()]
    vmem, dma = pltpu.VMEM, pltpu.SemaphoreType.DMA
    grid_part = (2, NROW, 2 * XR, 128)
    wrapped = 512 + 2 * NB
    scratch = [
        vmem((PAIRS, 2 * BLK, BLK), BF),
        vmem((NB, BLK, BLK), F32),
        vmem((2, 2, 128, N), F32),
        *[vmem((512, 512), BF)] * 4,
        *[vmem((128, 2048), BF)] * 2,
        *[vmem((N, N), BF)] * 2,
        dma((11,)),
        vmem((2, NB, 512), F32),
        vmem((NB, BLK), jnp.int32),
        *[vmem((NB, BLK, BLK), BF)] * 2,
        vmem((NB, 512, BLK), BF),
        vmem((NB, 2, BLK), F32),
        vmem((2 * NB, 512), F32),
        *[vmem((NB, 512), F32)] * 2,
        *[vmem((9, NB, 2 * BLK), BF)] * 3,
        *[vmem((PAIRS, 2 * BLK), F32)] * 4,
        vmem((NB, 2 * BLK), F32),
        vmem((2, N, 256), F32),
        vmem((wrapped, 128), BF),
        *[vmem((320, 2048), BF)] * 2,
        vmem((wrapped, 128), jnp.int32),
        *[vmem((2, 2 * XR, 512), BF)] * 2,
        vmem((4, wrapped, XR), BF),
        *[vmem((320, 2048), BF)] * 2,
        *[vmem((2 * XR, N), BF)] * 2,
        *[vmem((N, 256), BF)] * 2,
        *[vmem((512, 256), BF)] * 2,
        *[vmem(grid_part, BF)] * 4,
        *[dma((2, NROW))] * 4,
        *[vmem((NCOL * NB, 128), BF)] * 4,
        *[dma((NCOL,))] * 4,
        *[dma((9,))] * 4,
        vmem((NCOL * NB, 128), BF),
        vmem((wrapped, 128), jnp.int32),
        vmem((4, wrapped, XR), BF),
        *[vmem((2, 2, 2 * XR, 128), BF)] * 2,
        *[vmem((NCOL * NB, 128), BF)] * 2,
        dma((4,)),
    ]
    in_vmem = pl.BlockSpec(memory_space=pltpu.VMEM)
    in_smem = pl.BlockSpec(memory_space=pltpu.SMEM)
    anywhere = pl.BlockSpec(memory_space=pl.ANY)
    return pl.pallas_call(
        whole_kernel,
        out_shape=jax.ShapeDtypeStruct((2, NB * BLK), F32),
        in_specs=[in_vmem] * 4 + [in_smem] + [anywhere] * 11,
        out_specs=in_vmem,
        scratch_shapes=scratch,
        compiler_params=pltpu.CompilerParams(
            vmem_limit_bytes=VMEM_LIMIT, collective_id=1, has_side_effects=True
        ),
    )(
        currents,
        stencil_cells,
        pair_local,
        pair_ghost,
        pair_counts,
        near_blocks.reshape(PAIRS, 2 * BLK, BLK),
        projection,
        green,
        *tables,
    )


def solution(mesh):
    in_specs = (
        P(None, ("row", "col")),
        P(("row", "col"), None, None, None),
        P(("row", "col"), None),
        P(("row", "col"), None),
        P(("row", "col")),
        P(("row", "col"), None, None),
        P(("row", "col"), None),
        P(None, "col", "row", None),
    )
    out_specs = P(None, ("row", "col"))
    return jax.shard_map(
        per_device, mesh=mesh, in_specs=in_specs, out_specs=out_specs, check_vma=False
    )
```

```python
import math

import jax
import jax.numpy as jnp
import ml_dtypes
import numpy as np
from jax import lax
from jax.experimental import pallas as pl
from jax.experimental.pallas import tpu as pltpu
from jax.sharding import PartitionSpec as P

N = 1024
NGZ = 32
NROW = 8
NCOL = 16
NB = 32
BLK = 128
PAIRS = 128
XR = 144
WIDE_Y = 68
BF = jnp.bfloat16
F32 = jnp.float32
VMEM_LIMIT = 60 * 1024 * 1024


def bf(a):
    return np.asarray(a, dtype=np.float64).astype(ml_dtypes.bfloat16)


def split_np(a):
    high = bf(a)
    return high, bf(a - high.astype(np.float64))


def grid_tables():
    odd = 2 * np.arange(N) + 1
    angle = (odd[:, None] * odd[None, :] % (4 * N)) * (math.pi / (2 * N))
    return bf(np.cos(angle)), bf(np.sin(angle))


def depth_tables():
    index = np.arange(NGZ)[:, None] * np.arange(NGZ)[None, :] % NGZ
    angle = index * (2.0 * math.pi / NGZ)
    eye = np.eye(16)
    cos_high, cos_low = split_np(np.kron(np.cos(angle), eye))
    sin_high, sin_low = split_np(np.kron(np.sin(angle), eye))
    return cos_high, cos_low, sin_high, sin_low


def spread_tables():
    lane = np.arange(128)[:, None]
    plane, ex, b = lane // 16, lane // 4 % 4, lane % 4
    wide = np.arange(2048)[None, :]
    hits = (wide // 512 == ex) & (wide // 128 % 4 == plane) & (lane < 64)
    ahead = hits & ((wide + 2) % 4 == b)
    backwards = hits & ((wide + 2) % 4 == 3 - b)
    return bf(ahead.astype(np.float64)), bf(backwards.astype(np.float64))


def dot(a, b):
    return jnp.dot(a, b, preferred_element_type=F32)


def dot_nt(a, b):
    return lax.dot_general(a, b, (((1,), (1,)), ((), ())), preferred_element_type=F32)


def iota(shape, dim):
    return lax.broadcasted_iota(jnp.int32, shape, dim)


def high_low(a):
    high = a.astype(BF)
    return high, (a - high.astype(F32)).astype(BF)


def rows_high_low(a):
    high = a.astype(BF).astype(F32)
    return jnp.concatenate([high, a - high], axis=0).astype(BF)


def cell_codes(cells):
    z = cells & (NGZ - 1)
    t = cells >> 5
    x = (t * 15421) >> 20
    y = t - x * WIDE_Y
    corner_x = jnp.min(x, axis=1, keepdims=True)
    corner_y = jnp.min(y, axis=1, keepdims=True)
    code = z * 16 + (x - corner_x) * 4 + (y & 3)
    return code, corner_x, corner_y


def one_hot_rows(code_row):
    return jnp.where(iota((512, 128), 0) == code_row, 1.0, 0.0).astype(BF)


def store_twist(corner_x, corner_y, row, col, twist):
    lane = iota((NB, 128), 1)
    x = (corner_x + ((lane >> 2) & 3) + 128 * row - 2) & (N - 1)
    y = (corner_y + ((lane - corner_y) & 3) + 64 * col - 2) & (N - 1)
    angle = (x + y).astype(F32) * (math.pi / N)
    twist[0] = jnp.concatenate([jnp.cos(angle)] * 4, axis=1)
    twist[1] = jnp.concatenate([jnp.sin(angle)] * 4, axis=1)


def project(
    cur, proj, cells, tch, tcl, tsh, tsl, out, codes, p_high, p_low, hots, vals, boxed, row, col, twist
):
    code, corner_x, corner_y = cell_codes(cells[...])
    codes[...] = code

    def values_of(i, carry):
        for u in range(8):
            g = i * 8 + u
            lhs = rows_high_low(cur[:, pl.ds(pl.multiple_of(g * BLK, BLK), BLK)])
            high, low = high_low(proj[g])
            p_high[g] = high
            p_low[g] = low
            first = dot_nt(lhs, high)
            vals[g] = first[0:2] + first[2:4] + dot_nt(lhs, low)[0:2]
        return carry

    lax.fori_loop(0, NB // 8, values_of, 0)

    def boxes_of(i, carry):
        for u in range(8):
            g = i * 8 + u
            hot = one_hot_rows(codes[pl.ds(g, 1), :])
            hots[g] = hot
            placed = dot_nt(rows_high_low(vals[g]), hot)
            boxed[pl.ds(g, 1), :] = placed[0:1] + placed[2:3]
            boxed[pl.ds(NB + g, 1), :] = placed[1:2] + placed[3:4]
        return carry

    lax.fori_loop(0, NB // 8, boxes_of, 0)
    b_high, b_low = high_low(boxed[...])
    along_cos = dot(b_high, tch[...]) + dot(b_low, tch[...]) + dot(b_high, tcl[...])
    along_sin = dot(b_high, tsh[...]) + dot(b_low, tsh[...]) + dot(b_high, tsl[...])
    store_twist(corner_x, corner_y, row, col, twist)
    plain_real = along_cos[:NB] + along_sin[NB:]
    plain_imag = along_cos[NB:] - along_sin[:NB]
    real = plain_real * twist[0] - plain_imag * twist[1]
    imag = plain_real * twist[1] + plain_imag * twist[0]
    lane = iota((NB, 64), 1)
    corners = jnp.where(lane == 0, corner_x, jnp.where(lane == 1, corner_y, 0)).astype(F32)
    for c in range(NCOL):
        part = slice(32 * c, 32 * c + 32)
        message = jnp.concatenate([real[:, part], imag[:, part], corners], axis=1)
        out[NB * c : NB * c + NB, :] = message.astype(BF)


def local_x_of_row(shape, dim, band):
    row = iota(shape, dim)
    tile = row - 128
    main = jnp.where(band >= 4, 129 - row, row + 2)
    upper = jnp.where(lax.rem(band + 1, NROW) >= 4, 137 - tile, 130 + tile)
    upper = jnp.where((upper >= 130) & (upper < 132), upper, -64)
    lower = jnp.where(lax.rem(band + NROW - 1, NROW) >= 4, 9 - tile, tile - 14)
    lower = jnp.where((lower >= 0) & (lower < 2), lower, -64)
    return jnp.where(row < 128, main, jnp.where(tile < 8, upper, lower))


def store_starts(recv, starts):
    block = iota((512, 1), 0)
    start = recv[:, 65:66].astype(jnp.int32) + (block // NB) * 64 - 2
    starts[NB : NB + 512, :] = jnp.broadcast_to(start, (512, 128))
    starts[0:NB, :] = starts[512 : 512 + NB, :]
    starts[NB + 512 :, :] = starts[NB : 2 * NB, :]


def chunk_mask(starts, q):
    lane = iota((128, 128), 1)
    cell = 128 * q + lane if q < 4 else 128 * q + 127 - lane
    inside = ((cell - starts[64 * q : 64 * q + 128, :]) & (N - 1)) < 4
    return jnp.where(inside, 1.0, 0.0)


def image_chunk(q, corner, local_x, wides, starts):
    first = 64 * q if q < 4 else 64 * q - 256
    wide = wides[0] if q < 4 else wides[1]
    mask = chunk_mask(starts, q).astype(BF)
    mask = jnp.concatenate([mask] * 4, axis=1)
    offset = local_x - corner[0:1, 64 * q : 64 * q + 128].astype(jnp.int32)
    lhs = [jnp.where(offset == ex, 1.0, 0.0).astype(BF) for ex in range(4)]
    rhs = [wide[first : first + 128, 512 * ex : 512 * ex + 512] * mask for ex in range(4)]
    return dot(jnp.concatenate(lhs, axis=1), jnp.concatenate(rhs, axis=0))


def build_image(recv, band, spreads, padded, wides, starts, odd, even):
    padded[0:NB, :] = recv[512 - NB :, :]
    padded[NB : NB + 512, :] = recv[...]
    padded[NB + 512 :, :] = recv[0:NB, :]

    def spread_lanes(i, carry):
        lanes = pl.ds(pl.multiple_of(i * 512, 512), 512)
        wides[0][:, lanes] = dot(padded[0:320, :], spreads[0][:, lanes]).astype(BF)
        wides[1][:, lanes] = dot(padded[256:576, :], spreads[1][:, lanes]).astype(BF)
        return carry

    lax.fori_loop(0, 4, spread_lanes, 0)
    store_starts(recv, starts)
    pick = jnp.where(iota((16, 128), 1) == 64, 1.0, 0.0).astype(BF)
    corner = dot_nt(pick, recv[...])[0:8]
    corner = jnp.concatenate([corner[:, 480:], corner, corner[:, :NB]], axis=1)
    local_x = local_x_of_row((XR, 128), 0, band)
    for q in range(4):
        ahead = image_chunk(q, corner, local_x, wides, starts)
        backwards = image_chunk(7 - q, corner, local_x, wides, starts)
        minus, plus = (ahead - backwards).astype(BF), (ahead + backwards).astype(BF)
        for kz in range(2):
            for c in range(2):
                p = 2 * c + kz
                place = (kz, slice(XR * c, XR * c + XR), slice(128 * q, 128 * q + 128))
                odd[place] = minus[:, 128 * p : 128 * p + 128]
                even[place] = plus[:, 128 * p : 128 * p + 128]


def forward_y(kz, chip, odd, even, cos, sin, out, slot):
    lanes = pl.ds(pl.multiple_of(chip * 256, 256), 256)
    by_cos = dot(odd[kz], cos[0:512, lanes])
    by_sin = dot(even[kz], sin[0:512, lanes])
    real = (by_cos[:XR] + by_sin[XR:]).astype(BF)
    imag = (by_cos[XR:] - by_sin[:XR]).astype(BF)
    for j in range(2):
        out[kz, slot + j, 0:XR, :] = real[:, 128 * j : 128 * j + 128]
        out[kz, slot + j, XR:, :] = imag[:, 128 * j : 128 * j + 128]


def along_x(kz, recv, green, cos, sin, out, d_one, d_two, h_one, h_two):
    none = jnp.zeros((8, 128), F32)
    for r in range(NROW):
        before, after = (r - 1) % NROW, (r + 1) % NROW
        back = r >= 4
        start = 512 + 128 * (7 - r) if back else 128 * r
        rows = slice(start, start + 128)
        for c in range(2):
            base = XR * c
            main = recv[kz, r, base : base + 128, :]
            upper = recv[kz, before, base + 128 : base + XR, :].astype(F32)[0:8]
            lower = recv[kz, after, base + 128 : base + XR, :].astype(F32)[8:16]
            head, tail = (lower, upper) if back else (upper, lower)
            head = main[0:16].astype(F32) + jnp.concatenate([head, none], axis=0)
            tail = main[112:128].astype(F32) + jnp.concatenate([none, tail], axis=0)
            band = jnp.concatenate([head.astype(BF), main[16:112], tail.astype(BF)], axis=0)
            d_one[rows, 128 * c : 128 * c + 128] = -band if back else band
            d_two[rows, 128 - 128 * c : 256 - 128 * c] = -band if c == 0 else band

    def forward(i, carry):
        rows = pl.ds(pl.multiple_of(i * 256, 256), 256)
        high_rows = pl.ds(pl.multiple_of(i * 256 + 512, 256), 256)
        cos_i, sin_i = cos[rows, 0:512], sin[rows, 0:512]
        by_cos = dot(cos_i, d_one[0:512, :]) + dot(cos_i, d_one[512:, :])
        by_sin = dot(sin_i, d_two[0:512, :]) + dot(sin_i, d_two[512:, :])
        lanes = slice(128 * kz, 128 * kz + 128)
        parts = []
        for spec, where in ((by_sin + by_cos, rows), (by_sin - by_cos, high_rows)):
            real, imag = spec[:, :128], spec[:, 128:]
            g_real, g_imag = green[0, where, lanes], green[1, where, lanes]
            parts.append((real * g_real - imag * g_imag, real * g_imag + imag * g_real))
        (low_real, low_imag), (high_real, high_imag) = parts
        h_one[rows, 0:128] = (low_real - high_real).astype(BF)
        h_one[rows, 128:256] = (low_imag - high_imag).astype(BF)
        h_two[rows, 0:128] = -(low_imag + high_imag).astype(BF)
        h_two[rows, 128:256] = (low_real + high_real).astype(BF)
        return carry

    lax.fori_loop(0, 2, forward, 0)

    def inverse(i, carry):
        rows = pl.ds(pl.multiple_of(i * 256, 256), 256)
        by_cos = dot(cos[rows, 0:512], h_one[...])
        by_sin = dot(sin[rows, 0:512], h_two[...])
        low, high = (by_sin + by_cos).astype(BF), (by_sin - by_cos).astype(BF)
        for j in range(2):
            for c in range(2):
                place = (slice(128 * j, 128 * j + 128), slice(128 * c, 128 * c + 128))
                out[kz, 2 * i + j, XR * c : XR * c + 128, :] = low[place]
                out[kz, 7 - 2 * i - j, XR * c : XR * c + 128, :] = high[place]
        return carry

    lax.fori_loop(0, 2, inverse, 0)
    for r in range(NROW):
        before, after = (r - 1) % NROW, (r + 1) % NROW
        for c in range(2):
            base = XR * c
            above = out[kz, after, base : base + 16, :].astype(F32)[0:8]
            if after >= 4:
                above = out[kz, after, base + 112 : base + 128, :].astype(F32)[8:16]
            below = out[kz, before, base + 112 : base + 128, :].astype(F32)[8:16]
            if before >= 4:
                below = out[kz, before, base : base + 16, :].astype(F32)[0:8]
            out[kz, r, base + 128 : base + XR, :] = jnp.concatenate([above, below], axis=0).astype(BF)


def inverse_y(kz, recv, slots, chips, cos, sin, spec, pot):
    for m, slot in enumerate(slots):
        for j in range(2):
            spec[:, 256 * m + 128 * j : 256 * m + 128 * j + 128] = recv[kz, slot + j]

    def lanes_of(i, carry):
        lanes = pl.ds(pl.multiple_of(i * 256, 256), 256)
        by_cos, by_sin = 0.0, 0.0
        for m, chip in enumerate(chips):
            rows = pl.ds(pl.multiple_of(chip * 256, 256), 256)
            part = spec[:, 256 * m : 256 * m + 256]
            by_cos = by_cos + dot(part, cos[rows, lanes])
            by_sin = by_sin + dot(part, sin[rows, lanes])
        high_lanes = pl.ds(pl.multiple_of(i * 256 + 512, 256), 256)
        pot[0:XR, lanes] = (by_cos[:XR] - by_sin[XR:]).astype(BF)
        pot[XR:, lanes] = (by_cos[XR:] + by_sin[:XR]).astype(BF)
        pot[0:XR, high_lanes] = -(by_cos[:XR] + by_sin[XR:]).astype(BF)
        pot[XR:, high_lanes] = (by_sin[:XR] - by_cos[XR:]).astype(BF)
        return carry

    lax.fori_loop(0, 2, lanes_of, 0)


def build_hot(recv, band, hot):
    local_x = local_x_of_row((512, XR), 1, band)
    offset = local_x - recv[:, 64:65].astype(jnp.int32)
    for ex in range(4):
        hot[ex, NB : NB + 512, :] = jnp.where(offset == ex, 1.0, 0.0).astype(BF)
    hot[:, 0:NB, :] = hot[:, 512 : 512 + NB, :]
    hot[:, NB + 512 :, :] = hot[:, NB : 2 * NB, :]


def pick_cells(kz, pot, starts, hot, accs):
    for q in range(8):
        mask = chunk_mask(starts, q)
        mask = jnp.concatenate([mask] * 2, axis=1)
        lane = 128 * q if q < 4 else 512 + 128 * (7 - q)
        cells = [pot[XR * c : XR * c + XR, lane : lane + 128] for c in range(2)]
        cells = jnp.concatenate(cells, axis=1)
        first = 64 * q if q < 4 else 64 * q - 256
        rows = slice(first, first + 128)
        acc = accs[0] if q < 4 else accs[1]
        for ex in range(4):
            taken = (dot(hot[ex, 64 * q : 64 * q + 128, :], cells) * mask).astype(BF)
            for c in range(2):
                lane = 512 * ex + 256 * c + 128 * kz
                lanes = slice(lane, lane + 128)
                acc[rows, lanes] = acc[rows, lanes] + taken[:, 128 * c : 128 * c + 128]


def clear_cells(accs):
    for acc in accs:
        acc[...] = jnp.zeros_like(acc)


def fold_cells(accs, spreads, out, extra):
    a = dot_nt(accs[0][...], spreads[0][...])
    b = dot_nt(accs[1][...], spreads[1][...])
    pieces = [a[32:64] + b[288:320], a[64:256], a[256:320] + b[0:64], b[64:256], b[256:288] + a[0:32]]
    cells = jnp.concatenate(pieces, axis=0)
    if extra is not None:
        cells = cells + extra[...].astype(F32)
    out[...] = cells.astype(BF)


def back_project(
    recv, near, tch, tcl, tsh, tsl, out, p_high, p_low, hots, box_real, box_imag, vals, twist
):
    real = jnp.concatenate([recv[NB * c : NB * c + NB, 0:32] for c in range(NCOL)], axis=1)
    imag = jnp.concatenate([recv[NB * c : NB * c + NB, 32:64] for c in range(NCOL)], axis=1)
    real, imag = real.astype(F32), imag.astype(F32)
    turned_real = real * twist[0] + imag * twist[1]
    turned_imag = imag * twist[0] - real * twist[1]
    b_high, b_low = high_low(jnp.concatenate([turned_real, turned_imag], axis=0))
    along_cos = dot(b_high, tch[...]) + dot(b_low, tch[...]) + dot(b_high, tcl[...])
    along_sin = dot(b_high, tsh[...]) + dot(b_low, tsh[...]) + dot(b_high, tsl[...])
    box_real[...] = along_cos[:NB] - along_sin[NB:]
    box_imag[...] = along_cos[NB:] + along_sin[:NB]

    def values_of(i, carry):
        for u in range(8):
            g = i * 8 + u
            box = jnp.concatenate([box_real[pl.ds(g, 1), :], box_imag[pl.ds(g, 1), :]], axis=0)
            picked = dot(rows_high_low(box), hots[g])
            vals[g] = picked[0:2] + picked[2:4]
        return carry

    lax.fori_loop(0, NB // 8, values_of, 0)

    def blocks_of(i, carry):
        for u in range(8):
            g = i * 8 + u
            lhs = rows_high_low(vals[g])
            first = dot(lhs, p_high[g])
            far = first[0:2] + first[2:4] + dot(lhs, p_low[g])[0:2]
            row = near[pl.ds(g, 1), :]
            beside = jnp.concatenate([row[:, :BLK], row[:, BLK:]], axis=0)
            out[:, pl.ds(pl.multiple_of(g * BLK, BLK), BLK)] = far + beside
        return carry

    lax.fori_loop(0, NB // 8, blocks_of, 0)


def column_of(row):
    return jnp.transpose(jnp.broadcast_to(row.astype(F32), (8, 128)))[:, 0:1].astype(jnp.int32)


def near_backward(beside, owned, picks, count, matrices, back_a, lv_one, lv_two, spread_back):
    hits = jnp.where(iota((PAIRS, NB), 1) == column_of(owned[...]), 1.0, 0.0).astype(BF)
    local = dot(hits, beside[1, NB : 2 * NB, :])
    real, imag = local[:, :BLK], local[:, BLK:]
    lv_one[...] = jnp.concatenate([real, -imag], axis=1)
    lv_two[...] = jnp.concatenate([imag, real], axis=1)
    first_row = iota((8, 2 * BLK), 0) == 0

    def pairs_of(i, carry):
        for u in range(8):
            p = i * 8 + u
            lhs = jnp.where(first_row, lv_one[pl.ds(p, 1), :], lv_two[pl.ds(p, 1), :]).astype(BF)
            got = dot(lhs, matrices[p])
            back_a[pl.ds(p, 1), :] = jnp.concatenate([got[0:1], got[1:2]], axis=1)
        return carry

    lax.fori_loop(0, PAIRS // 8, pairs_of, 0)
    alive = iota((9 * NB, PAIRS), 1) < count[0]
    hits = (iota((9 * NB, PAIRS), 0) == picks[...]) & alive
    table = jnp.where(hits, 1.0, 0.0).astype(BF)
    high, low = high_low(back_a[...])
    total = (dot(table, high) + dot(table, low)).astype(BF)
    for n in range(9):
        rows = slice(NB * (n // 3), NB * (n // 3) + NB)
        spread_back[n % 3, rows, :] = total[NB * n : NB * n + NB, :]


def near_onward(beside, owned, picks, count, matrices, on_a, on_b, lv_one, near):
    hits = jnp.where(iota((PAIRS, 9 * NB), 1) == column_of(picks[...]), 1.0, 0.0).astype(BF)
    tiles = [beside[n % 3, NB * (n // 3) : NB * (n // 3) + NB, :] for n in range(9)]
    lv_one[...] = dot(hits, jnp.concatenate(tiles, axis=0))
    first_row = iota((8, BLK), 0) == 0

    def pairs_of(i, carry):
        for u in range(8):
            p = i * 8 + u
            row = lv_one[pl.ds(p, 1), :]
            lhs = jnp.where(first_row, row[:, :BLK], row[:, BLK:]).astype(BF)
            got = dot_nt(lhs, matrices[p])
            on_a[pl.ds(p, 1), :] = got[0:1]
            on_b[pl.ds(p, 1), :] = got[1:2]
        return carry

    lax.fori_loop(0, PAIRS // 8, pairs_of, 0)
    real = on_a[:, :BLK] - on_b[:, BLK:]
    imag = on_b[:, :BLK] + on_a[:, BLK:]
    alive = iota((NB, PAIRS), 1) < count[0]
    table = jnp.where((iota((NB, PAIRS), 0) == owned[...]) & alive, 1.0, 0.0).astype(BF)
    high, low = high_low(jnp.concatenate([real, imag], axis=1))
    near[...] = dot(table, high) + dot(table, low)


def turn_green(kz, green, turned):
    turn = jnp.where(iota((128, 128), 0) + iota((128, 128), 1) == 127, 1.0, 0.0).astype(BF)
    for c in range(2):

        def part(i, carry):
            rows = pl.ds(pl.multiple_of(i * 128, 128), 128)
            high_rows = pl.ds(pl.multiple_of(896 - i * 128, 128), 128)
            target = pl.ds(pl.multiple_of(i * 128 + 512, 128), 128)
            lanes = slice(128 * kz, 128 * kz + 128)
            scale = 1.0 / (N * N * NGZ)
            turned[c, rows, lanes] = jnp.transpose(green[c, kz, :, rows]) * scale
            high, low = high_low(green[c, kz, :, high_rows] * scale)
            turned[c, target, lanes] = dot_nt(turn, high) + dot_nt(turn, low)
            return carry

        lax.fori_loop(0, 4, part, 0)


def whole_kernel(
    cur, cells, owned, picks, count, near_hbm, proj_hbm, green_hbm,
    tch_hbm, tcl_hbm, tsh_hbm, tsl_hbm, ahead_hbm, backwards_hbm, cos_hbm, sin_hbm, out,
    matrices, proj, green, tch, tcl, tsh, tsl, ahead, backwards, cos, sin, load_sem, twist,
    codes, p_high, p_low, hots, vals, boxed, box_real, box_imag,
    beside, spread_back, back, kept, edges, edges_in, on_a, on_b, lv_one, lv_two, near, turned,
    padded, wide_a, wide_b, starts, odd, even, hot, acc_a, acc_b, spec, pot, d_one, d_two, h_one, h_two,
    send_a, recv_a, send_b, recv_b, sem_send_a, sem_recv_a, sem_send_b, sem_recv_b,
    send_c, recv_c, send_d, recv_d, sem_send_c, sem_recv_c, sem_send_d, sem_recv_d,
    sem_send_h, sem_recv_h, sem_send_r, sem_recv_r,
    far_c, far_starts, far_hot, far_a, recv_f, send_q, recv_q, sem_far,
):
    row, col = lax.axis_index("row"), lax.axis_index("col")
    mesh_ids = pl.DeviceIdType.MESH

    def row_peer(j):
        return (lax.rem(row + j, NROW), col)

    def col_peer(j):
        return (row, lax.rem(col + j, NCOL))

    def beside_peer(dim, step):
        if dim == 0:
            return (lax.rem(row + step + NROW, NROW), col)
        return (row, lax.rem(col + step + NCOL, NCOL))

    barrier = pltpu.get_barrier_semaphore()
    peers = [row_peer(j) for j in range(1, NROW)] + [col_peer(j) for j in range(1, NCOL)]
    for peer in peers:
        pl.semaphore_signal(barrier, inc=1, device_id=peer, device_id_type=mesh_ids)

    pairs = [
        (proj_hbm, proj), (tch_hbm, tch), (tcl_hbm, tcl), (tsh_hbm, tsh), (tsl_hbm, tsl),
        (near_hbm, matrices), (ahead_hbm, ahead), (backwards_hbm, backwards), (cos_hbm, cos),
        (sin_hbm, sin), (green_hbm, green),
    ]
    loads = [pltpu.make_async_copy(a, b, load_sem.at[i]) for i, (a, b) in enumerate(pairs)]
    for load in loads[:5]:
        load.start()

    def remote(source, target, sem_send, sem_recv, peer):
        return pltpu.make_async_remote_copy(
            src_ref=source,
            dst_ref=target,
            send_sem=sem_send,
            recv_sem=sem_recv,
            device_id=peer,
            device_id_type=mesh_ids,
        )

    z, core = row // 2, lax.rem(row, 2)
    sibling = 2 * z + 1 - core
    far, far_sibling = lax.rem(row + 4, NROW), lax.rem(sibling + 4, NROW)
    chips = [lax.rem(z + 1, 4), lax.rem(z + 3, 4)]

    def row_copy(kz, source, target, sems, j, peer):
        return remote(source, target, sems[0].at[kz, j], sems[1].at[kz, j], (peer, col))

    def tile_rows(c):
        return pl.ds(pl.multiple_of(c * NB, NB), NB)

    def col_copies(source, target, sem_send, sem_recv):
        return [
            remote(
                source.at[tile_rows(col_peer(j)[1])],
                target.at[tile_rows(col)],
                sem_send.at[j],
                sem_recv.at[j],
                col_peer(j),
            )
            for j in range(1, NCOL)
        ]

    for g in range(NB):
        two = cur[:, BLK * g : BLK * g + BLK]
        vals[g] = two
    rounded = jnp.concatenate([vals[:, 0, :], vals[:, 1, :]], axis=1).astype(BF)
    beside[1, NB : 2 * NB, :] = rounded
    for load in loads[:5]:
        load.wait()
    for load in loads[5:]:
        load.start()
    spreads, wides, accs = (ahead, backwards), (wide_a, wide_b), (acc_a, acc_b)
    project(
        cur, proj, cells, tch, tcl, tsh, tsl, send_c, codes, p_high, p_low, hots, vals, boxed,
        row, col, twist,
    )
    pl.semaphore_wait(barrier, len(peers))
    third = col_copies(send_c, recv_c, sem_send_c, sem_recv_c)
    for copy in third:
        copy.start()
    middle = pl.ds(NB, NB)
    halo = [
        remote(
            beside.at[1, middle],
            beside.at[1, pl.ds(NB * place, NB)],
            sem_send_h.at[place],
            sem_recv_h.at[place],
            beside_peer(0, step),
        )
        for step, place in ((1, 0), (-1, 2))
    ]
    for copy in halo:
        copy.start()
    recv_c[tile_rows(col), :] = send_c[tile_rows(col), :]
    loads[5].wait()
    near_backward(beside, owned, picks, count, matrices, on_a, lv_one, lv_two, spread_back)
    for copy in halo:
        copy.wait_recv()
    wide_halo = [
        remote(
            beside.at[1], beside.at[place], sem_send_h.at[3 + place], sem_recv_h.at[3 + place],
            beside_peer(1, step),
        )
        for step, place in ((1, 0), (-1, 2))
    ]
    returns = [
        remote(
            spread_back.at[place], back.at[place], sem_send_r.at[place], sem_recv_r.at[place],
            beside_peer(1, step),
        )
        for step, place in ((-1, 0), (1, 2))
    ]
    for copy in returns + wide_halo:
        copy.start()
    for load in loads[6:]:
        load.wait()
    for copy in third:
        copy.wait_recv()
    over = remote(recv_c, far_c, sem_far.at[0], sem_far.at[1], (far, col))
    over.start()
    build_image(recv_c, row, spreads, padded, wides, starts, odd, even)
    sems_a, sems_b = (sem_send_a, sem_recv_a), (sem_send_b, sem_recv_b)
    first, second, beyond = [[], []], [[], []], [[], []]
    for kz in range(2):
        for m in range(2):
            forward_y(kz, chips[m], odd, even, cos, sin, send_a, 2 * chips[m])
            for j in range(2):
                peer = 2 * chips[m] + lax.rem(core + j, 2)
                copy = row_copy(
                    kz, send_a.at[kz, peer], recv_a.at[kz, row], sems_a, 2 * m + j, peer
                )
                copy.start()
                first[kz].append(copy)
    for kz in range(2):
        forward_y(kz, z, odd, even, cos, sin, send_a, 2 * z)
        copy = row_copy(kz, send_a.at[kz, sibling], recv_a.at[kz, row], sems_a, 4, sibling)
        copy.start()
        first[kz].append(copy)
        recv_a[kz, row] = send_a[kz, row]
    over.wait_recv()
    build_image(far_c, far, spreads, padded, wides, far_starts, odd, even)
    for kz in range(2):
        forward_y(kz, z, odd, even, cos, sin, far_a, 0)
        copy = row_copy(kz, far_a.at[kz, 1 - core], recv_a.at[kz, far], sems_a, 5, sibling)
        copy.start()
        first[kz].append(copy)
        recv_a[kz, far] = far_a[kz, core]
    for copy in returns:
        copy.wait_recv()
    column = spread_back[1].astype(F32) + back[0].astype(F32) + back[2].astype(F32)
    kept[...] = column[NB : 2 * NB]
    edges[0] = column[:NB].astype(BF)
    edges[1] = column[2 * NB :].astype(BF)
    edge_copies = [
        remote(
            edges.at[place], edges_in.at[place], sem_send_r.at[3 + place], sem_recv_r.at[3 + place],
            beside_peer(0, step),
        )
        for step, place in ((-1, 0), (1, 1))
    ]
    for copy in edge_copies:
        copy.start()
    build_hot(recv_c, row, hot)
    build_hot(far_c, far, far_hot)
    clear_cells(accs)
    for kz in range(2):
        turn_green(kz, green, turned)
        for copy in first[kz]:
            copy.wait_recv()
        along_x(kz, recv_a, turned, cos, sin, send_b, d_one, d_two, h_one, h_two)
        targets = [2 * chip + lax.rem(core + j, 2) for chip in chips for j in range(2)]
        targets.append(sibling)
        for j, peer in enumerate(targets):
            copy = row_copy(kz, send_b.at[kz, peer], recv_b.at[kz, row], sems_b, j, peer)
            copy.start()
            second[kz].append(copy)
        copy = row_copy(kz, send_b.at[kz, far_sibling], recv_f.at[kz, core], sems_b, 5, sibling)
        copy.start()
        beyond[kz].append(copy)
        recv_b[kz, row] = send_b[kz, row]
        recv_f[kz, core] = send_b[kz, far]
    for kz in range(2):
        beyond[kz][0].wait_recv()
        inverse_y(kz, recv_f, [0], [z], cos, sin, spec, pot)
        pick_cells(kz, pot, far_starts, far_hot, accs)
    fold_cells(accs, spreads, send_q, None)
    home = remote(send_q, recv_q, sem_far.at[2], sem_far.at[3], (far, col))
    home.start()
    clear_cells(accs)
    held = [z] + chips
    for kz in range(2):
        for copy in second[kz]:
            copy.wait_recv()
        inverse_y(kz, recv_b, [2 * chip for chip in held], held, cos, sin, spec, pot)
        pick_cells(kz, pot, starts, hot, accs)
    home.wait_recv()
    fold_cells(accs, spreads, send_d, recv_q)
    fourth = col_copies(send_d, recv_d, sem_send_d, sem_recv_d)
    for copy in fourth:
        copy.start()
    recv_d[tile_rows(col), :] = send_d[tile_rows(col), :]
    for copy in wide_halo:
        copy.wait_recv()
    near_onward(beside, owned, picks, count, matrices, on_a, on_b, lv_one, near)
    for copy in edge_copies:
        copy.wait_recv()
    edge_sum = edges_in[0].astype(F32) + edges_in[1].astype(F32)
    near[...] = near[...] + kept[...] + edge_sum
    for copy in fourth:
        copy.wait_recv()
    back_project(
        recv_d, near, tch, tcl, tsh, tsl, out, p_high, p_low, hots, box_real, box_imag, vals, twist
    )
    for kz in range(2):
        for copy in first[kz] + second[kz] + beyond[kz]:
            copy.wait_send()
    for copy in third + fourth + halo + wide_halo + returns + edge_copies + [over, home]:
        copy.wait_send()


def per_device(
    currents, near_blocks, pair_local, pair_ghost, pair_counts, projection, stencil_cells, green
):
    tables = [jnp.asarray(t) for t in depth_tables()]
    tables += [jnp.asarray(t) for t in spread_tables()]
    tables += [jnp.asarray(t) for t in grid_tables()]
    vmem, dma = pltpu.VMEM, pltpu.SemaphoreType.DMA
    grid_part = (2, NROW, 2 * XR, 128)
    wrapped = 512 + 2 * NB
    scratch = [
        vmem((PAIRS, 2 * BLK, BLK), BF),
        vmem((NB, BLK, BLK), F32),
        vmem((2, 2, 128, N), F32),
        *[vmem((512, 512), BF)] * 4,
        *[vmem((128, 2048), BF)] * 2,
        *[vmem((N, N), BF)] * 2,
        dma((11,)),
        vmem((2, NB, 512), F32),
        vmem((NB, BLK), jnp.int32),
        *[vmem((NB, BLK, BLK), BF)] * 2,
        vmem((NB, 512, BLK), BF),
        vmem((NB, 2, BLK), F32),
        vmem((2 * NB, 512), F32),
        *[vmem((NB, 512), F32)] * 2,
        *[vmem((3, 3 * NB, 2 * BLK), BF)] * 3,
        vmem((NB, 2 * BLK), F32),
        *[vmem((2, NB, 2 * BLK), BF)] * 2,
        *[vmem((PAIRS, 2 * BLK), F32)] * 4,
        vmem((NB, 2 * BLK), F32),
        vmem((2, N, 256), F32),
        vmem((wrapped, 128), BF),
        *[vmem((320, 2048), BF)] * 2,
        vmem((wrapped, 128), jnp.int32),
        *[vmem((2, 2 * XR, 512), BF)] * 2,
        vmem((4, wrapped, XR), BF),
        *[vmem((320, 2048), BF)] * 2,
        *[vmem((2 * XR, N), BF)] * 2,
        *[vmem((N, 256), BF)] * 2,
        *[vmem((512, 256), BF)] * 2,
        *[vmem(grid_part, BF)] * 4,
        *[dma((2, NROW))] * 4,
        *[vmem((NCOL * NB, 128), BF)] * 4,
        *[dma((NCOL,))] * 4,
        *[dma((9,))] * 4,
        vmem((NCOL * NB, 128), BF),
        vmem((wrapped, 128), jnp.int32),
        vmem((4, wrapped, XR), BF),
        *[vmem((2, 2, 2 * XR, 128), BF)] * 2,
        *[vmem((NCOL * NB, 128), BF)] * 2,
        dma((4,)),
    ]
    in_vmem = pl.BlockSpec(memory_space=pltpu.VMEM)
    in_smem = pl.BlockSpec(memory_space=pltpu.SMEM)
    anywhere = pl.BlockSpec(memory_space=pl.ANY)
    return pl.pallas_call(
        whole_kernel,
        out_shape=jax.ShapeDtypeStruct((2, NB * BLK), F32),
        in_specs=[in_vmem] * 4 + [in_smem] + [anywhere] * 11,
        out_specs=in_vmem,
        scratch_shapes=scratch,
        compiler_params=pltpu.CompilerParams(
            vmem_limit_bytes=VMEM_LIMIT, collective_id=1, has_side_effects=True
        ),
    )(
        currents,
        stencil_cells,
        pair_local,
        pair_ghost,
        pair_counts,
        near_blocks.reshape(PAIRS, 2 * BLK, BLK),
        projection,
        green,
        *tables,
    )


def solution(mesh):
    in_specs = (
        P(None, ("row", "col")),
        P(("row", "col"), None, None, None),
        P(("row", "col"), None),
        P(("row", "col"), None),
        P(("row", "col")),
        P(("row", "col"), None, None),
        P(("row", "col"), None),
        P(None, "col", "row", None),
    )
    out_specs = P(None, ("row", "col"))
    return jax.shard_map(
        per_device, mesh=mesh, in_specs=in_specs, out_specs=out_specs, check_vma=False
    )
```

```python
import math

import jax
import jax.numpy as jnp
import ml_dtypes
import numpy as np
from jax import lax
from jax.experimental import pallas as pl
from jax.experimental.pallas import tpu as pltpu
from jax.sharding import PartitionSpec as P

N = 1024
NGZ = 32
NROW = 8
NCOL = 16
NB = 32
BLK = 128
PAIRS = 128
XR = 144
WIDE_Y = 68
BF = jnp.bfloat16
F32 = jnp.float32
VMEM_LIMIT = 60 * 1024 * 1024


def bf(a):
    return np.asarray(a, dtype=np.float64).astype(ml_dtypes.bfloat16)


def split_np(a):
    high = bf(a)
    return high, bf(a - high.astype(np.float64))


def grid_tables():
    odd = 2 * np.arange(N) + 1
    angle = (odd[:, None] * odd[None, :] % (4 * N)) * (math.pi / (2 * N))
    return bf(np.cos(angle)), bf(np.sin(angle))


def depth_tables():
    index = np.arange(NGZ)[:, None] * np.arange(NGZ)[None, :] % NGZ
    angle = index * (2.0 * math.pi / NGZ)
    eye = np.eye(16)
    cos_high, cos_low = split_np(np.kron(np.cos(angle), eye))
    sin_high, sin_low = split_np(np.kron(np.sin(angle), eye))
    return cos_high, cos_low, sin_high, sin_low


def spread_tables():
    lane = np.arange(128)[:, None]
    plane, ex, b = lane // 16, lane // 4 % 4, lane % 4
    wide = np.arange(2048)[None, :]
    hits = (wide // 512 == ex) & (wide // 128 % 4 == plane) & (lane < 64)
    ahead = hits & ((wide + 2) % 4 == b)
    backwards = hits & ((wide + 2) % 4 == 3 - b)
    return bf(ahead.astype(np.float64)), bf(backwards.astype(np.float64))


def dot(a, b):
    return jnp.dot(a, b, preferred_element_type=F32)


def dot_nt(a, b):
    return lax.dot_general(a, b, (((1,), (1,)), ((), ())), preferred_element_type=F32)


def iota(shape, dim):
    return lax.broadcasted_iota(jnp.int32, shape, dim)


def high_low(a):
    high = a.astype(BF)
    return high, (a - high.astype(F32)).astype(BF)


def rows_high_low(a):
    high = a.astype(BF).astype(F32)
    return jnp.concatenate([high, a - high], axis=0).astype(BF)


def cell_codes(cells):
    z = cells & (NGZ - 1)
    t = cells >> 5
    x = (t * 15421) >> 20
    y = t - x * WIDE_Y
    corner_x = jnp.min(x, axis=1, keepdims=True)
    corner_y = jnp.min(y, axis=1, keepdims=True)
    code = z * 16 + (x - corner_x) * 4 + (y & 3)
    return code, corner_x, corner_y


def one_hot_rows(code_row):
    return jnp.where(iota((512, 128), 0) == code_row, 1.0, 0.0).astype(BF)


def store_twist(corner_x, corner_y, row, col, twist):
    lane = iota((NB, 128), 1)
    x = (corner_x + ((lane >> 2) & 3) + 128 * row - 2) & (N - 1)
    y = (corner_y + ((lane - corner_y) & 3) + 64 * col - 2) & (N - 1)
    angle = (x + y).astype(F32) * (math.pi / N)
    twist[0] = jnp.concatenate([jnp.cos(angle)] * 4, axis=1)
    twist[1] = jnp.concatenate([jnp.sin(angle)] * 4, axis=1)


def project(
    cur, proj, cells, tch, tcl, tsh, tsl, out, codes, p_high, p_low, hots, vals, boxed, row, col, twist
):
    code, corner_x, corner_y = cell_codes(cells[...])
    codes[...] = code

    def values_of(i, carry):
        for u in range(8):
            g = i * 8 + u
            lhs = rows_high_low(cur[:, pl.ds(pl.multiple_of(g * BLK, BLK), BLK)])
            high, low = high_low(proj[g])
            p_high[g] = high
            p_low[g] = low
            first = dot_nt(lhs, high)
            vals[g] = first[0:2] + first[2:4] + dot_nt(lhs, low)[0:2]
        return carry

    lax.fori_loop(0, NB // 8, values_of, 0)

    def boxes_of(i, carry):
        for u in range(8):
            g = i * 8 + u
            hot = one_hot_rows(codes[pl.ds(g, 1), :])
            hots[g] = hot
            placed = dot_nt(rows_high_low(vals[g]), hot)
            boxed[pl.ds(g, 1), :] = placed[0:1] + placed[2:3]
            boxed[pl.ds(NB + g, 1), :] = placed[1:2] + placed[3:4]
        return carry

    lax.fori_loop(0, NB // 8, boxes_of, 0)
    b_high, b_low = high_low(boxed[...])
    both_parts = jnp.concatenate([b_high, b_low], axis=0)
    by_cos, by_sin = dot(both_parts, tch[...]), dot(both_parts, tsh[...])
    along_cos = by_cos[: 2 * NB] + by_cos[2 * NB :] + dot(b_high, tcl[...])
    along_sin = by_sin[: 2 * NB] + by_sin[2 * NB :] + dot(b_high, tsl[...])
    store_twist(corner_x, corner_y, row, col, twist)
    plain_real = along_cos[:NB] + along_sin[NB:]
    plain_imag = along_cos[NB:] - along_sin[:NB]
    real = plain_real * twist[0] - plain_imag * twist[1]
    imag = plain_real * twist[1] + plain_imag * twist[0]
    lane = iota((NB, 64), 1)
    corners = jnp.where(lane == 0, corner_x, jnp.where(lane == 1, corner_y, 0)).astype(F32)
    for c in range(NCOL):
        part = slice(32 * c, 32 * c + 32)
        message = jnp.concatenate([real[:, part], imag[:, part], corners], axis=1)
        out[NB * c : NB * c + NB, :] = message.astype(BF)


def local_x_of_row(shape, dim, band):
    row = iota(shape, dim)
    tile = row - 128
    main = jnp.where(band >= 4, 129 - row, row + 2)
    upper = jnp.where(lax.rem(band + 1, NROW) >= 4, 137 - tile, 130 + tile)
    upper = jnp.where((upper >= 130) & (upper < 132), upper, -64)
    lower = jnp.where(lax.rem(band + NROW - 1, NROW) >= 4, 9 - tile, tile - 14)
    lower = jnp.where((lower >= 0) & (lower < 2), lower, -64)
    return jnp.where(row < 128, main, jnp.where(tile < 8, upper, lower))


def store_starts(recv, starts):
    block = iota((512, 1), 0)
    start = recv[:, 65:66].astype(jnp.int32) + (block // NB) * 64 - 2
    starts[NB : NB + 512, :] = jnp.broadcast_to(start, (512, 128))
    starts[0:NB, :] = starts[512 : 512 + NB, :]
    starts[NB + 512 :, :] = starts[NB : 2 * NB, :]


def chunk_mask(starts, q):
    lane = iota((128, 128), 1)
    cell = 128 * q + lane if q < 4 else 128 * q + 127 - lane
    inside = ((cell - starts[64 * q : 64 * q + 128, :]) & (N - 1)) < 4
    return jnp.where(inside, 1.0, 0.0)


def image_chunk(q, corner, local_x, wides, starts):
    first = 64 * q if q < 4 else 64 * q - 256
    wide = wides[0] if q < 4 else wides[1]
    mask = chunk_mask(starts, q).astype(BF)
    mask = jnp.concatenate([mask] * 4, axis=1)
    offset = local_x - corner[0:1, 64 * q : 64 * q + 128].astype(jnp.int32)
    lhs = [jnp.where(offset == ex, 1.0, 0.0).astype(BF) for ex in range(4)]
    rhs = [wide[first : first + 128, 512 * ex : 512 * ex + 512] * mask for ex in range(4)]
    return dot(jnp.concatenate(lhs, axis=1), jnp.concatenate(rhs, axis=0))


def build_image(recv, band, spreads, padded, wides, starts, odd, even):
    padded[0:NB, :] = recv[512 - NB :, :]
    padded[NB : NB + 512, :] = recv[...]
    padded[NB + 512 :, :] = recv[0:NB, :]

    def spread_lanes(i, carry):
        lanes = pl.ds(pl.multiple_of(i * 512, 512), 512)
        wides[0][:, lanes] = dot(padded[0:320, :], spreads[0][:, lanes]).astype(BF)
        wides[1][:, lanes] = dot(padded[256:576, :], spreads[1][:, lanes]).astype(BF)
        return carry

    lax.fori_loop(0, 4, spread_lanes, 0)
    store_starts(recv, starts)
    pick = jnp.where(iota((16, 128), 1) == 64, 1.0, 0.0).astype(BF)
    corner = dot_nt(pick, recv[...])[0:8]
    corner = jnp.concatenate([corner[:, 480:], corner, corner[:, :NB]], axis=1)
    local_x = local_x_of_row((XR, 128), 0, band)
    for q in range(4):
        ahead = image_chunk(q, corner, local_x, wides, starts)
        backwards = image_chunk(7 - q, corner, local_x, wides, starts)
        minus, plus = (ahead - backwards).astype(BF), (ahead + backwards).astype(BF)
        for kz in range(2):
            for c in range(2):
                p = 2 * c + kz
                place = (kz, slice(XR * c, XR * c + XR), slice(128 * q, 128 * q + 128))
                odd[place] = minus[:, 128 * p : 128 * p + 128]
                even[place] = plus[:, 128 * p : 128 * p + 128]


def forward_y(kz, chip, odd, even, cos, sin, out, slot):
    lanes = pl.ds(pl.multiple_of(chip * 256, 256), 256)
    by_cos = dot(odd[kz], cos[0:512, lanes])
    by_sin = dot(even[kz], sin[0:512, lanes])
    real = (by_cos[:XR] + by_sin[XR:]).astype(BF)
    imag = (by_cos[XR:] - by_sin[:XR]).astype(BF)
    for j in range(2):
        out[kz, slot + j, 0:XR, :] = real[:, 128 * j : 128 * j + 128]
        out[kz, slot + j, XR:, :] = imag[:, 128 * j : 128 * j + 128]


def along_x(kz, recv, green, cos, sin, out, d_one, d_two, h_one, h_two):
    none = jnp.zeros((8, 128), F32)
    for r in range(NROW):
        before, after = (r - 1) % NROW, (r + 1) % NROW
        back = r >= 4
        start = 512 + 128 * (7 - r) if back else 128 * r
        rows = slice(start, start + 128)
        for c in range(2):
            base = XR * c
            main = recv[kz, r, base : base + 128, :]
            upper = recv[kz, before, base + 128 : base + XR, :].astype(F32)[0:8]
            lower = recv[kz, after, base + 128 : base + XR, :].astype(F32)[8:16]
            head, tail = (lower, upper) if back else (upper, lower)
            head = main[0:16].astype(F32) + jnp.concatenate([head, none], axis=0)
            tail = main[112:128].astype(F32) + jnp.concatenate([none, tail], axis=0)
            band = jnp.concatenate([head.astype(BF), main[16:112], tail.astype(BF)], axis=0)
            d_one[rows, 128 * c : 128 * c + 128] = -band if back else band
            d_two[rows, 128 - 128 * c : 256 - 128 * c] = -band if c == 0 else band

    def forward(i, carry):
        rows = pl.ds(pl.multiple_of(i * 256, 256), 256)
        high_rows = pl.ds(pl.multiple_of(i * 256 + 512, 256), 256)
        cos_i, sin_i = cos[rows, 0:512], sin[rows, 0:512]
        by_cos = dot(cos_i, d_one[0:512, :]) + dot(cos_i, d_one[512:, :])
        by_sin = dot(sin_i, d_two[0:512, :]) + dot(sin_i, d_two[512:, :])
        lanes = slice(128 * kz, 128 * kz + 128)
        parts = []
        for spec, where in ((by_sin + by_cos, rows), (by_sin - by_cos, high_rows)):
            real, imag = spec[:, :128], spec[:, 128:]
            g_real, g_imag = green[0, where, lanes], green[1, where, lanes]
            parts.append((real * g_real - imag * g_imag, real * g_imag + imag * g_real))
        (low_real, low_imag), (high_real, high_imag) = parts
        h_one[rows, 0:128] = (low_real - high_real).astype(BF)
        h_one[rows, 128:256] = (low_imag - high_imag).astype(BF)
        h_two[rows, 0:128] = -(low_imag + high_imag).astype(BF)
        h_two[rows, 128:256] = (low_real + high_real).astype(BF)
        return carry

    lax.fori_loop(0, 2, forward, 0)

    def inverse(i, carry):
        rows = pl.ds(pl.multiple_of(i * 256, 256), 256)
        by_cos = dot(cos[rows, 0:512], h_one[...])
        by_sin = dot(sin[rows, 0:512], h_two[...])
        low, high = (by_sin + by_cos).astype(BF), (by_sin - by_cos).astype(BF)
        for j in range(2):
            for c in range(2):
                place = (slice(128 * j, 128 * j + 128), slice(128 * c, 128 * c + 128))
                out[kz, 2 * i + j, XR * c : XR * c + 128, :] = low[place]
                out[kz, 7 - 2 * i - j, XR * c : XR * c + 128, :] = high[place]
        return carry

    lax.fori_loop(0, 2, inverse, 0)
    for r in range(NROW):
        before, after = (r - 1) % NROW, (r + 1) % NROW
        for c in range(2):
            base = XR * c
            above = out[kz, after, base : base + 16, :].astype(F32)[0:8]
            if after >= 4:
                above = out[kz, after, base + 112 : base + 128, :].astype(F32)[8:16]
            below = out[kz, before, base + 112 : base + 128, :].astype(F32)[8:16]
            if before >= 4:
                below = out[kz, before, base : base + 16, :].astype(F32)[0:8]
            out[kz, r, base + 128 : base + XR, :] = jnp.concatenate([above, below], axis=0).astype(BF)


def inverse_y(kz, recv, slots, chips, cos, sin, spec, pot):
    for m, slot in enumerate(slots):
        for j in range(2):
            spec[:, 256 * m + 128 * j : 256 * m + 128 * j + 128] = recv[kz, slot + j]

    def lanes_of(i, carry):
        lanes = pl.ds(pl.multiple_of(i * 256, 256), 256)
        by_cos, by_sin = 0.0, 0.0
        for m, chip in enumerate(chips):
            rows = pl.ds(pl.multiple_of(chip * 256, 256), 256)
            part = spec[:, 256 * m : 256 * m + 256]
            by_cos = by_cos + dot(part, cos[rows, lanes])
            by_sin = by_sin + dot(part, sin[rows, lanes])
        high_lanes = pl.ds(pl.multiple_of(i * 256 + 512, 256), 256)
        pot[0:XR, lanes] = (by_cos[:XR] - by_sin[XR:]).astype(BF)
        pot[XR:, lanes] = (by_cos[XR:] + by_sin[:XR]).astype(BF)
        pot[0:XR, high_lanes] = -(by_cos[:XR] + by_sin[XR:]).astype(BF)
        pot[XR:, high_lanes] = (by_sin[:XR] - by_cos[XR:]).astype(BF)
        return carry

    lax.fori_loop(0, 2, lanes_of, 0)


def build_hot(recv, band, hot):
    local_x = local_x_of_row((512, XR), 1, band)
    offset = local_x - recv[:, 64:65].astype(jnp.int32)
    for ex in range(4):
        hot[ex, NB : NB + 512, :] = jnp.where(offset == ex, 1.0, 0.0).astype(BF)
    hot[:, 0:NB, :] = hot[:, 512 : 512 + NB, :]
    hot[:, NB + 512 :, :] = hot[:, NB : 2 * NB, :]


def pick_cells(kz, pot, starts, hot, accs):
    for q in range(8):
        mask = chunk_mask(starts, q)
        mask = jnp.concatenate([mask] * 2, axis=1)
        lane = 128 * q if q < 4 else 512 + 128 * (7 - q)
        cells = [pot[XR * c : XR * c + XR, lane : lane + 128] for c in range(2)]
        cells = jnp.concatenate(cells, axis=1)
        first = 64 * q if q < 4 else 64 * q - 256
        rows = slice(first, first + 128)
        acc = accs[0] if q < 4 else accs[1]
        for ex in range(4):
            taken = (dot(hot[ex, 64 * q : 64 * q + 128, :], cells) * mask).astype(BF)
            for c in range(2):
                lane = 512 * ex + 256 * c + 128 * kz
                lanes = slice(lane, lane + 128)
                acc[rows, lanes] = acc[rows, lanes] + taken[:, 128 * c : 128 * c + 128]


def clear_cells(accs):
    for acc in accs:
        acc[...] = jnp.zeros_like(acc)


def fold_cells(accs, spreads, out, extra):
    a = dot_nt(accs[0][...], spreads[0][...])
    b = dot_nt(accs[1][...], spreads[1][...])
    pieces = [a[32:64] + b[288:320], a[64:256], a[256:320] + b[0:64], b[64:256], b[256:288] + a[0:32]]
    cells = jnp.concatenate(pieces, axis=0)
    if extra is not None:
        halves = [unpack_half(extra, 0), unpack_half(extra, 1)]
        cells = cells + jnp.concatenate(halves, axis=0)
    out[...] = cells.astype(BF)


def back_project(
    recv, near, tch, tcl, tsh, tsl, out, p_high, p_low, hots, box_real, box_imag, vals, twist
):
    real = jnp.concatenate([recv[NB * c : NB * c + NB, 0:32] for c in range(NCOL)], axis=1)
    imag = jnp.concatenate([recv[NB * c : NB * c + NB, 32:64] for c in range(NCOL)], axis=1)
    real, imag = real.astype(F32), imag.astype(F32)
    turned_real = real * twist[0] + imag * twist[1]
    turned_imag = imag * twist[0] - real * twist[1]
    b_high, b_low = high_low(jnp.concatenate([turned_real, turned_imag], axis=0))
    both_parts = jnp.concatenate([b_high, b_low], axis=0)
    by_cos, by_sin = dot(both_parts, tch[...]), dot(both_parts, tsh[...])
    along_cos = by_cos[: 2 * NB] + by_cos[2 * NB :] + dot(b_high, tcl[...])
    along_sin = by_sin[: 2 * NB] + by_sin[2 * NB :] + dot(b_high, tsl[...])
    box_real[...] = along_cos[:NB] - along_sin[NB:]
    box_imag[...] = along_cos[NB:] + along_sin[:NB]

    def values_of(i, carry):
        for u in range(8):
            g = i * 8 + u
            box = jnp.concatenate([box_real[pl.ds(g, 1), :], box_imag[pl.ds(g, 1), :]], axis=0)
            picked = dot(rows_high_low(box), hots[g])
            vals[g] = picked[0:2] + picked[2:4]
        return carry

    lax.fori_loop(0, NB // 8, values_of, 0)

    def blocks_of(i, carry):
        for u in range(8):
            g = i * 8 + u
            lhs = rows_high_low(vals[g])
            first = dot(lhs, p_high[g])
            far = first[0:2] + first[2:4] + dot(lhs, p_low[g])[0:2]
            row = near[pl.ds(g, 1), :]
            beside = jnp.concatenate([row[:, :BLK], row[:, BLK:]], axis=0)
            out[:, pl.ds(pl.multiple_of(g * BLK, BLK), BLK)] = far + beside
        return carry

    lax.fori_loop(0, NB // 8, blocks_of, 0)


def column_of(row):
    return jnp.transpose(jnp.broadcast_to(row.astype(F32), (8, 128)))[:, 0:1].astype(jnp.int32)


def near_backward(beside, owned, picks, count, matrices, back_a, lv_one, lv_two, spread_back):
    hits = jnp.where(iota((PAIRS, NB), 1) == column_of(owned[...]), 1.0, 0.0).astype(BF)
    local = dot(hits, beside[1, NB : 2 * NB, :])
    real, imag = local[:, :BLK], local[:, BLK:]
    lv_one[...] = jnp.concatenate([real, -imag], axis=1)
    lv_two[...] = jnp.concatenate([imag, real], axis=1)
    first_row = iota((8, 2 * BLK), 0) == 0

    def pairs_of(i, carry):
        for u in range(8):
            p = i * 8 + u
            lhs = jnp.where(first_row, lv_one[pl.ds(p, 1), :], lv_two[pl.ds(p, 1), :]).astype(BF)
            got = dot(lhs, matrices[p])
            back_a[pl.ds(p, 1), :] = jnp.concatenate([got[0:1], got[1:2]], axis=1)
        return carry

    lax.fori_loop(0, PAIRS // 8, pairs_of, 0)
    alive = iota((9 * NB, PAIRS), 1) < count[0]
    hits = (iota((9 * NB, PAIRS), 0) == picks[...]) & alive
    table = jnp.where(hits, 1.0, 0.0).astype(BF)
    high, low = high_low(back_a[...])
    total = (dot(table, high) + dot(table, low)).astype(BF)
    for n in range(9):
        rows = slice(NB * (n // 3), NB * (n // 3) + NB)
        spread_back[n % 3, rows, :] = total[NB * n : NB * n + NB, :]


def near_onward(beside, owned, picks, count, matrices, on_a, on_b, lv_one, near):
    hits = jnp.where(iota((PAIRS, 9 * NB), 1) == column_of(picks[...]), 1.0, 0.0).astype(BF)
    tiles = [beside[n % 3, NB * (n // 3) : NB * (n // 3) + NB, :] for n in range(9)]
    lv_one[...] = dot(hits, jnp.concatenate(tiles, axis=0))
    first_row = iota((8, BLK), 0) == 0

    def pairs_of(i, carry):
        for u in range(8):
            p = i * 8 + u
            row = lv_one[pl.ds(p, 1), :]
            lhs = jnp.where(first_row, row[:, :BLK], row[:, BLK:]).astype(BF)
            got = dot_nt(lhs, matrices[p])
            on_a[pl.ds(p, 1), :] = got[0:1]
            on_b[pl.ds(p, 1), :] = got[1:2]
        return carry

    lax.fori_loop(0, PAIRS // 8, pairs_of, 0)
    real = on_a[:, :BLK] - on_b[:, BLK:]
    imag = on_b[:, :BLK] + on_a[:, BLK:]
    alive = iota((NB, PAIRS), 1) < count[0]
    table = jnp.where((iota((NB, PAIRS), 0) == owned[...]) & alive, 1.0, 0.0).astype(BF)
    high, low = high_low(jnp.concatenate([real, imag], axis=1))
    near[...] = dot(table, high) + dot(table, low)


def turn_green(kz, green, turned):
    turn = jnp.where(iota((128, 128), 0) + iota((128, 128), 1) == 127, 1.0, 0.0).astype(BF)
    for c in range(2):

        def part(i, carry):
            rows = pl.ds(pl.multiple_of(i * 128, 128), 128)
            high_rows = pl.ds(pl.multiple_of(896 - i * 128, 128), 128)
            target = pl.ds(pl.multiple_of(i * 128 + 512, 128), 128)
            lanes = slice(128 * kz, 128 * kz + 128)
            scale = 1.0 / (N * N * NGZ)
            turned[c, rows, lanes] = jnp.transpose(green[c, kz, :, rows]) * scale
            high, low = high_low(green[c, kz, :, high_rows] * scale)
            turned[c, target, lanes] = dot_nt(turn, high) + dot_nt(turn, low)
            return carry

        lax.fori_loop(0, 4, part, 0)


def pack_halves(source, target):
    low = iota((256, 128), 1) < 64
    upper = pltpu.roll(source[256:512, :].astype(F32), 64, 1)
    target[0:256, :] = jnp.where(low, source[0:256, :].astype(F32), upper).astype(BF)


def unpack_half(packed, half):
    rows = packed[0:256, :].astype(F32)
    return rows if half == 0 else pltpu.roll(rows, 64, 1)


def pack_sources(source, target):
    pack_halves(source, target)
    which = iota((16, 128), 1) - 64
    pick = jnp.where((which == iota((16, 128), 0)) & (which < 2), 1.0, 0.0).astype(BF)
    corners = dot_nt(pick, source[...])
    rows = [corners[c : c + 1, 128 * m : 128 * m + 128] for c in range(2) for m in range(4)]
    target[256:272, :] = jnp.concatenate(rows + [jnp.zeros((8, 128), F32)], axis=0).astype(BF)


def unpack_sources(packed, target):
    corners = jnp.transpose(packed[256:272, :].astype(F32)[0:8])
    lane = iota((128, 128), 1)
    for m in range(4):
        part = unpack_half(packed, m // 2)[128 * (m % 2) : 128 * (m % 2) + 128]
        part = jnp.where(lane < 64, part, 0.0)
        part = jnp.where(lane == 64, corners[:, m : m + 1], part)
        part = jnp.where(lane == 65, corners[:, 4 + m : 5 + m], part)
        target[128 * m : 128 * m + 128, :] = part.astype(BF)


def whole_kernel(
    cur, cells, owned, picks, count, near_hbm, proj_hbm, green_hbm,
    tch_hbm, tcl_hbm, tsh_hbm, tsl_hbm, ahead_hbm, backwards_hbm, cos_hbm, sin_hbm, out,
    matrices, proj, green, tch, tcl, tsh, tsl, ahead, backwards, cos, sin, load_sem, twist,
    codes, p_high, p_low, hots, vals, boxed, box_real, box_imag,
    beside, spread_back, back, kept, edges, edges_in, on_a, on_b, lv_one, lv_two, near, turned,
    padded, wide_a, wide_b, starts, odd, even, hot, acc_a, acc_b, spec, pot, d_one, d_two, h_one, h_two,
    send_a, recv_a, send_b, recv_b, sem_send_a, sem_recv_a, sem_send_b, sem_recv_b,
    send_c, recv_c, send_d, recv_d, sem_send_c, sem_recv_c, sem_send_d, sem_recv_d,
    sem_send_h, sem_recv_h, sem_send_r, sem_recv_r,
    far_c, send_o, recv_o, far_starts, far_hot, far_a, recv_f, send_q, recv_q, sem_far,
):
    row, col = lax.axis_index("row"), lax.axis_index("col")
    mesh_ids = pl.DeviceIdType.MESH

    def row_peer(j):
        return (lax.rem(row + j, NROW), col)

    def col_peer(j):
        return (row, lax.rem(col + j, NCOL))

    def beside_peer(dim, step):
        if dim == 0:
            return (lax.rem(row + step + NROW, NROW), col)
        return (row, lax.rem(col + step + NCOL, NCOL))

    barrier = pltpu.get_barrier_semaphore()
    peers = [row_peer(j) for j in range(1, NROW)] + [col_peer(j) for j in range(1, NCOL)]
    for peer in peers:
        pl.semaphore_signal(barrier, inc=1, device_id=peer, device_id_type=mesh_ids)

    pairs = [
        (proj_hbm, proj), (tch_hbm, tch), (tcl_hbm, tcl), (tsh_hbm, tsh), (tsl_hbm, tsl),
        (near_hbm, matrices), (ahead_hbm, ahead), (backwards_hbm, backwards), (cos_hbm, cos),
        (sin_hbm, sin), (green_hbm, green),
    ]
    loads = [pltpu.make_async_copy(a, b, load_sem.at[i]) for i, (a, b) in enumerate(pairs)]
    for load in loads[:5]:
        load.start()

    def remote(source, target, sem_send, sem_recv, peer):
        return pltpu.make_async_remote_copy(
            src_ref=source,
            dst_ref=target,
            send_sem=sem_send,
            recv_sem=sem_recv,
            device_id=peer,
            device_id_type=mesh_ids,
        )

    z, core = row // 2, lax.rem(row, 2)
    sibling = 2 * z + 1 - core
    far, far_sibling = lax.rem(row + 4, NROW), lax.rem(sibling + 4, NROW)
    chips = [lax.rem(z + 1, 4), lax.rem(z + 3, 4)]

    def row_copy(kz, source, target, sems, j, peer):
        return remote(source, target, sems[0].at[kz, j], sems[1].at[kz, j], (peer, col))

    def tile_rows(c):
        return pl.ds(pl.multiple_of(c * NB, NB), NB)

    def col_copies(source, target, sem_send, sem_recv):
        return [
            remote(
                source.at[tile_rows(col_peer(j)[1])],
                target.at[tile_rows(col)],
                sem_send.at[j],
                sem_recv.at[j],
                col_peer(j),
            )
            for j in range(1, NCOL)
        ]

    for g in range(NB):
        two = cur[:, BLK * g : BLK * g + BLK]
        vals[g] = two
    rounded = jnp.concatenate([vals[:, 0, :], vals[:, 1, :]], axis=1).astype(BF)
    beside[1, NB : 2 * NB, :] = rounded
    for load in loads[:5]:
        load.wait()
    for load in loads[5:]:
        load.start()
    spreads, wides, accs = (ahead, backwards), (wide_a, wide_b), (acc_a, acc_b)
    project(
        cur, proj, cells, tch, tcl, tsh, tsl, send_c, codes, p_high, p_low, hots, vals, boxed,
        row, col, twist,
    )
    pl.semaphore_wait(barrier, len(peers))
    third = col_copies(send_c, recv_c, sem_send_c, sem_recv_c)
    for copy in third:
        copy.start()
    middle = pl.ds(NB, NB)
    halo = [
        remote(
            beside.at[1, middle],
            beside.at[1, pl.ds(NB * place, NB)],
            sem_send_h.at[place],
            sem_recv_h.at[place],
            beside_peer(0, step),
        )
        for step, place in ((1, 0), (-1, 2))
    ]
    for copy in halo:
        copy.start()
    recv_c[tile_rows(col), :] = send_c[tile_rows(col), :]
    loads[5].wait()
    near_backward(beside, owned, picks, count, matrices, on_a, lv_one, lv_two, spread_back)
    for copy in halo:
        copy.wait_recv()
    wide_halo = [
        remote(
            beside.at[1], beside.at[place], sem_send_h.at[3 + place], sem_recv_h.at[3 + place],
            beside_peer(1, step),
        )
        for step, place in ((1, 0), (-1, 2))
    ]
    returns = [
        remote(
            spread_back.at[place], back.at[place], sem_send_r.at[place], sem_recv_r.at[place],
            beside_peer(1, step),
        )
        for step, place in ((-1, 0), (1, 2))
    ]
    for copy in returns + wide_halo:
        copy.start()
    for load in loads[6:]:
        load.wait()
    for kz in range(2):
        turn_green(kz, green, turned)
    for copy in third:
        copy.wait_recv()
    pack_sources(recv_c, send_o)
    over = remote(send_o, recv_o, sem_far.at[0], sem_far.at[1], (far, col))
    over.start()
    build_image(recv_c, row, spreads, padded, wides, starts, odd, even)
    sems_a, sems_b = (sem_send_a, sem_recv_a), (sem_send_b, sem_recv_b)
    first, second, beyond = [[], []], [[], []], [[], []]
    for kz in range(2):
        for m in range(2):
            forward_y(kz, chips[m], odd, even, cos, sin, send_a, 2 * chips[m])
            for j in range(2):
                peer = 2 * chips[m] + lax.rem(core + j, 2)
                copy = row_copy(
                    kz, send_a.at[kz, peer], recv_a.at[kz, row], sems_a, 2 * m + j, peer
                )
                copy.start()
                first[kz].append(copy)
    for kz in range(2):
        forward_y(kz, z, odd, even, cos, sin, send_a, 2 * z)
        copy = row_copy(kz, send_a.at[kz, sibling], recv_a.at[kz, row], sems_a, 4, sibling)
        copy.start()
        first[kz].append(copy)
        recv_a[kz, row] = send_a[kz, row]
    over.wait_recv()
    unpack_sources(recv_o, far_c)
    build_image(far_c, far, spreads, padded, wides, far_starts, odd, even)
    for kz in range(2):
        forward_y(kz, z, odd, even, cos, sin, far_a, 0)
        copy = row_copy(kz, far_a.at[kz, 1 - core], recv_a.at[kz, far], sems_a, 5, sibling)
        copy.start()
        first[kz].append(copy)
        recv_a[kz, far] = far_a[kz, core]
    for copy in returns:
        copy.wait_recv()
    column = spread_back[1].astype(F32) + back[0].astype(F32) + back[2].astype(F32)
    kept[...] = column[NB : 2 * NB]
    edges[0] = column[:NB].astype(BF)
    edges[1] = column[2 * NB :].astype(BF)
    edge_copies = [
        remote(
            edges.at[place], edges_in.at[place], sem_send_r.at[3 + place], sem_recv_r.at[3 + place],
            beside_peer(0, step),
        )
        for step, place in ((-1, 0), (1, 1))
    ]
    for copy in edge_copies:
        copy.start()
    build_hot(recv_c, row, hot)
    build_hot(far_c, far, far_hot)
    clear_cells(accs)
    for kz in range(2):
        for copy in first[kz]:
            copy.wait_recv()
        along_x(kz, recv_a, turned, cos, sin, send_b, d_one, d_two, h_one, h_two)
        targets = [2 * chip + lax.rem(core + j, 2) for chip in chips for j in range(2)]
        targets.append(sibling)
        for j, peer in enumerate(targets):
            copy = row_copy(kz, send_b.at[kz, peer], recv_b.at[kz, row], sems_b, j, peer)
            copy.start()
            second[kz].append(copy)
        copy = row_copy(kz, send_b.at[kz, far_sibling], recv_f.at[kz, core], sems_b, 5, sibling)
        copy.start()
        beyond[kz].append(copy)
        recv_b[kz, row] = send_b[kz, row]
        recv_f[kz, core] = send_b[kz, far]
    for kz in range(2):
        beyond[kz][0].wait_recv()
        inverse_y(kz, recv_f, [0], [z], cos, sin, spec, pot)
        pick_cells(kz, pot, far_starts, far_hot, accs)
    fold_cells(accs, spreads, send_d, None)
    pack_halves(send_d, send_q)
    home = remote(send_q, recv_q, sem_far.at[2], sem_far.at[3], (far, col))
    home.start()
    clear_cells(accs)
    held = [z] + chips
    for kz in range(2):
        for copy in second[kz]:
            copy.wait_recv()
        inverse_y(kz, recv_b, [2 * chip for chip in held], held, cos, sin, spec, pot)
        pick_cells(kz, pot, starts, hot, accs)
    home.wait_recv()
    fold_cells(accs, spreads, send_d, recv_q)
    fourth = col_copies(send_d, recv_d, sem_send_d, sem_recv_d)
    for copy in fourth:
        copy.start()
    recv_d[tile_rows(col), :] = send_d[tile_rows(col), :]
    for copy in wide_halo:
        copy.wait_recv()
    near_onward(beside, owned, picks, count, matrices, on_a, on_b, lv_one, near)
    for copy in edge_copies:
        copy.wait_recv()
    edge_sum = edges_in[0].astype(F32) + edges_in[1].astype(F32)
    near[...] = near[...] + kept[...] + edge_sum
    for copy in fourth:
        copy.wait_recv()
    back_project(
        recv_d, near, tch, tcl, tsh, tsl, out, p_high, p_low, hots, box_real, box_imag, vals, twist
    )
    for kz in range(2):
        for copy in first[kz] + second[kz] + beyond[kz]:
            copy.wait_send()
    for copy in third + fourth + halo + wide_halo + returns + edge_copies + [over, home]:
        copy.wait_send()


def per_device(
    currents, near_blocks, pair_local, pair_ghost, pair_counts, projection, stencil_cells, green
):
    tables = [jnp.asarray(t) for t in depth_tables()]
    tables += [jnp.asarray(t) for t in spread_tables()]
    tables += [jnp.asarray(t) for t in grid_tables()]
    vmem, dma = pltpu.VMEM, pltpu.SemaphoreType.DMA
    grid_part = (2, NROW, 2 * XR, 128)
    wrapped = 512 + 2 * NB
    scratch = [
        vmem((PAIRS, 2 * BLK, BLK), BF),
        vmem((NB, BLK, BLK), F32),
        vmem((2, 2, 128, N), F32),
        *[vmem((512, 512), BF)] * 4,
        *[vmem((128, 2048), BF)] * 2,
        *[vmem((N, N), BF)] * 2,
        dma((11,)),
        vmem((2, NB, 512), F32),
        vmem((NB, BLK), jnp.int32),
        *[vmem((NB, BLK, BLK), BF)] * 2,
        vmem((NB, 512, BLK), BF),
        vmem((NB, 2, BLK), F32),
        vmem((2 * NB, 512), F32),
        *[vmem((NB, 512), F32)] * 2,
        *[vmem((3, 3 * NB, 2 * BLK), BF)] * 3,
        vmem((NB, 2 * BLK), F32),
        *[vmem((2, NB, 2 * BLK), BF)] * 2,
        *[vmem((PAIRS, 2 * BLK), F32)] * 4,
        vmem((NB, 2 * BLK), F32),
        vmem((2, N, 256), F32),
        vmem((wrapped, 128), BF),
        *[vmem((320, 2048), BF)] * 2,
        vmem((wrapped, 128), jnp.int32),
        *[vmem((2, 2 * XR, 512), BF)] * 2,
        vmem((4, wrapped, XR), BF),
        *[vmem((320, 2048), BF)] * 2,
        *[vmem((2 * XR, N), BF)] * 2,
        *[vmem((N, 256), BF)] * 2,
        *[vmem((512, 256), BF)] * 2,
        *[vmem(grid_part, BF)] * 4,
        *[dma((2, NROW))] * 4,
        *[vmem((NCOL * NB, 128), BF)] * 4,
        *[dma((NCOL,))] * 4,
        *[dma((9,))] * 4,
        vmem((NCOL * NB, 128), BF),
        *[vmem((272, 128), BF)] * 2,
        vmem((wrapped, 128), jnp.int32),
        vmem((4, wrapped, XR), BF),
        *[vmem((2, 2, 2 * XR, 128), BF)] * 2,
        *[vmem((256, 128), BF)] * 2,
        dma((4,)),
    ]
    in_vmem = pl.BlockSpec(memory_space=pltpu.VMEM)
    in_smem = pl.BlockSpec(memory_space=pltpu.SMEM)
    anywhere = pl.BlockSpec(memory_space=pl.ANY)
    return pl.pallas_call(
        whole_kernel,
        out_shape=jax.ShapeDtypeStruct((2, NB * BLK), F32),
        in_specs=[in_vmem] * 4 + [in_smem] + [anywhere] * 11,
        out_specs=in_vmem,
        scratch_shapes=scratch,
        compiler_params=pltpu.CompilerParams(
            vmem_limit_bytes=VMEM_LIMIT, collective_id=1, has_side_effects=True
        ),
    )(
        currents,
        stencil_cells,
        pair_local,
        pair_ghost,
        pair_counts,
        near_blocks.reshape(PAIRS, 2 * BLK, BLK),
        projection,
        green,
        *tables,
    )


def solution(mesh):
    in_specs = (
        P(None, ("row", "col")),
        P(("row", "col"), None, None, None),
        P(("row", "col"), None),
        P(("row", "col"), None),
        P(("row", "col")),
        P(("row", "col"), None, None),
        P(("row", "col"), None),
        P(None, "col", "row", None),
    )
    out_specs = P(None, ("row", "col"))
    return jax.shard_map(
        per_device, mesh=mesh, in_specs=in_specs, out_specs=out_specs, check_vma=False
    )
```

```python
import math

import jax
import jax.numpy as jnp
import ml_dtypes
import numpy as np
from jax import lax
from jax.experimental import pallas as pl
from jax.experimental.pallas import tpu as pltpu
from jax.sharding import PartitionSpec as P

N = 1024
NGZ = 32
NROW = 8
NCOL = 16
NB = 32
BLK = 128
PAIRS = 128
XR = 144
WIDE_Y = 68
BF = jnp.bfloat16
F32 = jnp.float32
VMEM_LIMIT = 60 * 1024 * 1024


def bf(a):
    return np.asarray(a, dtype=np.float64).astype(ml_dtypes.bfloat16)


def split_np(a):
    high = bf(a)
    return high, bf(a - high.astype(np.float64))


def grid_tables():
    odd = 2 * np.arange(N) + 1
    angle = (odd[:, None] * odd[None, :] % (4 * N)) * (math.pi / (2 * N))
    return bf(np.cos(angle)), bf(np.sin(angle))


def depth_tables():
    index = np.arange(NGZ)[:, None] * np.arange(NGZ)[None, :] % NGZ
    angle = index * (2.0 * math.pi / NGZ)
    eye = np.eye(16)
    cos_high, cos_low = split_np(np.kron(np.cos(angle), eye))
    sin_high, sin_low = split_np(np.kron(np.sin(angle), eye))
    return cos_high, cos_low, sin_high, sin_low


def spread_tables():
    lane = np.arange(128)[:, None]
    plane, ex, b = lane // 16, lane // 4 % 4, lane % 4
    wide = np.arange(2048)[None, :]
    hits = (wide // 512 == ex) & (wide // 128 % 4 == plane) & (lane < 64)
    ahead = hits & ((wide + 2) % 4 == b)
    backwards = hits & ((wide + 2) % 4 == 3 - b)
    return bf(ahead.astype(np.float64)), bf(backwards.astype(np.float64))


def dot(a, b):
    return jnp.dot(a, b, preferred_element_type=F32)


def dot_nt(a, b):
    return lax.dot_general(a, b, (((1,), (1,)), ((), ())), preferred_element_type=F32)


def iota(shape, dim):
    return lax.broadcasted_iota(jnp.int32, shape, dim)


def high_low(a):
    high = a.astype(BF)
    return high, (a - high.astype(F32)).astype(BF)


def rows_high_low(a):
    high = a.astype(BF).astype(F32)
    return jnp.concatenate([high, a - high], axis=0).astype(BF)


def cell_codes(cells):
    z = cells & (NGZ - 1)
    t = cells >> 5
    x = (t * 15421) >> 20
    y = t - x * WIDE_Y
    corner_x = jnp.min(x, axis=1, keepdims=True)
    corner_y = jnp.min(y, axis=1, keepdims=True)
    code = z * 16 + (x - corner_x) * 4 + (y & 3)
    return code, corner_x, corner_y


def one_hot_rows(code_row):
    return jnp.where(iota((512, 128), 0) == code_row, 1.0, 0.0).astype(BF)


def store_twist(corner_x, corner_y, row, col, twist):
    lane = iota((NB, 128), 1)
    x = (corner_x + ((lane >> 2) & 3) + 128 * row - 2) & (N - 1)
    y = (corner_y + ((lane - corner_y) & 3) + 64 * col - 2) & (N - 1)
    angle = (x + y).astype(F32) * (math.pi / N)
    twist[0] = jnp.concatenate([jnp.cos(angle)] * 4, axis=1)
    twist[1] = jnp.concatenate([jnp.sin(angle)] * 4, axis=1)


def project(
    cur, proj, cells, tch, tcl, tsh, tsl, out, codes, p_high, p_low, hots, vals, boxed, row, col, twist
):
    code, corner_x, corner_y = cell_codes(cells[...])
    codes[...] = code

    def values_of(i, carry):
        for u in range(8):
            g = i * 8 + u
            lhs = rows_high_low(cur[:, pl.ds(pl.multiple_of(g * BLK, BLK), BLK)])
            high, low = high_low(proj[g])
            p_high[g] = high
            p_low[g] = low
            first = dot_nt(lhs, high)
            vals[g] = first[0:2] + first[2:4] + dot_nt(lhs, low)[0:2]
        return carry

    lax.fori_loop(0, NB // 8, values_of, 0)

    def boxes_of(i, carry):
        for u in range(8):
            g = i * 8 + u
            hot = one_hot_rows(codes[pl.ds(g, 1), :])
            hots[g] = hot
            placed = dot_nt(rows_high_low(vals[g]), hot)
            boxed[pl.ds(g, 1), :] = placed[0:1] + placed[2:3]
            boxed[pl.ds(NB + g, 1), :] = placed[1:2] + placed[3:4]
        return carry

    lax.fori_loop(0, NB // 8, boxes_of, 0)
    b_high, b_low = high_low(boxed[...])
    both_parts = jnp.concatenate([b_high, b_low], axis=0)
    by_cos, by_sin = dot(both_parts, tch[...]), dot(both_parts, tsh[...])
    along_cos = by_cos[: 2 * NB] + by_cos[2 * NB :] + dot(b_high, tcl[...])
    along_sin = by_sin[: 2 * NB] + by_sin[2 * NB :] + dot(b_high, tsl[...])
    store_twist(corner_x, corner_y, row, col, twist)
    plain_real = along_cos[:NB] + along_sin[NB:]
    plain_imag = along_cos[NB:] - along_sin[:NB]
    real = plain_real * twist[0] - plain_imag * twist[1]
    imag = plain_real * twist[1] + plain_imag * twist[0]
    lane = iota((NB, 64), 1)
    corners = jnp.where(lane == 0, corner_x, jnp.where(lane == 1, corner_y, 0)).astype(F32)
    for c in range(NCOL):
        part = slice(32 * c, 32 * c + 32)
        message = jnp.concatenate([real[:, part], imag[:, part], corners], axis=1)
        out[NB * c : NB * c + NB, :] = message.astype(BF)


def local_x_of_row(shape, dim, band):
    row = iota(shape, dim)
    tile = row - 128
    main = jnp.where(band >= 4, 129 - row, row + 2)
    upper = jnp.where(lax.rem(band + 1, NROW) >= 4, 137 - tile, 130 + tile)
    upper = jnp.where((upper >= 130) & (upper < 132), upper, -64)
    lower = jnp.where(lax.rem(band + NROW - 1, NROW) >= 4, 9 - tile, tile - 14)
    lower = jnp.where((lower >= 0) & (lower < 2), lower, -64)
    return jnp.where(row < 128, main, jnp.where(tile < 8, upper, lower))


def store_starts(recv, starts):
    block = iota((512, 1), 0)
    start = recv[:, 65:66].astype(jnp.int32) + (block // NB) * 64 - 2
    starts[NB : NB + 512, :] = jnp.broadcast_to(start, (512, 128))
    starts[0:NB, :] = starts[512 : 512 + NB, :]
    starts[NB + 512 :, :] = starts[NB : 2 * NB, :]


def chunk_mask(starts, q):
    lane = iota((128, 128), 1)
    cell = 128 * q + lane if q < 4 else 128 * q + 127 - lane
    inside = ((cell - starts[64 * q : 64 * q + 128, :]) & (N - 1)) < 4
    return jnp.where(inside, 1.0, 0.0)


def image_chunk(q, corner, local_x, wides, starts, masks):
    first = 64 * q if q < 4 else 64 * q - 256
    wide = wides[0] if q < 4 else wides[1]
    mask = chunk_mask(starts, q)
    masks[q] = mask
    mask = jnp.concatenate([mask.astype(BF)] * 4, axis=1)
    offset = local_x - corner[0:1, 64 * q : 64 * q + 128].astype(jnp.int32)
    lhs = [jnp.where(offset == ex, 1.0, 0.0).astype(BF) for ex in range(4)]
    rhs = [wide[first : first + 128, 512 * ex : 512 * ex + 512] * mask for ex in range(4)]
    return dot(jnp.concatenate(lhs, axis=1), jnp.concatenate(rhs, axis=0))


def build_image(recv, band, spreads, padded, wides, starts, masks, odd, even):
    padded[0:NB, :] = recv[512 - NB :, :]
    padded[NB : NB + 512, :] = recv[...]
    padded[NB + 512 :, :] = recv[0:NB, :]

    def spread_lanes(i, carry):
        lanes = pl.ds(pl.multiple_of(i * 512, 512), 512)
        wides[0][:, lanes] = dot(padded[0:320, :], spreads[0][:, lanes]).astype(BF)
        wides[1][:, lanes] = dot(padded[256:576, :], spreads[1][:, lanes]).astype(BF)
        return carry

    lax.fori_loop(0, 4, spread_lanes, 0)
    store_starts(recv, starts)
    pick = jnp.where(iota((16, 128), 1) == 64, 1.0, 0.0).astype(BF)
    corner = dot_nt(pick, recv[...])[0:8]
    corner = jnp.concatenate([corner[:, 480:], corner, corner[:, :NB]], axis=1)
    local_x = local_x_of_row((XR, 128), 0, band)
    for q in range(4):
        ahead = image_chunk(q, corner, local_x, wides, starts, masks)
        backwards = image_chunk(7 - q, corner, local_x, wides, starts, masks)
        minus, plus = (ahead - backwards).astype(BF), (ahead + backwards).astype(BF)
        for kz in range(2):
            for c in range(2):
                p = 2 * c + kz
                place = (kz, slice(XR * c, XR * c + XR), slice(128 * q, 128 * q + 128))
                odd[place] = minus[:, 128 * p : 128 * p + 128]
                even[place] = plus[:, 128 * p : 128 * p + 128]


def forward_y(kz, chip, odd, even, cos, sin, out, slot):
    lanes = pl.ds(pl.multiple_of(chip * 256, 256), 256)
    by_cos = dot(odd[kz], cos[0:512, lanes])
    by_sin = dot(even[kz], sin[0:512, lanes])
    real = (by_cos[:XR] + by_sin[XR:]).astype(BF)
    imag = (by_cos[XR:] - by_sin[:XR]).astype(BF)
    for j in range(2):
        out[kz, slot + j, 0:XR, :] = real[:, 128 * j : 128 * j + 128]
        out[kz, slot + j, XR:, :] = imag[:, 128 * j : 128 * j + 128]


def along_x(kz, recv, green, cos, sin, out, d_one, d_two, h_one, h_two):
    none = jnp.zeros((8, 128), F32)
    for r in range(NROW):
        before, after = (r - 1) % NROW, (r + 1) % NROW
        back = r >= 4
        start = 512 + 128 * (7 - r) if back else 128 * r
        rows = slice(start, start + 128)
        for c in range(2):
            base = XR * c
            main = recv[kz, r, base : base + 128, :]
            upper = recv[kz, before, base + 128 : base + XR, :].astype(F32)[0:8]
            lower = recv[kz, after, base + 128 : base + XR, :].astype(F32)[8:16]
            head, tail = (lower, upper) if back else (upper, lower)
            head = main[0:16].astype(F32) + jnp.concatenate([head, none], axis=0)
            tail = main[112:128].astype(F32) + jnp.concatenate([none, tail], axis=0)
            band = jnp.concatenate([head.astype(BF), main[16:112], tail.astype(BF)], axis=0)
            d_one[rows, 128 * c : 128 * c + 128] = -band if back else band
            d_two[rows, 128 - 128 * c : 256 - 128 * c] = -band if c == 0 else band

    def forward(i, carry):
        rows = pl.ds(pl.multiple_of(i * 256, 256), 256)
        high_rows = pl.ds(pl.multiple_of(i * 256 + 512, 256), 256)
        cos_i, sin_i = cos[rows, 0:512], sin[rows, 0:512]
        by_cos = dot(cos_i, d_one[0:512, :]) + dot(cos_i, d_one[512:, :])
        by_sin = dot(sin_i, d_two[0:512, :]) + dot(sin_i, d_two[512:, :])
        lanes = slice(128 * kz, 128 * kz + 128)
        parts = []
        for spec, where in ((by_sin + by_cos, rows), (by_sin - by_cos, high_rows)):
            real, imag = spec[:, :128], spec[:, 128:]
            g_real, g_imag = green[0, where, lanes], green[1, where, lanes]
            parts.append((real * g_real - imag * g_imag, real * g_imag + imag * g_real))
        (low_real, low_imag), (high_real, high_imag) = parts
        h_one[rows, 0:128] = (low_real - high_real).astype(BF)
        h_one[rows, 128:256] = (low_imag - high_imag).astype(BF)
        h_two[rows, 0:128] = -(low_imag + high_imag).astype(BF)
        h_two[rows, 128:256] = (low_real + high_real).astype(BF)
        return carry

    lax.fori_loop(0, 2, forward, 0)

    def inverse(i, carry):
        rows = pl.ds(pl.multiple_of(i * 256, 256), 256)
        by_cos = dot(cos[rows, 0:512], h_one[...])
        by_sin = dot(sin[rows, 0:512], h_two[...])
        low, high = (by_sin + by_cos).astype(BF), (by_sin - by_cos).astype(BF)
        for j in range(2):
            for c in range(2):
                place = (slice(128 * j, 128 * j + 128), slice(128 * c, 128 * c + 128))
                out[kz, 2 * i + j, XR * c : XR * c + 128, :] = low[place]
                out[kz, 7 - 2 * i - j, XR * c : XR * c + 128, :] = high[place]
        return carry

    lax.fori_loop(0, 2, inverse, 0)
    for r in range(NROW):
        before, after = (r - 1) % NROW, (r + 1) % NROW
        for c in range(2):
            base = XR * c
            above = out[kz, after, base : base + 16, :].astype(F32)[0:8]
            if after >= 4:
                above = out[kz, after, base + 112 : base + 128, :].astype(F32)[8:16]
            below = out[kz, before, base + 112 : base + 128, :].astype(F32)[8:16]
            if before >= 4:
                below = out[kz, before, base : base + 16, :].astype(F32)[0:8]
            out[kz, r, base + 128 : base + XR, :] = jnp.concatenate([above, below], axis=0).astype(BF)


def inverse_y(kz, recv, slots, chips, cos, sin, spec, pot):
    for m, slot in enumerate(slots):
        for j in range(2):
            spec[:, 256 * m + 128 * j : 256 * m + 128 * j + 128] = recv[kz, slot + j]

    def lanes_of(i, carry):
        lanes = pl.ds(pl.multiple_of(i * 256, 256), 256)
        by_cos, by_sin = 0.0, 0.0
        for m, chip in enumerate(chips):
            rows = pl.ds(pl.multiple_of(chip * 256, 256), 256)
            part = spec[:, 256 * m : 256 * m + 256]
            by_cos = by_cos + dot(part, cos[rows, lanes])
            by_sin = by_sin + dot(part, sin[rows, lanes])
        high_lanes = pl.ds(pl.multiple_of(i * 256 + 512, 256), 256)
        pot[0:XR, lanes] = (by_cos[:XR] - by_sin[XR:]).astype(BF)
        pot[XR:, lanes] = (by_cos[XR:] + by_sin[:XR]).astype(BF)
        pot[0:XR, high_lanes] = -(by_cos[:XR] + by_sin[XR:]).astype(BF)
        pot[XR:, high_lanes] = (by_sin[:XR] - by_cos[XR:]).astype(BF)
        return carry

    lax.fori_loop(0, 2, lanes_of, 0)


def build_hot(recv, band, hot):
    local_x = local_x_of_row((512, XR), 1, band)
    offset = local_x - recv[:, 64:65].astype(jnp.int32)
    for ex in range(4):
        hot[ex, NB : NB + 512, :] = jnp.where(offset == ex, 1.0, 0.0).astype(BF)
    hot[:, 0:NB, :] = hot[:, 512 : 512 + NB, :]
    hot[:, NB + 512 :, :] = hot[:, NB : 2 * NB, :]


def pick_cells(kz, pot, masks, hot, accs):
    for q in range(8):
        mask = jnp.concatenate([masks[q]] * 2, axis=1)
        lane = 128 * q if q < 4 else 512 + 128 * (7 - q)
        cells = [pot[XR * c : XR * c + XR, lane : lane + 128] for c in range(2)]
        cells = jnp.concatenate(cells, axis=1)
        first = 64 * q if q < 4 else 64 * q - 256
        rows = slice(first, first + 128)
        acc = accs[0] if q < 4 else accs[1]
        for ex in range(4):
            taken = (dot(hot[ex, 64 * q : 64 * q + 128, :], cells) * mask).astype(BF)
            for c in range(2):
                lane = 512 * ex + 256 * c + 128 * kz
                lanes = slice(lane, lane + 128)
                acc[rows, lanes] = acc[rows, lanes] + taken[:, 128 * c : 128 * c + 128]


def clear_cells(accs):
    for acc in accs:
        acc[...] = jnp.zeros_like(acc)


def fold_cells(accs, spreads, out, extra):
    a = dot_nt(accs[0][...], spreads[0][...])
    b = dot_nt(accs[1][...], spreads[1][...])
    pieces = [a[32:64] + b[288:320], a[64:256], a[256:320] + b[0:64], b[64:256], b[256:288] + a[0:32]]
    cells = jnp.concatenate(pieces, axis=0)
    if extra is not None:
        halves = [unpack_half(extra, 0), unpack_half(extra, 1)]
        cells = cells + jnp.concatenate(halves, axis=0)
    out[...] = cells.astype(BF)


def back_project(
    recv, near, tch, tcl, tsh, tsl, out, p_high, p_low, hots, box_real, box_imag, vals, twist
):
    real = jnp.concatenate([recv[NB * c : NB * c + NB, 0:32] for c in range(NCOL)], axis=1)
    imag = jnp.concatenate([recv[NB * c : NB * c + NB, 32:64] for c in range(NCOL)], axis=1)
    real, imag = real.astype(F32), imag.astype(F32)
    turned_real = real * twist[0] + imag * twist[1]
    turned_imag = imag * twist[0] - real * twist[1]
    b_high, b_low = high_low(jnp.concatenate([turned_real, turned_imag], axis=0))
    both_parts = jnp.concatenate([b_high, b_low], axis=0)
    by_cos, by_sin = dot(both_parts, tch[...]), dot(both_parts, tsh[...])
    along_cos = by_cos[: 2 * NB] + by_cos[2 * NB :] + dot(b_high, tcl[...])
    along_sin = by_sin[: 2 * NB] + by_sin[2 * NB :] + dot(b_high, tsl[...])
    box_real[...] = along_cos[:NB] - along_sin[NB:]
    box_imag[...] = along_cos[NB:] + along_sin[:NB]

    def values_of(i, carry):
        for u in range(8):
            g = i * 8 + u
            box = jnp.concatenate([box_real[pl.ds(g, 1), :], box_imag[pl.ds(g, 1), :]], axis=0)
            picked = dot(rows_high_low(box), hots[g])
            vals[g] = picked[0:2] + picked[2:4]
        return carry

    lax.fori_loop(0, NB // 8, values_of, 0)

    def blocks_of(i, carry):
        for u in range(8):
            g = i * 8 + u
            lhs = rows_high_low(vals[g])
            first = dot(lhs, p_high[g])
            far = first[0:2] + first[2:4] + dot(lhs, p_low[g])[0:2]
            row = near[pl.ds(g, 1), :]
            beside = jnp.concatenate([row[:, :BLK], row[:, BLK:]], axis=0)
            out[:, pl.ds(pl.multiple_of(g * BLK, BLK), BLK)] = far + beside
        return carry

    lax.fori_loop(0, NB // 8, blocks_of, 0)


def column_of(row):
    return jnp.transpose(jnp.broadcast_to(row.astype(F32), (8, 128)))[:, 0:1].astype(jnp.int32)


def near_backward(beside, owned, picks, count, matrices, back_a, lv_one, lv_two, spread_back):
    hits = jnp.where(iota((PAIRS, NB), 1) == column_of(owned[...]), 1.0, 0.0).astype(BF)
    local = dot(hits, beside[1, NB : 2 * NB, :])
    real, imag = local[:, :BLK], local[:, BLK:]
    lv_one[...] = jnp.concatenate([real, -imag], axis=1)
    lv_two[...] = jnp.concatenate([imag, real], axis=1)
    first_row = iota((8, 2 * BLK), 0) == 0

    def pairs_of(i, carry):
        for u in range(8):
            p = i * 8 + u
            lhs = jnp.where(first_row, lv_one[pl.ds(p, 1), :], lv_two[pl.ds(p, 1), :]).astype(BF)
            got = dot(lhs, matrices[p])
            back_a[pl.ds(p, 1), :] = jnp.concatenate([got[0:1], got[1:2]], axis=1)
        return carry

    lax.fori_loop(0, PAIRS // 8, pairs_of, 0)
    alive = iota((9 * NB, PAIRS), 1) < count[0]
    hits = (iota((9 * NB, PAIRS), 0) == picks[...]) & alive
    table = jnp.where(hits, 1.0, 0.0).astype(BF)
    high, low = high_low(back_a[...])
    total = (dot(table, high) + dot(table, low)).astype(BF)
    for n in range(9):
        rows = slice(NB * (n // 3), NB * (n // 3) + NB)
        spread_back[n % 3, rows, :] = total[NB * n : NB * n + NB, :]


def near_onward(beside, owned, picks, count, matrices, on_a, on_b, lv_one, near):
    hits = jnp.where(iota((PAIRS, 9 * NB), 1) == column_of(picks[...]), 1.0, 0.0).astype(BF)
    tiles = [beside[n % 3, NB * (n // 3) : NB * (n // 3) + NB, :] for n in range(9)]
    lv_one[...] = dot(hits, jnp.concatenate(tiles, axis=0))
    first_row = iota((8, BLK), 0) == 0

    def pairs_of(i, carry):
        for u in range(8):
            p = i * 8 + u
            row = lv_one[pl.ds(p, 1), :]
            lhs = jnp.where(first_row, row[:, :BLK], row[:, BLK:]).astype(BF)
            got = dot_nt(lhs, matrices[p])
            on_a[pl.ds(p, 1), :] = got[0:1]
            on_b[pl.ds(p, 1), :] = got[1:2]
        return carry

    lax.fori_loop(0, PAIRS // 8, pairs_of, 0)
    real = on_a[:, :BLK] - on_b[:, BLK:]
    imag = on_b[:, :BLK] + on_a[:, BLK:]
    alive = iota((NB, PAIRS), 1) < count[0]
    table = jnp.where((iota((NB, PAIRS), 0) == owned[...]) & alive, 1.0, 0.0).astype(BF)
    high, low = high_low(jnp.concatenate([real, imag], axis=1))
    near[...] = dot(table, high) + dot(table, low)


def turn_green(kz, green, turned):
    turn = jnp.where(iota((128, 128), 0) + iota((128, 128), 1) == 127, 1.0, 0.0).astype(BF)
    for c in range(2):

        def part(i, carry):
            rows = pl.ds(pl.multiple_of(i * 128, 128), 128)
            high_rows = pl.ds(pl.multiple_of(896 - i * 128, 128), 128)
            target = pl.ds(pl.multiple_of(i * 128 + 512, 128), 128)
            lanes = slice(128 * kz, 128 * kz + 128)
            scale = 1.0 / (N * N * NGZ)
            turned[c, rows, lanes] = jnp.transpose(green[c, kz, :, rows]) * scale
            high, low = high_low(green[c, kz, :, high_rows] * scale)
            turned[c, target, lanes] = dot_nt(turn, high) + dot_nt(turn, low)
            return carry

        lax.fori_loop(0, 4, part, 0)


def pack_halves(source, target):
    low = iota((256, 128), 1) < 64
    upper = pltpu.roll(source[256:512, :].astype(F32), 64, 1)
    target[0:256, :] = jnp.where(low, source[0:256, :].astype(F32), upper).astype(BF)


def unpack_half(packed, half):
    rows = packed[0:256, :].astype(F32)
    return rows if half == 0 else pltpu.roll(rows, 64, 1)


def pack_sources(source, target):
    pack_halves(source, target)
    which = iota((16, 128), 1) - 64
    pick = jnp.where((which == iota((16, 128), 0)) & (which < 2), 1.0, 0.0).astype(BF)
    corners = dot_nt(pick, source[...])
    rows = [corners[c : c + 1, 128 * m : 128 * m + 128] for c in range(2) for m in range(4)]
    target[256:272, :] = jnp.concatenate(rows + [jnp.zeros((8, 128), F32)], axis=0).astype(BF)


def unpack_sources(packed, target):
    corners = jnp.transpose(packed[256:272, :].astype(F32)[0:8])
    lane = iota((128, 128), 1)
    for m in range(4):
        part = unpack_half(packed, m // 2)[128 * (m % 2) : 128 * (m % 2) + 128]
        part = jnp.where(lane < 64, part, 0.0)
        part = jnp.where(lane == 64, corners[:, m : m + 1], part)
        part = jnp.where(lane == 65, corners[:, 4 + m : 5 + m], part)
        target[128 * m : 128 * m + 128, :] = part.astype(BF)


def whole_kernel(
    cur, cells, owned, picks, count, near_hbm, proj_hbm, green_hbm,
    tch_hbm, tcl_hbm, tsh_hbm, tsl_hbm, ahead_hbm, backwards_hbm, cos_hbm, sin_hbm, out,
    matrices, proj, green, tch, tcl, tsh, tsl, ahead, backwards, cos, sin, load_sem, twist,
    codes, p_high, p_low, hots, vals, boxed, box_real, box_imag,
    beside, spread_back, back, kept, edges, edges_in, on_a, on_b, lv_one, lv_two, near, turned,
    padded, wide_a, wide_b, starts, odd, even, hot, acc_a, acc_b, spec, pot, d_one, d_two, h_one, h_two,
    send_a, recv_a, send_b, recv_b, sem_send_a, sem_recv_a, sem_send_b, sem_recv_b,
    send_c, recv_c, send_d, recv_d, sem_send_c, sem_recv_c, sem_send_d, sem_recv_d,
    sem_send_h, sem_recv_h, sem_send_r, sem_recv_r,
    far_c, send_o, recv_o, masks, far_masks, far_hot, far_a, recv_f, send_q, recv_q, sem_far,
):
    row, col = lax.axis_index("row"), lax.axis_index("col")
    mesh_ids = pl.DeviceIdType.MESH

    def row_peer(j):
        return (lax.rem(row + j, NROW), col)

    def col_peer(j):
        return (row, lax.rem(col + j, NCOL))

    def beside_peer(dim, step):
        if dim == 0:
            return (lax.rem(row + step + NROW, NROW), col)
        return (row, lax.rem(col + step + NCOL, NCOL))

    barrier = pltpu.get_barrier_semaphore()
    peers = [row_peer(j) for j in range(1, NROW)] + [col_peer(j) for j in range(1, NCOL)]
    for peer in peers:
        pl.semaphore_signal(barrier, inc=1, device_id=peer, device_id_type=mesh_ids)

    pairs = [
        (proj_hbm, proj), (tch_hbm, tch), (tcl_hbm, tcl), (tsh_hbm, tsh), (tsl_hbm, tsl),
        (near_hbm, matrices), (ahead_hbm, ahead), (backwards_hbm, backwards), (cos_hbm, cos),
        (sin_hbm, sin), (green_hbm, green),
    ]
    loads = [pltpu.make_async_copy(a, b, load_sem.at[i]) for i, (a, b) in enumerate(pairs)]
    for load in loads[:5]:
        load.start()

    def remote(source, target, sem_send, sem_recv, peer):
        return pltpu.make_async_remote_copy(
            src_ref=source,
            dst_ref=target,
            send_sem=sem_send,
            recv_sem=sem_recv,
            device_id=peer,
            device_id_type=mesh_ids,
        )

    z, core = row // 2, lax.rem(row, 2)
    sibling = 2 * z + 1 - core
    far, far_sibling = lax.rem(row + 4, NROW), lax.rem(sibling + 4, NROW)
    chips = [lax.rem(z + 1, 4), lax.rem(z + 3, 4)]

    def row_copy(kz, source, target, sems, j, peer):
        return remote(source, target, sems[0].at[kz, j], sems[1].at[kz, j], (peer, col))

    def tile_rows(c):
        return pl.ds(pl.multiple_of(c * NB, NB), NB)

    def col_copies(source, target, sem_send, sem_recv):
        return [
            remote(
                source.at[tile_rows(col_peer(j)[1])],
                target.at[tile_rows(col)],
                sem_send.at[j],
                sem_recv.at[j],
                col_peer(j),
            )
            for j in range(1, NCOL)
        ]

    for g in range(NB):
        two = cur[:, BLK * g : BLK * g + BLK]
        vals[g] = two
    rounded = jnp.concatenate([vals[:, 0, :], vals[:, 1, :]], axis=1).astype(BF)
    beside[1, NB : 2 * NB, :] = rounded
    for load in loads[:5]:
        load.wait()
    for load in loads[5:]:
        load.start()
    spreads, wides, accs = (ahead, backwards), (wide_a, wide_b), (acc_a, acc_b)
    project(
        cur, proj, cells, tch, tcl, tsh, tsl, send_c, codes, p_high, p_low, hots, vals, boxed,
        row, col, twist,
    )
    pl.semaphore_wait(barrier, len(peers))
    third = col_copies(send_c, recv_c, sem_send_c, sem_recv_c)
    for copy in third:
        copy.start()
    middle = pl.ds(NB, NB)
    halo = [
        remote(
            beside.at[1, middle],
            beside.at[1, pl.ds(NB * place, NB)],
            sem_send_h.at[place],
            sem_recv_h.at[place],
            beside_peer(0, step),
        )
        for step, place in ((1, 0), (-1, 2))
    ]
    for copy in halo:
        copy.start()
    recv_c[tile_rows(col), :] = send_c[tile_rows(col), :]
    loads[5].wait()
    near_backward(beside, owned, picks, count, matrices, on_a, lv_one, lv_two, spread_back)
    for copy in halo:
        copy.wait_recv()
    wide_halo = [
        remote(
            beside.at[1], beside.at[place], sem_send_h.at[3 + place], sem_recv_h.at[3 + place],
            beside_peer(1, step),
        )
        for step, place in ((1, 0), (-1, 2))
    ]
    returns = [
        remote(
            spread_back.at[place], back.at[place], sem_send_r.at[place], sem_recv_r.at[place],
            beside_peer(1, step),
        )
        for step, place in ((-1, 0), (1, 2))
    ]
    for copy in returns + wide_halo:
        copy.start()
    for load in loads[6:]:
        load.wait()
    for kz in range(2):
        turn_green(kz, green, turned)
    for copy in third:
        copy.wait_recv()
    pack_sources(recv_c, send_o)
    over = remote(send_o, recv_o, sem_far.at[0], sem_far.at[1], (far, col))
    over.start()
    build_image(recv_c, row, spreads, padded, wides, starts, masks, odd, even)
    sems_a, sems_b = (sem_send_a, sem_recv_a), (sem_send_b, sem_recv_b)
    first, second, beyond = [[], []], [[], []], [[], []]
    for kz in range(2):
        for m in range(2):
            forward_y(kz, chips[m], odd, even, cos, sin, send_a, 2 * chips[m])
            for j in range(2):
                peer = 2 * chips[m] + lax.rem(core + j, 2)
                copy = row_copy(
                    kz, send_a.at[kz, peer], recv_a.at[kz, row], sems_a, 2 * m + j, peer
                )
                copy.start()
                first[kz].append(copy)
    for kz in range(2):
        forward_y(kz, z, odd, even, cos, sin, send_a, 2 * z)
        copy = row_copy(kz, send_a.at[kz, sibling], recv_a.at[kz, row], sems_a, 4, sibling)
        copy.start()
        first[kz].append(copy)
        recv_a[kz, row] = send_a[kz, row]
    over.wait_recv()
    unpack_sources(recv_o, far_c)
    build_image(far_c, far, spreads, padded, wides, starts, far_masks, odd, even)
    for kz in range(2):
        forward_y(kz, z, odd, even, cos, sin, far_a, 0)
        copy = row_copy(kz, far_a.at[kz, 1 - core], recv_a.at[kz, far], sems_a, 5, sibling)
        copy.start()
        first[kz].append(copy)
        recv_a[kz, far] = far_a[kz, core]
    for kz in range(2):
        for copy in first[kz]:
            copy.wait_recv()
        along_x(kz, recv_a, turned, cos, sin, send_b, d_one, d_two, h_one, h_two)
        targets = [2 * chip + lax.rem(core + j, 2) for chip in chips for j in range(2)]
        targets.append(sibling)
        for j, peer in enumerate(targets):
            copy = row_copy(kz, send_b.at[kz, peer], recv_b.at[kz, row], sems_b, j, peer)
            copy.start()
            second[kz].append(copy)
        copy = row_copy(kz, send_b.at[kz, far_sibling], recv_f.at[kz, core], sems_b, 5, sibling)
        copy.start()
        beyond[kz].append(copy)
        recv_b[kz, row] = send_b[kz, row]
        recv_f[kz, core] = send_b[kz, far]
        if kz == 0:
            for copy in returns:
                copy.wait_recv()
            column = spread_back[1].astype(F32) + back[0].astype(F32) + back[2].astype(F32)
            kept[...] = column[NB : 2 * NB]
            edges[0] = column[:NB].astype(BF)
            edges[1] = column[2 * NB :].astype(BF)
            edge_copies = [
                remote(
                    edges.at[place], edges_in.at[place], sem_send_r.at[3 + place], sem_recv_r.at[3 + place],
                    beside_peer(0, step),
                )
                for step, place in ((-1, 0), (1, 1))
            ]
            for copy in edge_copies:
                copy.start()
            build_hot(recv_c, row, hot)
            build_hot(far_c, far, far_hot)
            clear_cells(accs)
    for kz in range(2):
        beyond[kz][0].wait_recv()
        inverse_y(kz, recv_f, [0], [z], cos, sin, spec, pot)
        pick_cells(kz, pot, far_masks, far_hot, accs)
    fold_cells(accs, spreads, send_d, None)
    pack_halves(send_d, send_q)
    home = remote(send_q, recv_q, sem_far.at[2], sem_far.at[3], (far, col))
    home.start()
    clear_cells(accs)
    held = [z] + chips
    for kz in range(2):
        for copy in second[kz]:
            copy.wait_recv()
        inverse_y(kz, recv_b, [2 * chip for chip in held], held, cos, sin, spec, pot)
        pick_cells(kz, pot, masks, hot, accs)
    home.wait_recv()
    fold_cells(accs, spreads, send_d, recv_q)
    fourth = col_copies(send_d, recv_d, sem_send_d, sem_recv_d)
    for copy in fourth:
        copy.start()
    recv_d[tile_rows(col), :] = send_d[tile_rows(col), :]
    for copy in wide_halo:
        copy.wait_recv()
    near_onward(beside, owned, picks, count, matrices, on_a, on_b, lv_one, near)
    for copy in edge_copies:
        copy.wait_recv()
    edge_sum = edges_in[0].astype(F32) + edges_in[1].astype(F32)
    near[...] = near[...] + kept[...] + edge_sum
    for copy in fourth:
        copy.wait_recv()
    back_project(
        recv_d, near, tch, tcl, tsh, tsl, out, p_high, p_low, hots, box_real, box_imag, vals, twist
    )
    for kz in range(2):
        for copy in first[kz] + second[kz] + beyond[kz]:
            copy.wait_send()
    for copy in third + fourth + halo + wide_halo + returns + edge_copies + [over, home]:
        copy.wait_send()


def per_device(
    currents, near_blocks, pair_local, pair_ghost, pair_counts, projection, stencil_cells, green
):
    tables = [jnp.asarray(t) for t in depth_tables()]
    tables += [jnp.asarray(t) for t in spread_tables()]
    tables += [jnp.asarray(t) for t in grid_tables()]
    vmem, dma = pltpu.VMEM, pltpu.SemaphoreType.DMA
    grid_part = (2, NROW, 2 * XR, 128)
    wrapped = 512 + 2 * NB
    scratch = [
        vmem((PAIRS, 2 * BLK, BLK), BF),
        vmem((NB, BLK, BLK), F32),
        vmem((2, 2, 128, N), F32),
        *[vmem((512, 512), BF)] * 4,
        *[vmem((128, 2048), BF)] * 2,
        *[vmem((N, N), BF)] * 2,
        dma((11,)),
        vmem((2, NB, 512), F32),
        vmem((NB, BLK), jnp.int32),
        *[vmem((NB, BLK, BLK), BF)] * 2,
        vmem((NB, 512, BLK), BF),
        vmem((NB, 2, BLK), F32),
        vmem((2 * NB, 512), F32),
        *[vmem((NB, 512), F32)] * 2,
        *[vmem((3, 3 * NB, 2 * BLK), BF)] * 3,
        vmem((NB, 2 * BLK), F32),
        *[vmem((2, NB, 2 * BLK), BF)] * 2,
        *[vmem((PAIRS, 2 * BLK), F32)] * 4,
        vmem((NB, 2 * BLK), F32),
        vmem((2, N, 256), F32),
        vmem((wrapped, 128), BF),
        *[vmem((320, 2048), BF)] * 2,
        vmem((wrapped, 128), jnp.int32),
        *[vmem((2, 2 * XR, 512), BF)] * 2,
        vmem((4, wrapped, XR), BF),
        *[vmem((320, 2048), BF)] * 2,
        *[vmem((2 * XR, N), BF)] * 2,
        *[vmem((N, 256), BF)] * 2,
        *[vmem((512, 256), BF)] * 2,
        *[vmem(grid_part, BF)] * 4,
        *[dma((2, NROW))] * 4,
        *[vmem((NCOL * NB, 128), BF)] * 4,
        *[dma((NCOL,))] * 4,
        *[dma((9,))] * 4,
        vmem((NCOL * NB, 128), BF),
        *[vmem((272, 128), BF)] * 2,
        *[vmem((8, 128, 128), F32)] * 2,
        vmem((4, wrapped, XR), BF),
        *[vmem((2, 2, 2 * XR, 128), BF)] * 2,
        *[vmem((256, 128), BF)] * 2,
        dma((4,)),
    ]
    in_vmem = pl.BlockSpec(memory_space=pltpu.VMEM)
    in_smem = pl.BlockSpec(memory_space=pltpu.SMEM)
    anywhere = pl.BlockSpec(memory_space=pl.ANY)
    return pl.pallas_call(
        whole_kernel,
        out_shape=jax.ShapeDtypeStruct((2, NB * BLK), F32),
        in_specs=[in_vmem] * 4 + [in_smem] + [anywhere] * 11,
        out_specs=in_vmem,
        scratch_shapes=scratch,
        compiler_params=pltpu.CompilerParams(
            vmem_limit_bytes=VMEM_LIMIT, collective_id=1, has_side_effects=True
        ),
    )(
        currents,
        stencil_cells,
        pair_local,
        pair_ghost,
        pair_counts,
        near_blocks.reshape(PAIRS, 2 * BLK, BLK),
        projection,
        green,
        *tables,
    )


def solution(mesh):
    in_specs = (
        P(None, ("row", "col")),
        P(("row", "col"), None, None, None),
        P(("row", "col"), None),
        P(("row", "col"), None),
        P(("row", "col")),
        P(("row", "col"), None, None),
        P(("row", "col"), None),
        P(None, "col", "row", None),
    )
    out_specs = P(None, ("row", "col"))
    return jax.shard_map(
        per_device, mesh=mesh, in_specs=in_specs, out_specs=out_specs, check_vma=False
    )
```

```python
import math

import jax
import jax.numpy as jnp
import ml_dtypes
import numpy as np
from jax import lax
from jax.experimental import pallas as pl
from jax.experimental.pallas import tpu as pltpu
from jax.sharding import PartitionSpec as P

N = 1024
NGZ = 32
NROW = 8
NCOL = 16
NB = 32
BLK = 128
PAIRS = 128
XR = 144
WIDE_Y = 68
BF = jnp.bfloat16
F32 = jnp.float32
VMEM_LIMIT = 60 * 1024 * 1024


def bf(a):
    return np.asarray(a, dtype=np.float64).astype(ml_dtypes.bfloat16)


def split_np(a):
    high = bf(a)
    return high, bf(a - high.astype(np.float64))


def grid_tables():
    odd = 2 * np.arange(N) + 1
    angle = (odd[:, None] * odd[None, :] % (4 * N)) * (math.pi / (2 * N))
    return bf(np.cos(angle)), bf(np.sin(angle))


def depth_tables():
    index = np.arange(NGZ)[:, None] * np.arange(NGZ)[None, :] % NGZ
    angle = index * (2.0 * math.pi / NGZ)
    eye = np.eye(16)
    cos_high, cos_low = split_np(np.kron(np.cos(angle), eye))
    sin_high, sin_low = split_np(np.kron(np.sin(angle), eye))
    return cos_high, cos_low, sin_high, sin_low


def spread_tables():
    lane = np.arange(128)[:, None]
    plane, ex, b = lane // 16, lane // 4 % 4, lane % 4
    wide = np.arange(2048)[None, :]
    hits = (wide // 512 == ex) & (wide // 128 % 4 == plane) & (lane < 64)
    ahead = hits & ((wide + 2) % 4 == b)
    backwards = hits & ((wide + 2) % 4 == 3 - b)
    return bf(ahead.astype(np.float64)), bf(backwards.astype(np.float64))


def dot(a, b):
    return jnp.dot(a, b, preferred_element_type=F32)


def dot_nt(a, b):
    return lax.dot_general(a, b, (((1,), (1,)), ((), ())), preferred_element_type=F32)


def iota(shape, dim):
    return lax.broadcasted_iota(jnp.int32, shape, dim)


def high_low(a):
    high = a.astype(BF)
    return high, (a - high.astype(F32)).astype(BF)


def rows_high_low(a):
    high = a.astype(BF).astype(F32)
    return jnp.concatenate([high, a - high], axis=0).astype(BF)


def cell_codes(cells):
    z = cells & (NGZ - 1)
    t = cells >> 5
    x = (t * 15421) >> 20
    y = t - x * WIDE_Y
    corner_x = jnp.min(x, axis=1, keepdims=True)
    corner_y = jnp.min(y, axis=1, keepdims=True)
    code = z * 16 + (x - corner_x) * 4 + (y & 3)
    return code, corner_x, corner_y


def one_hot_rows(code_row):
    return jnp.where(iota((512, 128), 0) == code_row, 1.0, 0.0).astype(BF)


def store_twist(corner_x, corner_y, row, col, twist):
    lane = iota((NB, 128), 1)
    x = (corner_x + ((lane >> 2) & 3) + 128 * row - 2) & (N - 1)
    y = (corner_y + ((lane - corner_y) & 3) + 64 * col - 2) & (N - 1)
    angle = (x + y).astype(F32) * (math.pi / N)
    twist[0] = jnp.concatenate([jnp.cos(angle)] * 4, axis=1)
    twist[1] = jnp.concatenate([jnp.sin(angle)] * 4, axis=1)


def project(
    cur, proj, cells, tch, tcl, tsh, tsl, out, codes, p_high, p_low, hots, vals, boxed, row, col, twist
):
    code, corner_x, corner_y = cell_codes(cells[...])
    codes[...] = code

    def values_of(i, carry):
        for u in range(16):
            g = i * 16 + u
            lhs = rows_high_low(cur[:, pl.ds(pl.multiple_of(g * BLK, BLK), BLK)])
            high, low = high_low(proj[g])
            p_high[g] = high
            p_low[g] = low
            first = dot_nt(lhs, high)
            vals[g] = first[0:2] + first[2:4] + dot_nt(lhs, low)[0:2]
        return carry

    lax.fori_loop(0, NB // 16, values_of, 0)

    def boxes_of(i, carry):
        for u in range(16):
            g = i * 16 + u
            hot = one_hot_rows(codes[pl.ds(g, 1), :])
            hots[g] = hot
            placed = dot_nt(rows_high_low(vals[g]), hot)
            boxed[pl.ds(g, 1), :] = placed[0:1] + placed[2:3]
            boxed[pl.ds(NB + g, 1), :] = placed[1:2] + placed[3:4]
        return carry

    lax.fori_loop(0, NB // 16, boxes_of, 0)
    b_high, b_low = high_low(boxed[...])
    both_parts = jnp.concatenate([b_high, b_low], axis=0)
    by_cos, by_sin = dot(both_parts, tch[...]), dot(both_parts, tsh[...])
    along_cos = by_cos[: 2 * NB] + by_cos[2 * NB :] + dot(b_high, tcl[...])
    along_sin = by_sin[: 2 * NB] + by_sin[2 * NB :] + dot(b_high, tsl[...])
    store_twist(corner_x, corner_y, row, col, twist)
    plain_real = along_cos[:NB] + along_sin[NB:]
    plain_imag = along_cos[NB:] - along_sin[:NB]
    real = plain_real * twist[0] - plain_imag * twist[1]
    imag = plain_real * twist[1] + plain_imag * twist[0]
    lane = iota((NB, 64), 1)
    corners = jnp.where(lane == 0, corner_x, jnp.where(lane == 1, corner_y, 0)).astype(F32)
    for c in range(NCOL):
        part = slice(32 * c, 32 * c + 32)
        message = jnp.concatenate([real[:, part], imag[:, part], corners], axis=1)
        out[NB * c : NB * c + NB, :] = message.astype(BF)


def local_x_of_row(shape, dim, band):
    row = iota(shape, dim)
    tile = row - 128
    main = jnp.where(band >= 4, 129 - row, row + 2)
    upper = jnp.where(lax.rem(band + 1, NROW) >= 4, 137 - tile, 130 + tile)
    upper = jnp.where((upper >= 130) & (upper < 132), upper, -64)
    lower = jnp.where(lax.rem(band + NROW - 1, NROW) >= 4, 9 - tile, tile - 14)
    lower = jnp.where((lower >= 0) & (lower < 2), lower, -64)
    return jnp.where(row < 128, main, jnp.where(tile < 8, upper, lower))


def store_starts(recv, starts):
    block = iota((512, 1), 0)
    start = recv[:, 65:66].astype(jnp.int32) + (block // NB) * 64 - 2
    starts[NB : NB + 512, :] = jnp.broadcast_to(start, (512, 128))
    starts[0:NB, :] = starts[512 : 512 + NB, :]
    starts[NB + 512 :, :] = starts[NB : 2 * NB, :]


def chunk_mask(starts, q):
    lane = iota((128, 128), 1)
    cell = 128 * q + lane if q < 4 else 128 * q + 127 - lane
    inside = ((cell - starts[64 * q : 64 * q + 128, :]) & (N - 1)) < 4
    return jnp.where(inside, 1.0, 0.0)


def image_chunk(q, corner, local_x, wides, starts, masks):
    first = 64 * q if q < 4 else 64 * q - 256
    wide = wides[0] if q < 4 else wides[1]
    mask = chunk_mask(starts, q)
    masks[q] = mask
    mask = jnp.concatenate([mask.astype(BF)] * 4, axis=1)
    offset = local_x - corner[0:1, 64 * q : 64 * q + 128].astype(jnp.int32)
    lhs = [jnp.where(offset == ex, 1.0, 0.0).astype(BF) for ex in range(4)]
    rhs = [wide[first : first + 128, 512 * ex : 512 * ex + 512] * mask for ex in range(4)]
    return dot(jnp.concatenate(lhs, axis=1), jnp.concatenate(rhs, axis=0))


def build_image(recv, band, spreads, padded, wides, starts, masks, odd, even):
    padded[0:NB, :] = recv[512 - NB :, :]
    padded[NB : NB + 512, :] = recv[...]
    padded[NB + 512 :, :] = recv[0:NB, :]

    def spread_lanes(i, carry):
        lanes = pl.ds(pl.multiple_of(i * 512, 512), 512)
        wides[0][:, lanes] = dot(padded[0:320, :], spreads[0][:, lanes]).astype(BF)
        wides[1][:, lanes] = dot(padded[256:576, :], spreads[1][:, lanes]).astype(BF)
        return carry

    lax.fori_loop(0, 4, spread_lanes, 0)
    store_starts(recv, starts)
    pick = jnp.where(iota((16, 128), 1) == 64, 1.0, 0.0).astype(BF)
    corner = dot_nt(pick, recv[...])[0:8]
    corner = jnp.concatenate([corner[:, 480:], corner, corner[:, :NB]], axis=1)
    local_x = local_x_of_row((XR, 128), 0, band)
    for q in range(4):
        ahead = image_chunk(q, corner, local_x, wides, starts, masks)
        backwards = image_chunk(7 - q, corner, local_x, wides, starts, masks)
        minus, plus = (ahead - backwards).astype(BF), (ahead + backwards).astype(BF)
        for kz in range(2):
            for c in range(2):
                p = 2 * c + kz
                place = (kz, slice(XR * c, XR * c + XR), slice(128 * q, 128 * q + 128))
                odd[place] = minus[:, 128 * p : 128 * p + 128]
                even[place] = plus[:, 128 * p : 128 * p + 128]


def forward_y(kz, chip, odd, even, cos, sin, out, slot):
    lanes = pl.ds(pl.multiple_of(chip * 256, 256), 256)
    by_cos = dot(odd[kz], cos[0:512, lanes])
    by_sin = dot(even[kz], sin[0:512, lanes])
    real = (by_cos[:XR] + by_sin[XR:]).astype(BF)
    imag = (by_cos[XR:] - by_sin[:XR]).astype(BF)
    for j in range(2):
        out[kz, slot + j, 0:XR, :] = real[:, 128 * j : 128 * j + 128]
        out[kz, slot + j, XR:, :] = imag[:, 128 * j : 128 * j + 128]


def along_x(kz, recv, green, cos, sin, out, d_one, d_two, h_one, h_two):
    none = jnp.zeros((8, 128), F32)
    for r in range(NROW):
        before, after = (r - 1) % NROW, (r + 1) % NROW
        back = r >= 4
        start = 512 + 128 * (7 - r) if back else 128 * r
        rows = slice(start, start + 128)
        for c in range(2):
            base = XR * c
            main = recv[kz, r, base : base + 128, :]
            upper = recv[kz, before, base + 128 : base + XR, :].astype(F32)[0:8]
            lower = recv[kz, after, base + 128 : base + XR, :].astype(F32)[8:16]
            head, tail = (lower, upper) if back else (upper, lower)
            head = main[0:16].astype(F32) + jnp.concatenate([head, none], axis=0)
            tail = main[112:128].astype(F32) + jnp.concatenate([none, tail], axis=0)
            band = jnp.concatenate([head.astype(BF), main[16:112], tail.astype(BF)], axis=0)
            d_one[rows, 128 * c : 128 * c + 128] = -band if back else band
            d_two[rows, 128 - 128 * c : 256 - 128 * c] = -band if c == 0 else band

    def forward(i, carry):
        rows = pl.ds(pl.multiple_of(i * 256, 256), 256)
        high_rows = pl.ds(pl.multiple_of(i * 256 + 512, 256), 256)
        cos_i, sin_i = cos[rows, 0:512], sin[rows, 0:512]
        by_cos = dot(cos_i, d_one[0:512, :]) + dot(cos_i, d_one[512:, :])
        by_sin = dot(sin_i, d_two[0:512, :]) + dot(sin_i, d_two[512:, :])
        lanes = slice(128 * kz, 128 * kz + 128)
        parts = []
        for spec, where in ((by_sin + by_cos, rows), (by_sin - by_cos, high_rows)):
            real, imag = spec[:, :128], spec[:, 128:]
            g_real, g_imag = green[0, where, lanes], green[1, where, lanes]
            parts.append((real * g_real - imag * g_imag, real * g_imag + imag * g_real))
        (low_real, low_imag), (high_real, high_imag) = parts
        h_one[rows, 0:128] = (low_real - high_real).astype(BF)
        h_one[rows, 128:256] = (low_imag - high_imag).astype(BF)
        h_two[rows, 0:128] = -(low_imag + high_imag).astype(BF)
        h_two[rows, 128:256] = (low_real + high_real).astype(BF)
        return carry

    lax.fori_loop(0, 2, forward, 0)

    def inverse(i, carry):
        rows = pl.ds(pl.multiple_of(i * 256, 256), 256)
        by_cos = dot(cos[rows, 0:512], h_one[...])
        by_sin = dot(sin[rows, 0:512], h_two[...])
        low, high = (by_sin + by_cos).astype(BF), (by_sin - by_cos).astype(BF)
        for j in range(2):
            for c in range(2):
                place = (slice(128 * j, 128 * j + 128), slice(128 * c, 128 * c + 128))
                out[kz, 2 * i + j, XR * c : XR * c + 128, :] = low[place]
                out[kz, 7 - 2 * i - j, XR * c : XR * c + 128, :] = high[place]
        return carry

    lax.fori_loop(0, 2, inverse, 0)
    for r in range(NROW):
        before, after = (r - 1) % NROW, (r + 1) % NROW
        for c in range(2):
            base = XR * c
            above = out[kz, after, base : base + 16, :].astype(F32)[0:8]
            if after >= 4:
                above = out[kz, after, base + 112 : base + 128, :].astype(F32)[8:16]
            below = out[kz, before, base + 112 : base + 128, :].astype(F32)[8:16]
            if before >= 4:
                below = out[kz, before, base : base + 16, :].astype(F32)[0:8]
            out[kz, r, base + 128 : base + XR, :] = jnp.concatenate([above, below], axis=0).astype(BF)


def inverse_y(kz, recv, slots, chips, cos, sin, spec, pot):
    for m, slot in enumerate(slots):
        for j in range(2):
            spec[:, 256 * m + 128 * j : 256 * m + 128 * j + 128] = recv[kz, slot + j]

    def lanes_of(i, carry):
        lanes = pl.ds(pl.multiple_of(i * 256, 256), 256)
        by_cos, by_sin = 0.0, 0.0
        for m, chip in enumerate(chips):
            rows = pl.ds(pl.multiple_of(chip * 256, 256), 256)
            part = spec[:, 256 * m : 256 * m + 256]
            by_cos = by_cos + dot(part, cos[rows, lanes])
            by_sin = by_sin + dot(part, sin[rows, lanes])
        high_lanes = pl.ds(pl.multiple_of(i * 256 + 512, 256), 256)
        pot[0:XR, lanes] = (by_cos[:XR] - by_sin[XR:]).astype(BF)
        pot[XR:, lanes] = (by_cos[XR:] + by_sin[:XR]).astype(BF)
        pot[0:XR, high_lanes] = -(by_cos[:XR] + by_sin[XR:]).astype(BF)
        pot[XR:, high_lanes] = (by_sin[:XR] - by_cos[XR:]).astype(BF)
        return carry

    lax.fori_loop(0, 2, lanes_of, 0)


def build_hot(recv, band, hot):
    local_x = local_x_of_row((512, XR), 1, band)
    offset = local_x - recv[:, 64:65].astype(jnp.int32)
    for ex in range(4):
        hot[ex, NB : NB + 512, :] = jnp.where(offset == ex, 1.0, 0.0).astype(BF)
    hot[:, 0:NB, :] = hot[:, 512 : 512 + NB, :]
    hot[:, NB + 512 :, :] = hot[:, NB : 2 * NB, :]


def pick_cells(kz, pot, masks, hot, accs):
    for q in range(8):
        mask = jnp.concatenate([masks[q]] * 2, axis=1)
        lane = 128 * q if q < 4 else 512 + 128 * (7 - q)
        cells = [pot[XR * c : XR * c + XR, lane : lane + 128] for c in range(2)]
        cells = jnp.concatenate(cells, axis=1)
        first = 64 * q if q < 4 else 64 * q - 256
        rows = slice(first, first + 128)
        acc = accs[0] if q < 4 else accs[1]
        for ex in range(4):
            taken = (dot(hot[ex, 64 * q : 64 * q + 128, :], cells) * mask).astype(BF)
            for c in range(2):
                lane = 512 * ex + 256 * c + 128 * kz
                lanes = slice(lane, lane + 128)
                acc[rows, lanes] = acc[rows, lanes] + taken[:, 128 * c : 128 * c + 128]


def clear_cells(accs):
    for acc in accs:
        acc[...] = jnp.zeros_like(acc)


def fold_cells(accs, spreads, out, extra):
    a = dot_nt(accs[0][...], spreads[0][...])
    b = dot_nt(accs[1][...], spreads[1][...])
    pieces = [a[32:64] + b[288:320], a[64:256], a[256:320] + b[0:64], b[64:256], b[256:288] + a[0:32]]
    cells = jnp.concatenate(pieces, axis=0)
    if extra is not None:
        halves = [unpack_half(extra, 0), unpack_half(extra, 1)]
        cells = cells + jnp.concatenate(halves, axis=0)
    out[...] = cells.astype(BF)


def back_project(
    recv, near, tch, tcl, tsh, tsl, out, p_high, p_low, hots, box_real, box_imag, vals, twist
):
    real = jnp.concatenate([recv[NB * c : NB * c + NB, 0:32] for c in range(NCOL)], axis=1)
    imag = jnp.concatenate([recv[NB * c : NB * c + NB, 32:64] for c in range(NCOL)], axis=1)
    real, imag = real.astype(F32), imag.astype(F32)
    turned_real = real * twist[0] + imag * twist[1]
    turned_imag = imag * twist[0] - real * twist[1]
    b_high, b_low = high_low(jnp.concatenate([turned_real, turned_imag], axis=0))
    both_parts = jnp.concatenate([b_high, b_low], axis=0)
    by_cos, by_sin = dot(both_parts, tch[...]), dot(both_parts, tsh[...])
    along_cos = by_cos[: 2 * NB] + by_cos[2 * NB :] + dot(b_high, tcl[...])
    along_sin = by_sin[: 2 * NB] + by_sin[2 * NB :] + dot(b_high, tsl[...])
    box_real[...] = along_cos[:NB] - along_sin[NB:]
    box_imag[...] = along_cos[NB:] + along_sin[:NB]

    def values_of(i, carry):
        for u in range(16):
            g = i * 16 + u
            box = jnp.concatenate([box_real[pl.ds(g, 1), :], box_imag[pl.ds(g, 1), :]], axis=0)
            picked = dot(rows_high_low(box), hots[g])
            vals[g] = picked[0:2] + picked[2:4]
        return carry

    lax.fori_loop(0, NB // 16, values_of, 0)

    def blocks_of(i, carry):
        for u in range(16):
            g = i * 16 + u
            lhs = rows_high_low(vals[g])
            first = dot(lhs, p_high[g])
            far = first[0:2] + first[2:4] + dot(lhs, p_low[g])[0:2]
            row = near[pl.ds(g, 1), :]
            beside = jnp.concatenate([row[:, :BLK], row[:, BLK:]], axis=0)
            out[:, pl.ds(pl.multiple_of(g * BLK, BLK), BLK)] = far + beside
        return carry

    lax.fori_loop(0, NB // 16, blocks_of, 0)


def column_of(row):
    return jnp.transpose(jnp.broadcast_to(row.astype(F32), (8, 128)))[:, 0:1].astype(jnp.int32)


def near_backward(beside, owned, picks, count, matrices, back_a, lv_one, lv_two, spread_back):
    hits = jnp.where(iota((PAIRS, NB), 1) == column_of(owned[...]), 1.0, 0.0).astype(BF)
    local = dot(hits, beside[1, NB : 2 * NB, :])
    real, imag = local[:, :BLK], local[:, BLK:]
    lv_one[...] = jnp.concatenate([real, -imag], axis=1)
    lv_two[...] = jnp.concatenate([imag, real], axis=1)
    first_row = iota((8, 2 * BLK), 0) == 0

    def pairs_of(i, carry):
        for u in range(8):
            p = i * 8 + u
            lhs = jnp.where(first_row, lv_one[pl.ds(p, 1), :], lv_two[pl.ds(p, 1), :]).astype(BF)
            got = dot(lhs, matrices[p])
            back_a[pl.ds(p, 1), :] = jnp.concatenate([got[0:1], got[1:2]], axis=1)
        return carry

    lax.fori_loop(0, PAIRS // 8, pairs_of, 0)
    alive = iota((9 * NB, PAIRS), 1) < count[0]
    hits = (iota((9 * NB, PAIRS), 0) == picks[...]) & alive
    table = jnp.where(hits, 1.0, 0.0).astype(BF)
    high, low = high_low(back_a[...])
    total = (dot(table, high) + dot(table, low)).astype(BF)
    for n in range(9):
        rows = slice(NB * (n // 3), NB * (n // 3) + NB)
        spread_back[n % 3, rows, :] = total[NB * n : NB * n + NB, :]


def near_onward(beside, owned, picks, count, matrices, on_a, on_b, lv_one, near):
    hits = jnp.where(iota((PAIRS, 9 * NB), 1) == column_of(picks[...]), 1.0, 0.0).astype(BF)
    tiles = [beside[n % 3, NB * (n // 3) : NB * (n // 3) + NB, :] for n in range(9)]
    lv_one[...] = dot(hits, jnp.concatenate(tiles, axis=0))
    first_row = iota((8, BLK), 0) == 0

    def pairs_of(i, carry):
        for u in range(8):
            p = i * 8 + u
            row = lv_one[pl.ds(p, 1), :]
            lhs = jnp.where(first_row, row[:, :BLK], row[:, BLK:]).astype(BF)
            got = dot_nt(lhs, matrices[p])
            on_a[pl.ds(p, 1), :] = got[0:1]
            on_b[pl.ds(p, 1), :] = got[1:2]
        return carry

    lax.fori_loop(0, PAIRS // 8, pairs_of, 0)
    real = on_a[:, :BLK] - on_b[:, BLK:]
    imag = on_b[:, :BLK] + on_a[:, BLK:]
    alive = iota((NB, PAIRS), 1) < count[0]
    table = jnp.where((iota((NB, PAIRS), 0) == owned[...]) & alive, 1.0, 0.0).astype(BF)
    high, low = high_low(jnp.concatenate([real, imag], axis=1))
    near[...] = dot(table, high) + dot(table, low)


def turn_green(kz, green, turned):
    turn = jnp.where(iota((128, 128), 0) + iota((128, 128), 1) == 127, 1.0, 0.0).astype(BF)
    for c in range(2):

        def part(i, carry):
            rows = pl.ds(pl.multiple_of(i * 128, 128), 128)
            high_rows = pl.ds(pl.multiple_of(896 - i * 128, 128), 128)
            target = pl.ds(pl.multiple_of(i * 128 + 512, 128), 128)
            lanes = slice(128 * kz, 128 * kz + 128)
            scale = 1.0 / (N * N * NGZ)
            turned[c, rows, lanes] = jnp.transpose(green[c, kz, :, rows]) * scale
            high, low = high_low(green[c, kz, :, high_rows] * scale)
            turned[c, target, lanes] = dot_nt(turn, high) + dot_nt(turn, low)
            return carry

        lax.fori_loop(0, 4, part, 0)


def pack_halves(source, target):
    low = iota((256, 128), 1) < 64
    upper = pltpu.roll(source[256:512, :].astype(F32), 64, 1)
    target[0:256, :] = jnp.where(low, source[0:256, :].astype(F32), upper).astype(BF)


def unpack_half(packed, half):
    rows = packed[0:256, :].astype(F32)
    return rows if half == 0 else pltpu.roll(rows, 64, 1)


def pack_sources(source, target):
    pack_halves(source, target)
    which = iota((16, 128), 1) - 64
    pick = jnp.where((which == iota((16, 128), 0)) & (which < 2), 1.0, 0.0).astype(BF)
    corners = dot_nt(pick, source[...])
    rows = [corners[c : c + 1, 128 * m : 128 * m + 128] for c in range(2) for m in range(4)]
    target[256:272, :] = jnp.concatenate(rows + [jnp.zeros((8, 128), F32)], axis=0).astype(BF)


def unpack_sources(packed, target):
    corners = jnp.transpose(packed[256:272, :].astype(F32)[0:8])
    lane = iota((128, 128), 1)
    for m in range(4):
        part = unpack_half(packed, m // 2)[128 * (m % 2) : 128 * (m % 2) + 128]
        part = jnp.where(lane < 64, part, 0.0)
        part = jnp.where(lane == 64, corners[:, m : m + 1], part)
        part = jnp.where(lane == 65, corners[:, 4 + m : 5 + m], part)
        target[128 * m : 128 * m + 128, :] = part.astype(BF)


def whole_kernel(
    cur, cells, owned, picks, count, near_hbm, proj_hbm, green_hbm,
    tch_hbm, tcl_hbm, tsh_hbm, tsl_hbm, ahead_hbm, backwards_hbm, cos_hbm, sin_hbm, out,
    matrices, proj, green, tch, tcl, tsh, tsl, ahead, backwards, cos, sin, load_sem, twist,
    codes, p_high, p_low, hots, vals, boxed, box_real, box_imag,
    beside, spread_back, back, kept, edges, edges_in, on_a, on_b, lv_one, lv_two, near, turned,
    padded, wide_a, wide_b, starts, odd, even, hot, acc_a, acc_b, spec, pot, d_one, d_two, h_one, h_two,
    send_a, recv_a, send_b, recv_b, sem_send_a, sem_recv_a, sem_send_b, sem_recv_b,
    send_c, recv_c, send_d, recv_d, sem_send_c, sem_recv_c, sem_send_d, sem_recv_d,
    sem_send_h, sem_recv_h, sem_send_r, sem_recv_r,
    far_c, send_o, recv_o, masks, far_masks, far_hot, far_a, recv_f, send_q, recv_q, sem_far,
):
    row, col = lax.axis_index("row"), lax.axis_index("col")
    mesh_ids = pl.DeviceIdType.MESH

    def row_peer(j):
        return (lax.rem(row + j, NROW), col)

    def col_peer(j):
        return (row, lax.rem(col + j, NCOL))

    def beside_peer(dim, step):
        if dim == 0:
            return (lax.rem(row + step + NROW, NROW), col)
        return (row, lax.rem(col + step + NCOL, NCOL))

    barrier = pltpu.get_barrier_semaphore()
    peers = [row_peer(j) for j in range(1, NROW)] + [col_peer(j) for j in range(1, NCOL)]
    for peer in peers:
        pl.semaphore_signal(barrier, inc=1, device_id=peer, device_id_type=mesh_ids)

    pairs = [
        (proj_hbm, proj), (tch_hbm, tch), (tcl_hbm, tcl), (tsh_hbm, tsh), (tsl_hbm, tsl),
        (near_hbm, matrices), (ahead_hbm, ahead), (backwards_hbm, backwards), (cos_hbm, cos),
        (sin_hbm, sin), (green_hbm, green),
    ]
    loads = [pltpu.make_async_copy(a, b, load_sem.at[i]) for i, (a, b) in enumerate(pairs)]
    for load in loads[:5]:
        load.start()

    def remote(source, target, sem_send, sem_recv, peer):
        return pltpu.make_async_remote_copy(
            src_ref=source,
            dst_ref=target,
            send_sem=sem_send,
            recv_sem=sem_recv,
            device_id=peer,
            device_id_type=mesh_ids,
        )

    z, core = row // 2, lax.rem(row, 2)
    sibling = 2 * z + 1 - core
    far, far_sibling = lax.rem(row + 4, NROW), lax.rem(sibling + 4, NROW)
    chips = [lax.rem(z + 1, 4), lax.rem(z + 3, 4)]

    def row_copy(kz, source, target, sems, j, peer):
        return remote(source, target, sems[0].at[kz, j], sems[1].at[kz, j], (peer, col))

    def tile_rows(c):
        return pl.ds(pl.multiple_of(c * NB, NB), NB)

    def col_copies(source, target, sem_send, sem_recv):
        return [
            remote(
                source.at[tile_rows(col_peer(j)[1])],
                target.at[tile_rows(col)],
                sem_send.at[j],
                sem_recv.at[j],
                col_peer(j),
            )
            for j in range(1, NCOL)
        ]

    for g in range(NB):
        two = cur[:, BLK * g : BLK * g + BLK]
        vals[g] = two
    rounded = jnp.concatenate([vals[:, 0, :], vals[:, 1, :]], axis=1).astype(BF)
    beside[1, NB : 2 * NB, :] = rounded
    for load in loads[:5]:
        load.wait()
    for load in loads[5:]:
        load.start()
    spreads, wides, accs = (ahead, backwards), (wide_a, wide_b), (acc_a, acc_b)
    project(
        cur, proj, cells, tch, tcl, tsh, tsl, send_c, codes, p_high, p_low, hots, vals, boxed,
        row, col, twist,
    )
    pl.semaphore_wait(barrier, len(peers))
    third = col_copies(send_c, recv_c, sem_send_c, sem_recv_c)
    for copy in third:
        copy.start()
    middle = pl.ds(NB, NB)
    halo = [
        remote(
            beside.at[1, middle],
            beside.at[1, pl.ds(NB * place, NB)],
            sem_send_h.at[place],
            sem_recv_h.at[place],
            beside_peer(0, step),
        )
        for step, place in ((1, 0), (-1, 2))
    ]
    for copy in halo:
        copy.start()
    recv_c[tile_rows(col), :] = send_c[tile_rows(col), :]
    loads[5].wait()
    near_backward(beside, owned, picks, count, matrices, on_a, lv_one, lv_two, spread_back)
    for copy in halo:
        copy.wait_recv()
    wide_halo = [
        remote(
            beside.at[1], beside.at[place], sem_send_h.at[3 + place], sem_recv_h.at[3 + place],
            beside_peer(1, step),
        )
        for step, place in ((1, 0), (-1, 2))
    ]
    returns = [
        remote(
            spread_back.at[place], back.at[place], sem_send_r.at[place], sem_recv_r.at[place],
            beside_peer(1, step),
        )
        for step, place in ((-1, 0), (1, 2))
    ]
    for copy in returns + wide_halo:
        copy.start()
    for load in loads[6:]:
        load.wait()
    for kz in range(2):
        turn_green(kz, green, turned)
    for copy in third:
        copy.wait_recv()
    pack_sources(recv_c, send_o)
    over = remote(send_o, recv_o, sem_far.at[0], sem_far.at[1], (far, col))
    over.start()
    build_image(recv_c, row, spreads, padded, wides, starts, masks, odd, even)
    sems_a, sems_b = (sem_send_a, sem_recv_a), (sem_send_b, sem_recv_b)
    first, second, beyond = [[], []], [[], []], [[], []]
    for kz in range(2):
        for m in range(2):
            forward_y(kz, chips[m], odd, even, cos, sin, send_a, 2 * chips[m])
            for j in range(2):
                peer = 2 * chips[m] + lax.rem(core + j, 2)
                copy = row_copy(
                    kz, send_a.at[kz, peer], recv_a.at[kz, row], sems_a, 2 * m + j, peer
                )
                copy.start()
                first[kz].append(copy)
    for kz in range(2):
        forward_y(kz, z, odd, even, cos, sin, send_a, 2 * z)
        copy = row_copy(kz, send_a.at[kz, sibling], recv_a.at[kz, row], sems_a, 4, sibling)
        copy.start()
        first[kz].append(copy)
        recv_a[kz, row] = send_a[kz, row]
    over.wait_recv()
    unpack_sources(recv_o, far_c)
    build_image(far_c, far, spreads, padded, wides, starts, far_masks, odd, even)
    for kz in range(2):
        forward_y(kz, z, odd, even, cos, sin, far_a, 0)
        copy = row_copy(kz, far_a.at[kz, 1 - core], recv_a.at[kz, far], sems_a, 5, sibling)
        copy.start()
        first[kz].append(copy)
        recv_a[kz, far] = far_a[kz, core]
    for copy in returns:
        copy.wait_recv()
    column = spread_back[1].astype(F32) + back[0].astype(F32) + back[2].astype(F32)
    kept[...] = column[NB : 2 * NB]
    edges[0] = column[:NB].astype(BF)
    edges[1] = column[2 * NB :].astype(BF)
    edge_copies = [
        remote(
            edges.at[place], edges_in.at[place], sem_send_r.at[3 + place], sem_recv_r.at[3 + place],
            beside_peer(0, step),
        )
        for step, place in ((-1, 0), (1, 1))
    ]
    for copy in edge_copies:
        copy.start()
    build_hot(recv_c, row, hot)
    build_hot(far_c, far, far_hot)
    clear_cells(accs)
    for kz in range(2):
        for copy in first[kz]:
            copy.wait_recv()
        along_x(kz, recv_a, turned, cos, sin, send_b, d_one, d_two, h_one, h_two)
        targets = [2 * chip + lax.rem(core + j, 2) for chip in chips for j in range(2)]
        targets.append(sibling)
        for j, peer in enumerate(targets):
            copy = row_copy(kz, send_b.at[kz, peer], recv_b.at[kz, row], sems_b, j, peer)
            copy.start()
            second[kz].append(copy)
        copy = row_copy(kz, send_b.at[kz, far_sibling], recv_f.at[kz, core], sems_b, 5, sibling)
        copy.start()
        beyond[kz].append(copy)
        recv_b[kz, row] = send_b[kz, row]
        recv_f[kz, core] = send_b[kz, far]
    for kz in range(2):
        beyond[kz][0].wait_recv()
        inverse_y(kz, recv_f, [0], [z], cos, sin, spec, pot)
        pick_cells(kz, pot, far_masks, far_hot, accs)
    fold_cells(accs, spreads, send_d, None)
    pack_halves(send_d, send_q)
    home = remote(send_q, recv_q, sem_far.at[2], sem_far.at[3], (far, col))
    home.start()
    clear_cells(accs)
    held = [z] + chips
    for kz in range(2):
        for copy in second[kz]:
            copy.wait_recv()
        inverse_y(kz, recv_b, [2 * chip for chip in held], held, cos, sin, spec, pot)
        pick_cells(kz, pot, masks, hot, accs)
    home.wait_recv()
    fold_cells(accs, spreads, send_d, recv_q)
    fourth = col_copies(send_d, recv_d, sem_send_d, sem_recv_d)
    for copy in fourth:
        copy.start()
    recv_d[tile_rows(col), :] = send_d[tile_rows(col), :]
    for copy in wide_halo:
        copy.wait_recv()
    near_onward(beside, owned, picks, count, matrices, on_a, on_b, lv_one, near)
    for copy in edge_copies:
        copy.wait_recv()
    edge_sum = edges_in[0].astype(F32) + edges_in[1].astype(F32)
    near[...] = near[...] + kept[...] + edge_sum
    for copy in fourth:
        copy.wait_recv()
    back_project(
        recv_d, near, tch, tcl, tsh, tsl, out, p_high, p_low, hots, box_real, box_imag, vals, twist
    )
    for kz in range(2):
        for copy in first[kz] + second[kz] + beyond[kz]:
            copy.wait_send()
    for copy in third + fourth + halo + wide_halo + returns + edge_copies + [over, home]:
        copy.wait_send()


def per_device(
    currents, near_blocks, pair_local, pair_ghost, pair_counts, projection, stencil_cells, green
):
    tables = [jnp.asarray(t) for t in depth_tables()]
    tables += [jnp.asarray(t) for t in spread_tables()]
    tables += [jnp.asarray(t) for t in grid_tables()]
    vmem, dma = pltpu.VMEM, pltpu.SemaphoreType.DMA
    grid_part = (2, NROW, 2 * XR, 128)
    wrapped = 512 + 2 * NB
    scratch = [
        vmem((PAIRS, 2 * BLK, BLK), BF),
        vmem((NB, BLK, BLK), F32),
        vmem((2, 2, 128, N), F32),
        *[vmem((512, 512), BF)] * 4,
        *[vmem((128, 2048), BF)] * 2,
        *[vmem((N, N), BF)] * 2,
        dma((11,)),
        vmem((2, NB, 512), F32),
        vmem((NB, BLK), jnp.int32),
        *[vmem((NB, BLK, BLK), BF)] * 2,
        vmem((NB, 512, BLK), BF),
        vmem((NB, 2, BLK), F32),
        vmem((2 * NB, 512), F32),
        *[vmem((NB, 512), F32)] * 2,
        *[vmem((3, 3 * NB, 2 * BLK), BF)] * 3,
        vmem((NB, 2 * BLK), F32),
        *[vmem((2, NB, 2 * BLK), BF)] * 2,
        *[vmem((PAIRS, 2 * BLK), F32)] * 4,
        vmem((NB, 2 * BLK), F32),
        vmem((2, N, 256), F32),
        vmem((wrapped, 128), BF),
        *[vmem((320, 2048), BF)] * 2,
        vmem((wrapped, 128), jnp.int32),
        *[vmem((2, 2 * XR, 512), BF)] * 2,
        vmem((4, wrapped, XR), BF),
        *[vmem((320, 2048), BF)] * 2,
        *[vmem((2 * XR, N), BF)] * 2,
        *[vmem((N, 256), BF)] * 2,
        *[vmem((512, 256), BF)] * 2,
        *[vmem(grid_part, BF)] * 4,
        *[dma((2, NROW))] * 4,
        *[vmem((NCOL * NB, 128), BF)] * 4,
        *[dma((NCOL,))] * 4,
        *[dma((9,))] * 4,
        vmem((NCOL * NB, 128), BF),
        *[vmem((272, 128), BF)] * 2,
        *[vmem((8, 128, 128), F32)] * 2,
        vmem((4, wrapped, XR), BF),
        *[vmem((2, 2, 2 * XR, 128), BF)] * 2,
        *[vmem((256, 128), BF)] * 2,
        dma((4,)),
    ]
    in_vmem = pl.BlockSpec(memory_space=pltpu.VMEM)
    in_smem = pl.BlockSpec(memory_space=pltpu.SMEM)
    anywhere = pl.BlockSpec(memory_space=pl.ANY)
    return pl.pallas_call(
        whole_kernel,
        out_shape=jax.ShapeDtypeStruct((2, NB * BLK), F32),
        in_specs=[in_vmem] * 4 + [in_smem] + [anywhere] * 11,
        out_specs=in_vmem,
        scratch_shapes=scratch,
        compiler_params=pltpu.CompilerParams(
            vmem_limit_bytes=VMEM_LIMIT, collective_id=1, has_side_effects=True
        ),
    )(
        currents,
        stencil_cells,
        pair_local,
        pair_ghost,
        pair_counts,
        near_blocks.reshape(PAIRS, 2 * BLK, BLK),
        projection,
        green,
        *tables,
    )


def solution(mesh):
    in_specs = (
        P(None, ("row", "col")),
        P(("row", "col"), None, None, None),
        P(("row", "col"), None),
        P(("row", "col"), None),
        P(("row", "col")),
        P(("row", "col"), None, None),
        P(("row", "col"), None),
        P(None, "col", "row", None),
    )
    out_specs = P(None, ("row", "col"))
    return jax.shard_map(
        per_device, mesh=mesh, in_specs=in_specs, out_specs=out_specs, check_vma=False
    )
```
